32 devices in a mesh: dp: 4 (over y, x), fsdp: 8 (over z, core).
Axes of the slice: x: 2, y: 2, z: 4, core: 2. Of those that a mesh axis runs over, the one named last changes fastest.
Arguments:
- inputs: bfloat16 [32, 2048, 256], P(('dp', 'fsdp')), may hold values from -6 to 6
- inject: bfloat16 [32, 2048, 256], P(('dp', 'fsdp')), may hold values from -6 to 6
- segments: int32 [32, 2048], P(('dp', 'fsdp')), may hold values from -1 to 45, as said below
- cotangent: bfloat16 [32, 2048, 256], P(('dp', 'fsdp')), may hold values from -6 to 6
- qkv_weight: bfloat16 [256, 768], P(None, 'fsdp'), may hold values from -0.5 to 0.5
- out_weight: bfloat16 [256, 256], P(None, 'fsdp'), may hold values from -1 to 1
- up_weight: bfloat16 [256, 1024], P(None, 'fsdp'), may hold values from -0.375 to 0.375
- down_weight: bfloat16 [1024, 256], P(None, 'fsdp'), may hold values from -0.1875 to 0.1875
- query_bias: bfloat16 [256], P('fsdp'), may hold values from -1.796875 to 1.796875
- value_bias: bfloat16 [256], P('fsdp'), may hold values from -1.796875 to 1.796875
- out_bias: bfloat16 [256], P('fsdp'), may hold values from -1.796875 to 1.796875
- up_bias: bfloat16 [1024], P('fsdp'), may hold values from -1.796875 to 1.796875
- down_bias: bfloat16 [256], P('fsdp'), may hold values from -1.796875 to 1.796875
- attn_gain: bfloat16 [256], P('fsdp'), may hold values from 0.5 to 1.5
- attn_shift: bfloat16 [256], P('fsdp'), may hold values from -1.796875 to 1.796875
- mlp_gain: bfloat16 [256], P('fsdp'), may hold values from 0.5 to 1.5
- mlp_shift: bfloat16 [256], P('fsdp'), may hold values from -1.796875 to 1.796875
Outputs:
- result: bfloat16 [32, 2048, 256], P(('dp', 'fsdp'))
- grad_inputs: bfloat16 [32, 2048, 256], P(('dp', 'fsdp'))
- grad_inject: bfloat16 [32, 2048, 256], P(('dp', 'fsdp'))
- grad_qkv_weight: float32 [256, 768], P(None, 'fsdp')
- grad_out_weight: float32 [256, 256], P(None, 'fsdp')
- grad_up_weight: float32 [256, 1024], P(None, 'fsdp')
- grad_down_weight: float32 [1024, 256], P(None, 'fsdp')
- grad_query_bias: float32 [256], P('fsdp')
- grad_value_bias: float32 [256], P('fsdp')
- grad_out_bias: float32 [256], P('fsdp')
- grad_up_bias: float32 [1024], P('fsdp')
- grad_down_bias: float32 [256], P('fsdp')
- grad_attn_gain: float32 [256], P('fsdp')
- grad_attn_shift: float32 [256], P('fsdp')
- grad_mlp_gain: float32 [256], P('fsdp')
- grad_mlp_shift: float32 [256], P('fsdp')
The draws below stay inside these ranges and needn't reach their ends.
Inputs may be any that keep to these rules, and one draw needn't show every extreme that they name: `segments`: in each row ids start at 0 and rise by one from prompt to prompt; every prompt covers 41 to 101 positions and one prompt of each row covers exactly 101; the positions after the last prompt hold -1, and there are 102 or more of them.
All inputs are finite; a program needn't handle non-finite values.
Results may differ from the reference program's by a relative error of at most 0.018.
Values may be sent and summed in bfloat16 or wider, within the bound.
No kernel may reach another device: no remote copies, remote signals or barrier semaphores. Data moves between devices by JAX's collectives and lax.ppermute only.
A program may use at most 192 MiB of HBM per device.

```python
import jax
import jax.numpy as jnp
from jax import lax

D = 256
HEADS = 8
HD = 32
FF = 1024
LOOPS = 2
ROW = 2048
PROMPT_MIN = 41
PROMPT_MAX = 101
MARGIN = 128
QBLOCK = 512
ROWS = 32


def draw_segments(key, part):
    key = jax.random.fold_in(key, 7)
    subkeys = jax.random.split(key, 3)
    slot_count = ROW // PROMPT_MIN + 2
    fill_cap = ROW - ROW // 20
    lengths = jax.random.randint(subkeys[0], (ROWS, slot_count), PROMPT_MIN, PROMPT_MAX + 1)
    dense_row = jax.random.randint(subkeys[2], (), 0, ROWS)
    row_index = jnp.arange(ROWS, dtype=jnp.int32)[:, None]
    lengths = jnp.where(row_index == dense_row, PROMPT_MIN, lengths)
    long_slot = jax.random.randint(subkeys[1], (ROWS, 1), 0, 2)
    slot_index = jnp.arange(slot_count, dtype=jnp.int32)[None, :]
    lengths = jnp.where(slot_index == long_slot, PROMPT_MAX, lengths)
    prompt_ends = jnp.cumsum(lengths, axis=1)
    inside = prompt_ends <= fill_cap
    positions = jnp.arange(ROW, dtype=jnp.int32)
    finished = (prompt_ends[:, None, :] <= positions[None, :, None]) & inside[:, None, :]
    prompt_ids = jnp.sum(finished.astype(jnp.int32), axis=2)
    filled_end = jnp.max(jnp.where(inside, prompt_ends, 0), axis=1)
    return jnp.where(positions[None, :] < filled_end[:, None], prompt_ids, -1).astype(jnp.int32)


def raised(drawn, own_key, source, target, blocks, factor):
    owner, partner = [(jnp.arange(drawn.shape[dim]) // (drawn.shape[dim] // blocks)).reshape([-1 if axis == dim else 1 for axis in range(drawn.ndim)]) for dim in (source, target)]
    chosen = jax.random.permutation(own_key, blocks)[partner]
    strong = (owner == chosen) | (owner == (partner + blocks // 2) % blocks)
    return jnp.where(strong, factor * drawn, drawn)


def steps_of(stream_key, dims, shards, low, largest):
    def one(axis_at, blocks):
        steps = jax.random.uniform(jax.random.fold_in(jax.random.fold_in(stream_key, 6), axis_at), (blocks,), jnp.float32, low / len(shards), largest / len(shards))
        return jnp.repeat(jnp.exp(steps), dims[axis_at] // blocks).reshape((-1,) + (1,) * (len(dims) - axis_at - 1))

    loudness = one(*shards[0])
    for cut in shards[1:]:
        loudness = loudness * one(*cut)
    return loudness


def bell_draw(stream_key, dims, deviation, limit, shards=(), kind=jnp.bfloat16):
    values = jax.random.normal(stream_key, dims, jnp.float32) * deviation
    if len(shards) > 0:
        values = steps_of(stream_key, dims, shards, -0.22, 0.18) * values
    return jnp.clip(values, min=-limit, max=limit).astype(kind)


def noise_with(key, extent, deviation, most, shards, heavy, kind=jnp.bfloat16):
    array = deviation * jax.random.normal(key, extent, jnp.float32)
    if shards:
        array = array * steps_of(key, extent, shards, -0.22, 0.18)
    return jnp.clip(raised(array, jax.random.fold_in(key, 3), *heavy), -most, most).astype(kind)


def setup_inputs(seed: int = 0) -> dict:
    streams_of = jax.random.split(jax.random.key(seed), 18)
    return {
        "inputs": bell_draw(streams_of[0], (ROWS, ROW, D), 1.0, 6.0, ((0, 32),)),
        "inject": bell_draw(streams_of[1], (ROWS, ROW, D), 1.0, 6.0, ((0, 32),)),
        "segments": draw_segments(jax.random.fold_in(streams_of[17], 71), 0),
        "cotangent": noise_with(streams_of[3], (ROWS, ROW, D), 1.0, 6.0, ((0, 32),), (0, 2, 32, 2.75)),
        "qkv_weight": bell_draw(streams_of[4], (D, 3 * D), (D // 2) ** -0.5, 0.5, ((1, 8),)),
        "out_weight": bell_draw(streams_of[5], (D, D), (D // 8) ** -0.5, 1.0, ((1, 8),)),
        "up_weight": bell_draw(streams_of[6], (D, FF), D ** -0.5, 0.375, ((1, 8),)),
        "down_weight": bell_draw(streams_of[7], (FF, D), FF ** -0.5, 0.1875, ((1, 8),)),
        "query_bias": bell_draw(streams_of[8], (D,), 0.3, 1.796875, ((0, 8),)),
        "value_bias": bell_draw(streams_of[9], (D,), 0.3, 1.796875, ((0, 8),)),
        "out_bias": bell_draw(streams_of[10], (D,), 0.3, 1.796875, ((0, 8),)),
        "up_bias": bell_draw(streams_of[11], (FF,), 0.3, 1.796875, ((0, 8),)),
        "down_bias": bell_draw(streams_of[12], (D,), 0.3, 1.796875, ((0, 8),)),
        "attn_gain": jnp.clip(1.0 + 0.1 * jax.random.normal(streams_of[13], (D,), jnp.float32), 0.5, 1.5).astype(jnp.bfloat16),
        "attn_shift": bell_draw(streams_of[14], (D,), 0.3, 1.796875, ((0, 8),)),
        "mlp_gain": jnp.clip(1.0 + 0.1 * jax.random.normal(streams_of[15], (D,), jnp.float32), 0.5, 1.5).astype(jnp.bfloat16),
        "mlp_shift": bell_draw(streams_of[16], (D,), 0.3, 1.796875, ((0, 8),)),
    }


@jax.custom_vjp
def low(v):
    return lax.optimization_barrier(v.astype(jnp.bfloat16)).astype(jnp.float32)

@jax.custom_vjp
def low_back(v):
    return v

def low_keep(v):
    return (low(v), None)

def low_pass(kept, grad):
    return (grad,)

def back_keep(v):
    return (v, None)

def back_low(kept, grad):
    return (low(grad),)
low.defvjp(low_keep, low_pass)
low_back.defvjp(back_keep, back_low)
norm_eps = 1e-05
masked_score = -1e+30

def matmul_full(left_op, right_op):
    return jnp.dot(left_op, right_op, precision=lax.Precision.HIGHEST, preferred_element_type=jnp.float32)

def layer_norm(values, gain_vec, shift_vec):
    centre = values - lax.optimization_barrier(jnp.mean(values, axis=-1, keepdims=True))
    variance = lax.optimization_barrier(jnp.mean(centre * centre, axis=-1, keepdims=True))
    return centre * lax.rsqrt(variance + norm_eps) * gain_vec + shift_vec

def allowed_pairs(seg_query, seg_keys):
    query_len = seg_query.shape[0]
    keys_len = seg_keys.shape[0]
    query_place = lax.broadcasted_iota(jnp.int32, (query_len, keys_len), 0) + (keys_len - query_len)
    key_place = lax.broadcasted_iota(jnp.int32, (query_len, keys_len), 1)
    same_prompt = (seg_query[:, None] == seg_keys[None, :]) & (seg_query[:, None] >= 0) & (key_place <= query_place)
    return same_prompt | (key_place == query_place)

def attend(query_rows, key_rows, value_rows, seg_row):
    zero_rows = jnp.zeros((MARGIN, D), jnp.float32)
    keys_pad = jnp.concatenate([zero_rows, key_rows], axis=0)
    values_pad = jnp.concatenate([zero_rows, value_rows], axis=0)
    seg_int = seg_row.astype(jnp.int32)
    seg_pad = jnp.concatenate([jnp.full((MARGIN,), -2, jnp.int32), seg_int], axis=0)
    score_scale = HD ** (-0.5)

    def one_block(block_id):
        block_start = (block_id * QBLOCK).astype(jnp.int32)
        query_tile = lax.dynamic_slice_in_dim(query_rows, block_start, QBLOCK, 0).reshape(QBLOCK, HEADS, HD)
        key_tile = lax.dynamic_slice_in_dim(keys_pad, block_start, QBLOCK + MARGIN, 0).reshape(QBLOCK + MARGIN, HEADS, HD)
        value_tile = lax.dynamic_slice_in_dim(values_pad, block_start, QBLOCK + MARGIN, 0).reshape(QBLOCK + MARGIN, HEADS, HD)
        seg_query = lax.dynamic_slice_in_dim(seg_int, block_start, QBLOCK, 0)
        seg_keys = lax.dynamic_slice_in_dim(seg_pad, block_start, QBLOCK + MARGIN, 0)
        scores = jnp.einsum('qhd,khd->hqk', query_tile, key_tile, precision=lax.Precision.HIGHEST) * score_scale
        scores = low_back(scores)
        scores = jnp.where(allowed_pairs(seg_query, seg_keys)[None], scores, masked_score)
        row_max = lax.optimization_barrier(jnp.max(scores, axis=-1, keepdims=True))
        exp_scores = jnp.exp(scores - row_max)
        prob_low = low(exp_scores / lax.optimization_barrier(jnp.sum(exp_scores, axis=-1, keepdims=True)))
        context = jnp.einsum('hqk,khd->qhd', prob_low, value_tile, precision=lax.Precision.HIGHEST)
        return context.reshape(QBLOCK, D)
    blocks = lax.map(jax.checkpoint(one_block), jnp.arange(ROW // QBLOCK, dtype=jnp.int32))
    return blocks.reshape(ROW, D)

def forward(start_rows, inject_row, params, seg_row):
    qkv_weight, out_weight, up_weight, down_weight, query_bias, value_bias, out_bias, up_bias, down_bias, attn_gain, attn_shift, mlp_gain, mlp_shift = params
    qkv_bias = jnp.concatenate([query_bias, jnp.zeros_like(query_bias), value_bias])
    hidden_state = start_rows
    for repeat in range(LOOPS):
        injected = hidden_state + inject_row
        normed = low(layer_norm(injected, attn_gain, attn_shift))
        qkv_rows = low_back(low(matmul_full(normed, qkv_weight) + qkv_bias))
        context = low_back(low(attend(qkv_rows[:, :D], qkv_rows[:, D:2 * D], qkv_rows[:, 2 * D:], seg_row)))
        after_attn = injected + low_back(matmul_full(context, out_weight) + out_bias)
        normed_mlp = low(layer_norm(after_attn, mlp_gain, mlp_shift))
        pre_act = low_back(matmul_full(normed_mlp, up_weight) + up_bias)
        hidden = low(jax.nn.gelu(pre_act, approximate=True))
        hidden_state = after_attn + low_back(matmul_full(hidden, down_weight) + down_bias)
    return hidden_state

def reference(inputs, inject, segments, cotangent, qkv_weight, out_weight, up_weight, down_weight, query_bias, value_bias, out_bias, up_bias, down_bias, attn_gain, attn_shift, mlp_gain, mlp_shift):
    params = tuple((weight.astype(jnp.float32) for weight in (qkv_weight, out_weight, up_weight, down_weight, query_bias, value_bias, out_bias, up_bias, down_bias, attn_gain, attn_shift, mlp_gain, mlp_shift)))

    def one_row(totals, row_data):
        input_row, inject_row, seg_row, cot_row = row_data

        def row_forward(start_rows, inject_rows, weights):
            return forward(start_rows, inject_rows, weights, seg_row)
        output_row, pullback = jax.vjp(row_forward, input_row.astype(jnp.float32), inject_row.astype(jnp.float32), params)
        grad_input, grad_injection, grad_params = pullback(cot_row.astype(jnp.float32))
        totals = tuple((running + addend for running, addend in zip(totals, grad_params)))
        return (totals, (output_row.astype(jnp.bfloat16), grad_input.astype(jnp.bfloat16), grad_injection.astype(jnp.bfloat16)))
    start_totals = tuple((jnp.zeros(weight.shape, jnp.float32) for weight in params))
    totals, outputs = lax.scan(one_row, start_totals, (inputs, inject, segments, cotangent))
    result, grad_inputs, grad_inject = outputs
    grad_qkv_weight, grad_out_weight, grad_up_weight, grad_down_weight, grad_query_bias, grad_value_bias, grad_out_bias, grad_up_bias, grad_down_bias, grad_attn_gain, grad_attn_shift, grad_mlp_gain, grad_mlp_shift = totals
    return (result, grad_inputs, grad_inject, grad_qkv_weight, grad_out_weight, grad_up_weight, grad_down_weight, grad_query_bias, grad_value_bias, grad_out_bias, grad_up_bias, grad_down_bias, grad_attn_gain, grad_attn_shift, grad_mlp_gain, grad_mlp_shift)
```

```python
import math
from functools import partial

import jax
import jax.numpy as jnp
from jax import lax
from jax.experimental import pallas as pl
from jax.experimental.pallas import tpu as pltpu
from jax.sharding import PartitionSpec as P

HEADS = 8
HD = 32
CHUNK = 256
BLOCK = 128
PAIRS = HEADS // 2

norm_eps = 1e-05
masked_score = -1e30
score_scale = HD ** (-0.5)
exp2_scale = score_scale * math.log2(math.e)
gelu_c0 = math.sqrt(2.0 / math.pi)
gelu_c1 = 0.044715 * gelu_c0

f32 = jnp.float32
bf16 = jnp.bfloat16

(
    Q_BIAS,
    V_BIAS,
    OUT_BIAS,
    DOWN_BIAS,
    ATTN_GAIN,
    ATTN_SHIFT,
    MLP_GAIN,
    MLP_SHIFT,
    UP_BIAS,
) = range(9)


def mm(left_op, right_op):
    return lax.dot_general(
        left_op, right_op, (((1,), (0,)), ((), ())), preferred_element_type=f32
    )


def mm_nt(left_op, right_op):
    return lax.dot_general(
        left_op, right_op, (((1,), (1,)), ((), ())), preferred_element_type=f32
    )


def identity(size):
    rows = lax.broadcasted_iota(jnp.int32, (size, size), 0)
    cols = lax.broadcasted_iota(jnp.int32, (size, size), 1)
    return jnp.where(rows == cols, 1.0, 0.0).astype(bf16)


def flipped(block):
    return mm_nt(identity(block.shape[1]), block).astype(bf16)


def half(index):
    return slice(index * BLOCK, (index + 1) * BLOCK)


def spread(column):
    return jnp.broadcast_to(column, (column.shape[0], BLOCK))


def row_sum(values):
    return jnp.sum(values, axis=0, keepdims=True)


def norm_forward(values, gain, shift):
    scale = 1.0 / values.shape[0]
    centre = values - row_sum(values) * scale
    inverse = lax.rsqrt(row_sum(centre * centre) * scale + norm_eps)
    unit = centre * inverse
    return unit, inverse, unit * gain + shift


def norm_backward(grad_normed, unit, inverse, gain):
    scale = 1.0 / unit.shape[0]
    scaled = grad_normed * gain
    gain_term = grad_normed * unit
    mean_scaled = row_sum(scaled) * scale
    mean_unit = row_sum(gain_term * gain) * scale
    return inverse * (scaled - mean_scaled - unit * mean_unit), gain_term


def below_mask():
    key_at = lax.broadcasted_iota(jnp.int32, (BLOCK, BLOCK), 0)
    query_at = lax.broadcasted_iota(jnp.int32, (BLOCK, BLOCK), 1)
    return key_at <= query_at, key_at == query_at


def stack(side, pair):
    base = (side * PAIRS + pair) * BLOCK
    return slice(base, base + BLOCK)


def twice(values):
    return jnp.concatenate([values, values], axis=1)


def set_pairs(dest, source, lanes):
    for pair in range(PAIRS):
        base = 64 * (pair % 2)
        for side in range(2):
            dest[pair, base + HD * side : base + HD * (side + 1), half(side)] = source[
                64 * pair + HD * side : 64 * pair + HD * (side + 1), lanes
            ]


def front(u_ref, seg_ref, first, bcast, w_qkv, out, carry, q_pairs):
    unit_o, inv_o, normed_o, qk_o, vtok_o, probs_o, context_o, v_s, ktok_s = out
    kprev, vprev, segprev = carry
    for side in range(2):
        unit, inverse, normed = norm_forward(
            u_ref[:, half(side)], bcast[ATTN_GAIN], bcast[ATTN_SHIFT]
        )
        unit_o[:, half(side)] = unit.astype(bf16)
        inv_o[:, half(side)] = inverse
        normed_o[:, half(side)] = normed.astype(bf16)
    normed = normed_o[...]
    model = w_qkv.shape[1]
    for part in range(3):
        rows = mm(w_qkv[model * part : model * (part + 1), :], normed)
        if part == 0:
            qk_o[:model, :] = (rows + twice(bcast[Q_BIAS])).astype(bf16)
        elif part == 1:
            qk_o[model:, :] = rows.astype(bf16)
        else:
            v_s[...] = (rows + twice(bcast[V_BIAS])).astype(bf16)
    eye = identity(model)
    ktok_s[...] = mm_nt(eye, qk_o[model:, :]).astype(bf16)
    vtok_o[...] = mm_nt(eye, v_s[...]).astype(bf16)

    @pl.when(first)
    def _():
        segprev[...] = jnp.full(segprev.shape, -2.0, f32)

    below, diagonal = below_mask()
    below2 = twice(below)
    for side in range(2):
        lanes = half(side)
        seg_row = seg_ref[:, lanes].astype(f32)
        seg_col = jnp.transpose(jnp.broadcast_to(seg_row, (BLOCK, BLOCK)))
        seg_key = jnp.where(below, seg_col, segprev[...])
        segprev[...] = seg_col
        allowed = ((seg_key == seg_row) & (seg_row >= 0)) | diagonal
        bias = twice(jnp.where(allowed, 0.0, masked_score))
        set_pairs(q_pairs.at[side], qk_o, lanes)
        if side == 0:
            key_win = jnp.concatenate([kprev[...], ktok_s[:BLOCK, :]], axis=0)
            value_win = jnp.concatenate([vprev[...], v_s[:, :BLOCK]], axis=1)
        else:
            key_win = ktok_s[...]
            value_win = v_s[...]
        for pair in range(PAIRS):
            group = pair // 2
            scores = mm(key_win[:, half(group)], q_pairs[side, pair])
            folded = jnp.where(below2, scores[BLOCK:], scores[:BLOCK]) * exp2_scale + bias
            top = jnp.max(folded, axis=0, keepdims=True)
            weights = jnp.exp2(folded - top)
            probs = (weights * (1.0 / row_sum(weights))).astype(bf16)
            probs_o[stack(side, pair), :] = probs
            zero = jnp.zeros_like(probs)
            window = jnp.concatenate(
                [jnp.where(below2, zero, probs), jnp.where(below2, probs, zero)], axis=0
            )
            both = mm(value_win[64 * pair : 64 * (pair + 1), :], window)
            context_o[64 * pair : 64 * pair + HD, lanes] = both[:HD, :BLOCK].astype(bf16)
            context_o[64 * pair + HD : 64 * (pair + 1), lanes] = both[HD:, BLOCK:].astype(bf16)
    kprev[...] = ktok_s[BLOCK:, :]
    vprev[...] = v_s[:, BLOCK:]


def feed_forward(u_ref, m_ref, h_ref, context, bcast, up_bias, w_out, w_up, w_down, out):
    unit_o, inv_o, normed_o, hidden_o, slope_o = out
    mixed = mm(w_out[...], context)
    for side in range(2):
        lanes = half(side)
        after = u_ref[:, lanes] + (mixed[:, lanes] + bcast[OUT_BIAS])
        m_ref[:, lanes] = after
        unit, inverse, normed = norm_forward(after, bcast[MLP_GAIN], bcast[MLP_SHIFT])
        unit_o[:, lanes] = unit.astype(bf16)
        inv_o[:, lanes] = inverse
        normed_o[:, lanes] = normed.astype(bf16)
    normed = normed_o[...]
    ff = w_up.shape[0]
    total = None
    for part in range(ff // CHUNK):
        rows = slice(part * CHUNK, (part + 1) * CHUNK)
        pre = mm(w_up[rows, :], normed)
        for side in range(2):
            lanes = half(side)
            z = pre[:, lanes] + up_bias[rows, :]
            z2 = z * z
            gate = 0.5 * jnp.tanh(z * (gelu_c0 + gelu_c1 * z2)) + 0.5
            act = z * gate
            slope = gate + (act * (1.0 - gate)) * (2.0 * gelu_c0 + 6.0 * gelu_c1 * z2)
            hidden_o[rows, lanes] = act.astype(bf16)
            slope_o[rows, lanes] = slope.astype(bf16)
        term = mm(w_down[:, rows], hidden_o[rows, :])
        total = term if total is None else total + term
    for side in range(2):
        lanes = half(side)
        h_ref[:, lanes] = m_ref[:, lanes] + (total[:, lanes] + bcast[DOWN_BIAS])


def back_feed_forward(g_ref, dm_ref, saved, bcast, weights, sums, dy_s, dz_s, db_s, do_ref):
    unit, inverse, normed, hidden, slope = saved
    w_down_n, w_up_n = weights
    sum_down, sum_up, sum_up_bias, sum_vec = sums
    for side in range(2):
        lanes = half(side)
        grad = g_ref[:, lanes]
        sum_vec[DOWN_BIAS] += grad
        dy_s[:, lanes] = grad.astype(bf16)
    dy = dy_s[...]
    ff = w_down_n.shape[0]
    total = None
    for part in range(ff // CHUNK):
        rows = slice(part * CHUNK, (part + 1) * CHUNK)
        grad_hidden = mm(w_down_n[rows, :], dy)
        for side in range(2):
            lanes = half(side)
            dz = grad_hidden[:, lanes] * slope[rows, lanes].astype(f32)
            sum_up_bias[rows, :] += dz
            dz_s[rows, lanes] = dz.astype(bf16)
        term = mm(w_up_n[:, rows], dz_s[rows, :])
        total = term if total is None else total + term
    sum_down[...] += mm_nt(hidden[...], dy)
    sum_up[...] += mm_nt(dz_s[...], normed[...])
    for side in range(2):
        lanes = half(side)
        grad_normed = total[:, lanes]
        back, gain_term = norm_backward(
            grad_normed, unit[:, lanes].astype(f32), inverse[:, lanes], bcast[MLP_GAIN]
        )
        sum_vec[MLP_GAIN] += gain_term
        sum_vec[MLP_SHIFT] += grad_normed
        dm = g_ref[:, lanes] + back
        dm_ref[:, lanes] = dm
        sum_vec[OUT_BIAS] += dm
        do_ref[:, lanes] = dm.astype(bf16)


def back_out(do_ref, context, w_out_n, sum_out, dc_ref):
    grad = do_ref[...]
    sum_out[...] += mm_nt(grad, context[...])
    dc_ref[...] = mm(w_out_n[...], grad).astype(bf16)


def back_attention(dc_ref, context, qk, kt_prev, vtok, vtok_prev, probs_ref, pairs, sums, carry, dqkv):
    q_pairs, c_pairs = pairs
    dk_carry, dv_carry = carry
    model = vtok.shape[1]
    below, _ = below_mask()
    below2 = twice(below)
    for side in (1, 0):
        lanes = half(side)
        set_pairs(q_pairs.at[side], qk, lanes)
        set_pairs(c_pairs.at[side], dc_ref, lanes)
        weighted = dc_ref[:, lanes].astype(f32) * context[:, lanes].astype(f32)
        if side == 1:
            key_win = qk[model:, :]
            value_win = vtok[...]
        else:
            key_win = jnp.concatenate([kt_prev[...], qk[model:, :BLOCK]], axis=1)
            value_win = jnp.concatenate([vtok_prev[...], vtok[:BLOCK, :]], axis=0)
        for pair in range(PAIRS):
            group = pair // 2
            base = 64 * (pair % 2)
            rows = slice(64 * pair, 64 * (pair + 1))
            grad_probs = mm(value_win[:, half(group)], c_pairs[side, pair])
            folded = jnp.where(below2, grad_probs[BLOCK:], grad_probs[:BLOCK])
            delta = jnp.concatenate(
                [
                    row_sum(weighted[64 * pair : 64 * pair + HD]),
                    row_sum(weighted[64 * pair + HD : 64 * (pair + 1)]),
                ],
                axis=1,
            )
            probs = probs_ref[stack(side, pair), :]
            grad_scores = (probs.astype(f32) * (folded - delta)).astype(bf16)
            zero = jnp.zeros_like(probs)
            prob_win = jnp.concatenate(
                [jnp.where(below2, zero, probs), jnp.where(below2, probs, zero)], axis=0
            )
            grad_win = jnp.concatenate(
                [jnp.where(below2, zero, grad_scores), jnp.where(below2, grad_scores, zero)],
                axis=0,
            )
            dq = mm(key_win[rows, :], grad_win) * score_scale
            dqkv[64 * pair : 64 * pair + HD, lanes] = dq[:HD, :BLOCK].astype(bf16)
            dqkv[64 * pair + HD : 64 * (pair + 1), lanes] = dq[HD:, BLOCK:].astype(bf16)
            dk = mm_nt(q_pairs[side, pair, base : base + 64, :], grad_win) * score_scale
            dv = mm_nt(c_pairs[side, pair, base : base + 64, :], prob_win)
            krows = slice(model + 64 * pair, model + 64 * (pair + 1))
            vrows = slice(2 * model + 64 * pair, 2 * model + 64 * (pair + 1))
            dqkv[krows, lanes] = (dk[:, BLOCK:] + dk_carry[rows, :]).astype(bf16)
            dqkv[vrows, lanes] = (dv[:, BLOCK:] + dv_carry[rows, :]).astype(bf16)
            dk_carry[rows, :] = dk[:, :BLOCK]
            dv_carry[rows, :] = dv[:, :BLOCK]


def back_front(dm_ref, dqkv, unit, inverse, normed, bcast, w_qkv_n, sum_qkv, sum_vec, du_ref):
    grads = dqkv[...]
    model = dm_ref.shape[0]
    sum_qkv[...] += mm_nt(grads, normed[...])
    grad_normed_all = mm(w_qkv_n[...], grads)
    for side in range(2):
        lanes = half(side)
        sum_vec[Q_BIAS] += dqkv[:model, lanes].astype(f32)
        sum_vec[V_BIAS] += dqkv[2 * model :, lanes].astype(f32)
        grad_normed = grad_normed_all[:, lanes]
        back, gain_term = norm_backward(
            grad_normed, unit[:, lanes].astype(f32), inverse[:, lanes], bcast[ATTN_GAIN]
        )
        sum_vec[ATTN_GAIN] += gain_term
        sum_vec[ATTN_SHIFT] += grad_normed
        du_ref[:, lanes] = dm_ref[:, lanes] + back


def unpack_first(packed, w_qkv, vec):
    owners, _, model = packed.shape
    rows = 3 * model // owners
    for owner in range(owners):
        w_qkv[rows * owner : rows * (owner + 1), :] = packed[owner, :rows, :]
        vec[32 * owner : 32 * (owner + 1), :] = packed[owner, rows:, :BLOCK].astype(f32)


def unpack_second(packed, w_out, w_up_n, w_down):
    owners = packed.shape[0]
    for owner in range(owners):
        rows = slice(32 * owner, 32 * (owner + 1))
        w_out[rows, :] = packed[owner, :32, :]
        for side in range(2):
            w_up_n[half(side), half(owner)] = packed[owner, 32:160, half(side)]
        for part in range(4):
            w_down[rows, part * CHUNK : (part + 1) * CHUNK] = packed[
                owner, 160 + 32 * part : 192 + 32 * part, :
            ]


def spread_vectors(vec, bcast, which):
    values = vec[...]
    for index in which:
        bcast[index] = spread(values[:, index : index + 1])


def token_sum(left_tokens, right_tokens, dest):
    eye = identity(left_tokens.shape[1])
    dest[...] = mm_nt(eye, left_tokens) + mm_nt(eye, right_tokens)


def kernel_one(
    rows_chunks, x, inj, seg, first_weights,
    u_o, unit_o, inv_o, normed_o, qk_o, vtok_o, probs_o, context_o,
    w_qkv, vec, bcast, v_s, ktok_s, kprev, vprev, segprev, q_pairs,
):
    step = pl.program_id(0)

    @pl.when(step == 0)
    def _():
        unpack_first(first_weights, w_qkv, vec)
        spread_vectors(vec, bcast, (Q_BIAS, V_BIAS, ATTN_GAIN, ATTN_SHIFT))
        kprev[...] = jnp.zeros_like(kprev)
        vprev[...] = jnp.zeros_like(vprev)
        q_pairs[...] = jnp.zeros_like(q_pairs)

    token_sum(x[...], inj[...], u_o.at[0])
    out = [r.at[0] for r in (unit_o, inv_o, normed_o, qk_o, vtok_o, probs_o, context_o)]
    front(
        u_o.at[0], seg.at[0], lax.rem(step, rows_chunks) == 0, bcast, w_qkv,
        out + [v_s, ktok_s], (kprev, vprev, segprev), q_pairs,
    )


def kernel_two(
    rows_chunks, chunks,
    u1, c1, inj, cot, seg, first_weights, second_weights,
    result_o, dm_o, dc_o, du_o, grads_o, sum_qkv_o, vec_o,
    w_qkv, vec, w_out, w_up_n, w_down, bcast, up_bias, w_up, w_down_n, w_out_n, w_qkv_n,
    u_s, m_s, h_s, g_s, v_s, ktok_s, kprev, vprev, segprev, q_pairs, c_pairs,
    unit_m1, inv_m1, norm_m1, hid1, slope1,
    unit2, inv2, norm2, qk2, vtok2, probs2, ctx2,
    unit_m2, inv_m2, norm_m2, hid2, slope2,
    dy_s, dz_s, do_s, dc_s, dqkv_s, dk_carry, dv_carry,
    sum_down, sum_up, sum_out, sum_up_bias, sum_vec, pcopy,
):
    step = pl.program_id(0)
    model = w_out.shape[0]
    ff = w_up.shape[0]

    @pl.when(step == 0)
    def _():
        unpack_first(first_weights, w_qkv, vec)
        unpack_second(second_weights, w_out, w_up_n, w_down)
        spread_vectors(vec, bcast, range(8))
        values = vec[...]
        for owner in range(ff // BLOCK):
            for col in range(4):
                up_bias[BLOCK * owner + 32 * col : BLOCK * owner + 32 * (col + 1), :] = spread(
                    values[32 * owner : 32 * (owner + 1), UP_BIAS + col : UP_BIAS + col + 1]
                )
        for part in range(ff // CHUNK):
            rows = slice(part * CHUNK, (part + 1) * CHUNK)
            w_up[rows, :] = flipped(w_up_n[:, rows])
            w_down_n[rows, :] = flipped(w_down[:, rows])
        w_out_n[...] = flipped(w_out[...])
        for part in range(3):
            rows = slice(part * model, (part + 1) * model)
            w_qkv_n[:, rows] = flipped(w_qkv[rows, :])
        for ref in (kprev, vprev, q_pairs, c_pairs, dk_carry, dv_carry,
                    sum_down, sum_up, sum_out, sum_up_bias, sum_vec):
            ref[...] = jnp.zeros_like(ref)
        sum_qkv_o[...] = jnp.zeros_like(sum_qkv_o)

    @pl.when(step < chunks)
    def _():
        i = step
        feed_forward(
            u1.at[0], m_s, h_s, c1[0], bcast, up_bias, w_out, w_up, w_down,
            [r.at[i] for r in (unit_m1, inv_m1, norm_m1, hid1, slope1)],
        )
        u_s[...] = h_s[...] + mm_nt(identity(model), inj[...])
        out = [r.at[i] for r in (unit2, inv2, norm2, qk2, vtok2, probs2, ctx2)]
        front(
            u_s, seg.at[0], lax.rem(step, rows_chunks) == 0, bcast, w_qkv,
            out + [v_s, ktok_s], (kprev, vprev, segprev), q_pairs,
        )
        feed_forward(
            u_s, m_s, h_s, ctx2[i], bcast, up_bias, w_out, w_up, w_down,
            [r.at[i] for r in (unit_m2, inv_m2, norm_m2, hid2, slope2)],
        )
        result_o[...] = mm_nt(identity(CHUNK), h_s[...].astype(bf16)).astype(bf16)

    @pl.when(step >= chunks)
    def _():
        i = 2 * chunks - 1 - step
        before = jnp.maximum(i - 1, 0)
        g_s[...] = mm_nt(identity(model), cot[...])
        pcopy[...] = probs2[i]
        sums = (sum_down, sum_up, sum_up_bias, sum_vec)
        back_feed_forward(
            g_s, m_s, [r.at[i] for r in (unit_m2, inv_m2, norm_m2, hid2, slope2)],
            bcast, (w_down_n, w_up_n), sums, dy_s, dz_s, None, do_s,
        )
        back_out(do_s, ctx2.at[i], w_out_n, sum_out, dc_s)
        back_attention(
            dc_s, ctx2.at[i], qk2.at[i], qk2.at[before, model:, BLOCK:], vtok2.at[i],
            vtok2.at[before, BLOCK:, :], pcopy, (q_pairs, c_pairs), None,
            (dk_carry, dv_carry), dqkv_s,
        )
        back_front(
            m_s, dqkv_s, unit2.at[i], inv2.at[i], norm2.at[i], bcast, w_qkv_n,
            sum_qkv_o, sum_vec, g_s,
        )
        du_o[0] = g_s[...]
        back_feed_forward(
            g_s, dm_o.at[0], [r.at[i] for r in (unit_m1, inv_m1, norm_m1, hid1, slope1)],
            bcast, (w_down_n, w_up_n), sums, dy_s, dz_s, None, do_s,
        )
        back_out(do_s, c1.at[0], w_out_n, sum_out, dc_o.at[0])

    @pl.when(step == 2 * chunks - 1)
    def _():
        owners = grads_o.shape[0]
        for part in range(ff // CHUNK):
            rows = slice(part * CHUNK, (part + 1) * CHUNK)
            up_block = flipped(sum_up[rows, :].astype(bf16))
            for within in range(2):
                for side in range(2):
                    grads_o[2 * part + within, 32:160, half(side)] = up_block[
                        half(side), half(within)
                    ]
            down_block = flipped(sum_down[rows, :].astype(bf16))
            for owner in range(owners):
                grads_o[owner, 160 + 32 * part : 192 + 32 * part, :] = down_block[
                    32 * owner : 32 * (owner + 1), :
                ]
        for owner in range(owners):
            grads_o[owner, :32, :] = sum_out[32 * owner : 32 * (owner + 1), :].astype(bf16)
        vec_o[...] = jnp.zeros_like(vec_o)
        for index in range(8):
            vec_o[:, index : index + 1] = jnp.sum(sum_vec[index], axis=1, keepdims=True)
        for owner in range(ff // BLOCK):
            for col in range(4):
                vec_o[32 * owner : 32 * (owner + 1), UP_BIAS + col : UP_BIAS + col + 1] = jnp.sum(
                    sum_up_bias[BLOCK * owner + 32 * col : BLOCK * owner + 32 * (col + 1), :],
                    axis=1, keepdims=True,
                )


def kernel_three(
    chunks,
    unit, inv, normed, qk, kt_prev, vtok, vtok_prev, probs, ctx, dm, dc, du2, first_weights, sum_qkv_i, vec_i,
    gin_o, ginj_o, grads_o,
    w_qkv, vec, bcast, w_qkv_n, q_pairs, c_pairs, dqkv_s, dk_carry, dv_carry, g_s, sum_qkv, sum_vec,
):
    step = pl.program_id(0)
    model = w_qkv.shape[1]
    owners = grads_o.shape[0]

    @pl.when(step == 0)
    def _():
        unpack_first(first_weights, w_qkv, vec)
        spread_vectors(vec, bcast, (ATTN_GAIN,))
        for part in range(3):
            rows = slice(part * model, (part + 1) * model)
            w_qkv_n[:, rows] = flipped(w_qkv[rows, :])
        for ref in (q_pairs, c_pairs, dk_carry, dv_carry, sum_vec):
            ref[...] = jnp.zeros_like(ref)
        sum_qkv[...] = sum_qkv_i[...]

    back_attention(
        dc.at[0], ctx.at[0], qk.at[0], kt_prev.at[0], vtok.at[0], vtok_prev.at[0], probs.at[0],
        (q_pairs, c_pairs), None, (dk_carry, dv_carry), dqkv_s,
    )
    back_front(
        dm.at[0], dqkv_s, unit.at[0], inv.at[0], normed.at[0], bcast, w_qkv_n,
        sum_qkv, sum_vec, g_s,
    )
    eye = identity(CHUNK)
    gin_o[...] = mm_nt(eye, g_s[...].astype(bf16)).astype(bf16)
    ginj_o[...] = mm_nt(eye, (g_s[...] + du2[0]).astype(bf16)).astype(bf16)

    @pl.when(step == chunks - 1)
    def _():
        rows = 3 * model // owners
        vec[...] = vec_i[...]
        for index in (Q_BIAS, V_BIAS, ATTN_GAIN, ATTN_SHIFT):
            vec[:, index : index + 1] += jnp.sum(sum_vec[index], axis=1, keepdims=True)
        for owner in range(owners):
            grads_o[owner, :rows, :] = sum_qkv[rows * owner : rows * (owner + 1), :].astype(bf16)
            grads_o[owner, rows:, :] = twice(vec[32 * owner : 32 * (owner + 1), :].astype(bf16))


def whole(array):
    zeros = (0,) * len(array.shape)
    return pl.BlockSpec(array.shape, lambda j: zeros)


def shape(dims, kind):
    return jax.ShapeDtypeStruct(dims, kind)


def vmem(dims, kind):
    return pltpu.VMEM(dims, kind)


params = pltpu.CompilerParams(vmem_limit_bytes=62 * 1024 * 1024)


def run_one(x, inj, seg, first_weights, per_row):
    tokens, model = x.shape
    chunks = tokens // CHUNK

    def lead(dims):
        return pl.BlockSpec((1,) + dims, lambda j: (j,) + (0,) * len(dims))

    token_spec = pl.BlockSpec((CHUNK, model), lambda j: (j, 0))
    outs = [
        ((model, CHUNK), f32),
        ((model, CHUNK), bf16),
        ((1, CHUNK), f32),
        ((model, CHUNK), bf16),
        ((2 * model, CHUNK), bf16),
        ((CHUNK, model), bf16),
        ((2 * PAIRS * BLOCK, CHUNK), bf16),
        ((model, CHUNK), bf16),
    ]
    return pl.pallas_call(
        partial(kernel_one, per_row),
        grid=(chunks,),
        in_specs=[token_spec, token_spec, lead((1, CHUNK)), whole(first_weights)],
        out_specs=[lead(dims) for dims, _ in outs],
        out_shape=[shape((chunks,) + dims, kind) for dims, kind in outs],
        scratch_shapes=[
            vmem((3 * model, model), bf16),
            vmem((model, BLOCK), f32),
            vmem((8, model, BLOCK), f32),
            vmem((model, CHUNK), bf16),
            vmem((CHUNK, model), bf16),
            vmem((BLOCK, model), bf16),
            vmem((model, BLOCK), bf16),
            vmem((BLOCK, BLOCK), f32),
            vmem((2, PAIRS, BLOCK, CHUNK), bf16),
        ],
        compiler_params=params,
        name="attend_first",
    )(x, inj, seg, first_weights)


def run_two(u1, c1, inj, cot, seg, first_weights, second_weights, per_row):
    chunks, model, _ = u1.shape
    tokens = chunks * CHUNK
    owners = second_weights.shape[0]
    ff = BLOCK * owners
    last = chunks - 1

    def up_then_hold(j):
        return jnp.minimum(j, last)

    def up_then_down(j):
        return jnp.where(j < chunks, j, 2 * chunks - 1 - j)

    def hold_then_down(j):
        return jnp.where(j < chunks, last, 2 * chunks - 1 - j)

    def lead(dims, order):
        return pl.BlockSpec((1,) + dims, lambda j: (order(j),) + (0,) * len(dims))

    def tok(order):
        return pl.BlockSpec((CHUNK, model), lambda j: (order(j), 0))

    square = (model, CHUNK)
    mlp_saved = [
        vmem((chunks,) + square, bf16),
        vmem((chunks, 1, CHUNK), f32),
        vmem((chunks,) + square, bf16),
        vmem((chunks, ff, CHUNK), bf16),
        vmem((chunks, ff, CHUNK), bf16),
    ]
    return pl.pallas_call(
        partial(kernel_two, per_row, chunks),
        grid=(2 * chunks,),
        in_specs=[
            lead(square, up_then_hold),
            lead(square, up_then_down),
            tok(up_then_hold),
            tok(hold_then_down),
            lead((1, CHUNK), up_then_hold),
            whole(first_weights),
            whole(second_weights),
        ],
        out_specs=[
            tok(up_then_hold),
            lead(square, hold_then_down),
            lead(square, hold_then_down),
            lead(square, hold_then_down),
            whole(second_weights),
            pl.BlockSpec((3 * model, model), lambda j: (0, 0)),
            pl.BlockSpec((model, BLOCK), lambda j: (0, 0)),
        ],
        out_shape=[
            shape((tokens, model), bf16),
            shape((chunks,) + square, f32),
            shape((chunks,) + square, bf16),
            shape((chunks,) + square, f32),
            shape(second_weights.shape, bf16),
            shape((3 * model, model), f32),
            shape((model, BLOCK), f32),
        ],
        scratch_shapes=[
            vmem((3 * model, model), bf16),
            vmem((model, BLOCK), f32),
            vmem((model, model), bf16),
            vmem((model, ff), bf16),
            vmem((model, ff), bf16),
            vmem((8, model, BLOCK), f32),
            vmem((ff, BLOCK), f32),
            vmem((ff, model), bf16),
            vmem((ff, model), bf16),
            vmem((model, model), bf16),
            vmem((model, 3 * model), bf16),
            vmem(square, f32),
            vmem(square, f32),
            vmem(square, f32),
            vmem(square, f32),
            vmem(square, bf16),
            vmem((CHUNK, model), bf16),
            vmem((BLOCK, model), bf16),
            vmem((model, BLOCK), bf16),
            vmem((BLOCK, BLOCK), f32),
            vmem((2, PAIRS, BLOCK, CHUNK), bf16),
            vmem((2, PAIRS, BLOCK, CHUNK), bf16),
        ]
        + mlp_saved
        + [
            vmem((chunks,) + square, bf16),
            vmem((chunks, 1, CHUNK), f32),
            vmem((chunks,) + square, bf16),
            vmem((chunks, 2 * model, CHUNK), bf16),
            vmem((chunks, CHUNK, model), bf16),
            vmem((chunks, 2 * PAIRS * BLOCK, CHUNK), bf16),
            vmem((chunks,) + square, bf16),
        ]
        + mlp_saved
        + [
            vmem(square, bf16),
            vmem((ff, CHUNK), bf16),
            vmem(square, bf16),
            vmem(square, bf16),
            vmem((3 * model, CHUNK), bf16),
            vmem((model, BLOCK), f32),
            vmem((model, BLOCK), f32),
            vmem((ff, model), f32),
            vmem((ff, model), f32),
            vmem((model, model), f32),
            vmem((ff, BLOCK), f32),
            vmem((8, model, BLOCK), f32),
            vmem((2 * PAIRS * BLOCK, CHUNK), bf16),
        ],
        compiler_params=params,
        name="middle",
    )(u1, c1, inj, cot, seg, first_weights, second_weights)


def run_three(saved, dm, dc, du2, first_weights, sum_qkv, vec_in):
    unit, inv, normed, qk, vtok, probs, ctx = saved
    chunks, model, _ = dm.shape
    tokens = chunks * CHUNK

    def at(j):
        return chunks - 1 - j

    def before(j):
        return jnp.maximum(chunks - 2 - j, 0)

    def lead(array):
        dims = array.shape[1:]
        return pl.BlockSpec((1,) + dims, lambda j: (at(j),) + (0,) * len(dims))

    tok = pl.BlockSpec((CHUNK, model), lambda j: (at(j), 0))
    return pl.pallas_call(
        partial(kernel_three, chunks),
        grid=(chunks,),
        in_specs=[
            lead(unit),
            lead(inv),
            lead(normed),
            lead(qk),
            pl.BlockSpec((1, model, BLOCK), lambda j: (before(j), 1, 1)),
            lead(vtok),
            pl.BlockSpec((1, BLOCK, model), lambda j: (before(j), 1, 0)),
            lead(probs),
            lead(ctx),
            lead(dm),
            lead(dc),
            lead(du2),
            whole(first_weights),
            whole(sum_qkv),
            whole(vec_in),
        ],
        out_specs=[
            tok,
            tok,
            whole(first_weights),
        ],
        out_shape=[
            shape((tokens, model), bf16),
            shape((tokens, model), bf16),
            shape(first_weights.shape, bf16),
        ],
        scratch_shapes=[
            vmem((3 * model, model), bf16),
            vmem((model, BLOCK), f32),
            vmem((8, model, BLOCK), f32),
            vmem((model, 3 * model), bf16),
            vmem((2, PAIRS, BLOCK, CHUNK), bf16),
            vmem((2, PAIRS, BLOCK, CHUNK), bf16),
            vmem((3 * model, CHUNK), bf16),
            vmem((model, BLOCK), f32),
            vmem((model, BLOCK), f32),
            vmem((model, CHUNK), f32),
            vmem((3 * model, model), f32),
            vmem((8, model, BLOCK), f32),
        ],
        compiler_params=params,
        name="attend_back",
    )(unit, inv, normed, qk, qk, vtok, vtok, probs, ctx, dm, dc, du2, first_weights, sum_qkv, vec_in)


OWNERS = 8


def pack_first(qkv_t, vectors):
    rows, model = qkv_t.shape
    count = rows // 96
    columns = [vector.reshape(count, 1, 32) for vector in vectors[:3] + vectors[4:]]
    columns.insert(8, vectors[3].reshape(count, 4, 32))
    block = jnp.concatenate(columns, axis=1).transpose(0, 2, 1)
    block = jnp.pad(block, ((0, 0), (0, 0), (0, model - block.shape[2])))
    return jnp.concatenate([qkv_t.reshape(count, 96, model), block], axis=1)


def unpack_vectors(block):
    columns = [block[:, :, index].reshape(-1) for index in range(8)]
    columns.insert(3, block[:, :, 8:12].transpose(0, 2, 1).reshape(-1))
    return columns


def pack_second(out_t, up, down_t):
    rows, model = out_t.shape
    count = rows // 32
    up_part = up.reshape(2, model // 2, count, 128).transpose(2, 1, 0, 3).reshape(count, 128, 256)
    down_part = down_t.reshape(count, 32, 4, 256).transpose(0, 2, 1, 3).reshape(count, 128, 256)
    return jnp.concatenate([out_t.reshape(count, 32, model), up_part, down_part], axis=1)


def unpack_second_grads(block):
    count, _, model = block.shape
    out_t = block[:, :32].reshape(count * 32, model)
    up = block[:, 32:160].reshape(count, 128, 2, 128).transpose(2, 1, 0, 3)
    down_t = block[:, 160:].reshape(count, 4, 32, 256).transpose(0, 2, 1, 3)
    return out_t, up.reshape(model, 128 * count), down_t.reshape(32 * count, 1024)


def exchange(block, axis, size, distance):
    return lax.ppermute(block, axis, [(k, k ^ distance) for k in range(size)])


def scatter_sum(parts):
    me = lax.axis_index("fsdp")
    total = lax.dynamic_index_in_dim(parts, me, 0, False).astype(f32)
    for distance in range(1, OWNERS):
        block = lax.dynamic_index_in_dim(parts, me ^ distance, 0, False)
        total = total + exchange(block, "fsdp", OWNERS, distance).astype(f32)
    groups = lax.all_gather(total.astype(bf16), "dp", axis=0)
    return jnp.sum(groups.astype(f32), axis=0)


def scatter_sum_any(full, axis):
    own = lax.psum_scatter(full, "fsdp", scatter_dimension=axis, tiled=True)
    return lax.psum(own, "dp")


def local(
    inputs,
    inject,
    segments,
    cotangent,
    qkv_weight,
    out_weight,
    up_weight,
    down_weight,
    *vectors,
):
    row_count, length, model = inputs.shape
    tokens = row_count * length
    chunks = tokens // CHUNK
    x = inputs.reshape(tokens, model)
    inj = inject.reshape(tokens, model)
    cot = cotangent.reshape(tokens, model)
    seg = segments.reshape(chunks, 1, CHUNK)
    per_row = length // CHUNK
    packed = out_weight.shape[1] * OWNERS == model
    if packed:
        first_own = pack_first(qkv_weight.T, vectors)[0]
        second_own = pack_second(out_weight.T, up_weight, down_weight.T)[0]
        first_weights = lax.all_gather(first_own, "fsdp", axis=0)
        second_weights = lax.all_gather(second_own, "fsdp", axis=0)
    else:

        def gathered(array, axis):
            return lax.all_gather(array, "fsdp", axis=axis, tiled=True)

        first_weights = pack_first(
            gathered(qkv_weight, 1).T, tuple(gathered(vector, 0) for vector in vectors)
        )
        second_weights = pack_second(
            gathered(out_weight, 1).T, gathered(up_weight, 1), gathered(down_weight, 1).T
        )
    u1, *saved = run_one(x, inj, seg, first_weights, per_row)
    result, dm, dc, du2, second_grads, sum_qkv, vec_mid = run_two(
        u1, saved[-1], inj, cot, seg, first_weights, second_weights, per_row
    )
    if packed:
        second_sum = scatter_sum(second_grads)
    grad_inputs, grad_inject, first_grads = run_three(
        saved, dm, dc, du2, first_weights, sum_qkv, vec_mid
    )
    if packed:
        first_sum = scatter_sum(first_grads)[None]
        out_t, up, down_t = unpack_second_grads(second_sum[None])
        weight_grads = (first_sum[0, :96].T, out_t.T, up, down_t.T)
        vector_grads = unpack_vectors(first_sum[:, 96:])
    else:
        first_all = first_grads.astype(f32)
        out_t, up, down_t = unpack_second_grads(second_grads.astype(f32))
        weight_grads = tuple(
            scatter_sum_any(grad, 1)
            for grad in (first_all[:, :96].reshape(3 * model, model).T, out_t.T, up, down_t.T)
        )
        vector_grads = [scatter_sum_any(grad, 0) for grad in unpack_vectors(first_all[:, 96:])]
    dims = inputs.shape
    return (
        result.reshape(dims),
        grad_inputs.reshape(dims),
        grad_inject.reshape(dims),
        *weight_grads,
        *vector_grads,
    )


def solution(mesh):
    placed = (
        P(("dp", "fsdp"), None, None),
        P(("dp", "fsdp"), None, None),
        P(("dp", "fsdp"), None),
        P(("dp", "fsdp"), None, None),
        P(None, "fsdp"),
        P(None, "fsdp"),
        P(None, "fsdp"),
        P(None, "fsdp"),
        P("fsdp"),
        P("fsdp"),
        P("fsdp"),
        P("fsdp"),
        P("fsdp"),
        P("fsdp"),
        P("fsdp"),
        P("fsdp"),
        P("fsdp"),
    )
    return jax.shard_map(
        local,
        mesh=mesh,
        in_specs=placed,
        out_specs=(
            P(("dp", "fsdp"), None, None),
            P(("dp", "fsdp"), None, None),
            P(("dp", "fsdp"), None, None),
            P(None, "fsdp"),
            P(None, "fsdp"),
            P(None, "fsdp"),
            P(None, "fsdp"),
            P("fsdp"),
            P("fsdp"),
            P("fsdp"),
            P("fsdp"),
            P("fsdp"),
            P("fsdp"),
            P("fsdp"),
            P("fsdp"),
            P("fsdp"),
        ),
        check_vma=False,
    )
```

```python
import math
from functools import partial

import jax
import jax.numpy as jnp
from jax import lax
from jax.experimental import pallas as pl
from jax.experimental.pallas import tpu as pltpu
from jax.sharding import PartitionSpec as P

HEADS = 8
HD = 32
CHUNK = 256
BLOCK = 128
PAIRS = HEADS // 2
OWNERS = 8

norm_eps = 1e-05
masked_score = -1e30
score_scale = HD ** (-0.5)
exp2_scale = score_scale * math.log2(math.e)
gelu_c0 = math.sqrt(2.0 / math.pi)
gelu_c1 = 0.044715 * gelu_c0

f32 = jnp.float32
bf16 = jnp.bfloat16

(
    Q_BIAS,
    V_BIAS,
    OUT_BIAS,
    DOWN_BIAS,
    ATTN_GAIN,
    ATTN_SHIFT,
    MLP_GAIN,
    MLP_SHIFT,
    UP_BIAS,
) = range(9)


def mm(left_op, right_op):
    return lax.dot_general(
        left_op, right_op, (((1,), (0,)), ((), ())), preferred_element_type=f32
    )


def mm_nt(left_op, right_op):
    return lax.dot_general(
        left_op, right_op, (((1,), (1,)), ((), ())), preferred_element_type=f32
    )


def identity(size):
    rows = lax.broadcasted_iota(jnp.int32, (size, size), 0)
    cols = lax.broadcasted_iota(jnp.int32, (size, size), 1)
    return jnp.where(rows == cols, 1.0, 0.0).astype(bf16)


def flipped(block):
    return mm_nt(identity(block.shape[1]), block).astype(bf16)


def half(index):
    return slice(index * BLOCK, (index + 1) * BLOCK)


def spread(column):
    return jnp.broadcast_to(column, (column.shape[0], BLOCK))


def row_sum(values):
    return jnp.sum(values, axis=0, keepdims=True)


def norm_forward(values, gain, shift):
    scale = 1.0 / values.shape[0]
    centre = values - row_sum(values) * scale
    inverse = lax.rsqrt(row_sum(centre * centre) * scale + norm_eps)
    unit = centre * inverse
    return unit, inverse, unit * gain + shift


def norm_backward(grad_normed, unit, inverse, gain):
    scale = 1.0 / unit.shape[0]
    scaled = grad_normed * gain
    gain_term = grad_normed * unit
    mean_scaled = row_sum(scaled) * scale
    mean_unit = row_sum(gain_term * gain) * scale
    return inverse * (scaled - mean_scaled - unit * mean_unit), gain_term


def below_mask():
    key_at = lax.broadcasted_iota(jnp.int32, (BLOCK, BLOCK), 0)
    query_at = lax.broadcasted_iota(jnp.int32, (BLOCK, BLOCK), 1)
    return key_at <= query_at, key_at == query_at


def set_masks(masks):
    below, _ = below_mask()
    own = jnp.where(twice(below), 1.0, 0.0)
    masks[0] = (1.0 - own).astype(bf16)
    masks[1] = own.astype(bf16)


def stack(side, pair):
    base = (side * PAIRS + pair) * BLOCK
    return slice(base, base + BLOCK)


def twice(values):
    return jnp.concatenate([values, values], axis=1)


def set_pairs(dest, source, lanes):
    for pair in range(PAIRS):
        base = 64 * (pair % 2)
        for side in range(2):
            rows = source[64 * pair + HD * side : 64 * pair + HD * (side + 1), :]
            dest[pair, base + HD * side : base + HD * (side + 1), half(side)] = rows[:, lanes]


def weave(*streams):
    order = []
    for index, (_, steps) in enumerate(streams):
        order += [((turn + 0.5) / steps, index) for turn in range(steps)]
    for _, index in sorted(order):
        next(streams[index][0], None)
    for generator, _ in streams:
        for _ in generator:
            pass


def project(u_ref, bcast, w_qkv, out):
    unit_o, inv_o, normed_o, qk_o, vtok_o, v_s, ktok_s = out
    model = w_qkv.shape[1]
    for side in range(2):
        unit, inverse, normed = norm_forward(
            u_ref[:, half(side)], bcast[ATTN_GAIN], bcast[ATTN_SHIFT]
        )
        unit_o[:, half(side)] = unit.astype(bf16)
        inv_o[:, half(side)] = inverse
        normed_o[:, half(side)] = normed.astype(bf16)
        yield
    eye = identity(model)
    normed = normed_o[...]
    rows = mm(w_qkv[model : 2 * model, :], normed)
    qk_o[model:, :] = rows.astype(bf16)
    yield
    rows = mm(w_qkv[2 * model :, :], normed)
    v_s[...] = (rows + twice(bcast[V_BIAS])).astype(bf16)
    yield
    rows = mm(w_qkv[:model, :], normed)
    qk_o[:model, :] = (rows + twice(bcast[Q_BIAS])).astype(bf16)
    yield
    ktok_s[...] = mm_nt(eye, qk_o[model:, :]).astype(bf16)
    yield
    vtok_o[...] = mm_nt(eye, v_s[...]).astype(bf16)
    yield


def hand_over(qk, v_s, ktok_s, q_pairs, key_win, value_win):
    key_win[:BLOCK, :] = key_win[CHUNK:, :]
    value_win[:, :BLOCK] = value_win[:, CHUNK:]
    key_win[BLOCK:, :] = ktok_s[...]
    value_win[:, BLOCK:] = v_s[...]
    for side in range(2):
        set_pairs(q_pairs.at[side], qk, half(side))


def attend(seg_ref, segprev, masks, q_pairs, key_win, value_win, probs_o, context_o):
    below, diagonal = below_mask()
    below2 = twice(below)
    items = [(side, pair) for side in range(2) for pair in range(PAIRS)]
    biases, scores, windows = {}, {}, {}
    for turn in range(len(items) + 2):
        if turn < len(items):
            side, pair = items[turn]
            span = slice(side * BLOCK, side * BLOCK + CHUNK)
            scores[turn] = mm(key_win[span, half(pair // 2)], q_pairs[side, pair])
            if pair == 0:
                seg_row = seg_ref[:, half(side)].astype(f32)
                seg_col = jnp.transpose(jnp.broadcast_to(seg_row, (BLOCK, BLOCK)))
                seg_key = jnp.where(below, seg_col, segprev[...])
                segprev[...] = seg_col
                allowed = ((seg_key == seg_row) & (seg_row >= 0)) | diagonal
                biases[side] = jnp.where(allowed, 0.0, masked_score)
        if turn >= 2:
            side, pair = items[turn - 2]
            lanes = half(side)
            span = slice(side * BLOCK, side * BLOCK + CHUNK)
            both = mm(value_win[64 * pair : 64 * (pair + 1), span], windows.pop(turn - 2))
            context_o[64 * pair : 64 * pair + HD, lanes] = both[:HD, :BLOCK].astype(bf16)
            context_o[64 * pair + HD : 64 * (pair + 1), lanes] = both[HD:, BLOCK:].astype(bf16)
        if 1 <= turn <= len(items):
            side, pair = items[turn - 1]
            table = scores.pop(turn - 1)
            folded = jnp.where(below2, table[BLOCK:], table[:BLOCK]) * exp2_scale + twice(
                biases[side]
            )
            top = jnp.max(folded, axis=0, keepdims=True)
            weights = jnp.exp2(folded - top)
            probs = (weights * (1.0 / row_sum(weights))).astype(bf16)
            probs_o[stack(side, pair), :] = probs
            windows[turn - 1] = jnp.concatenate([probs * masks[0], probs * masks[1]], axis=0)
        yield


def feed_forward(u_ref, m_ref, context, bcast, up_bias, w_out, w_up, w_down, out, finish):
    unit_o, inv_o, normed_o, hidden_o, slope_o = out
    mixed = mm(w_out[...], context)
    yield
    for side in range(2):
        lanes = half(side)
        after = u_ref[:, lanes] + (mixed[:, lanes] + bcast[OUT_BIAS])
        m_ref[:, lanes] = after
        unit, inverse, normed = norm_forward(after, bcast[MLP_GAIN], bcast[MLP_SHIFT])
        unit_o[:, lanes] = unit.astype(bf16)
        inv_o[:, lanes] = inverse
        normed_o[:, lanes] = normed.astype(bf16)
        yield
    normed = normed_o[...]
    parts = w_up.shape[0] // CHUNK

    def rows_of(part):
        return slice(part * CHUNK, (part + 1) * CHUNK)

    pre = mm(w_up[rows_of(0), :], normed)
    for part in range(parts):
        rows = rows_of(part)
        current = pre
        if part + 1 < parts:
            pre = mm(w_up[rows_of(part + 1), :], normed)
        for piece in range(2):
            inner = slice(piece * BLOCK, (piece + 1) * BLOCK)
            outer = slice(part * CHUNK + piece * BLOCK, part * CHUNK + (piece + 1) * BLOCK)
            z = (current[inner, :] + twice(up_bias[outer, :])).astype(bf16)
            z2 = z * z
            gate = 0.5 * jnp.tanh(z * (gelu_c0 + gelu_c1 * z2)) + 0.5
            act = z * gate
            slope = gate + (act * (1.0 - gate)) * (2.0 * gelu_c0 + 6.0 * gelu_c1 * z2)
            hidden_o[outer, :] = act
            slope_o[outer, :] = slope
            yield
    total = mm(w_down[...], hidden_o[...])
    yield
    for side in range(2):
        lanes = half(side)
        finish(side, m_ref[:, lanes] + (total[:, lanes] + bcast[DOWN_BIAS]))
    yield


def back_feed_forward(g_ref, dm_ref, saved, bcast, weights, sums, dy_s, dz_s, do_ref):
    unit, inverse, normed, hidden, slope = saved
    w_down_n, w_up_n = weights
    sum_down, sum_up, sum_up_bias, sum_vec = sums
    for side in range(2):
        lanes = half(side)
        grad = g_ref[:, lanes]
        sum_vec[DOWN_BIAS] += grad
        dy_s[:, lanes] = grad.astype(bf16)
    dy = dy_s[...]
    yield
    parts = w_down_n.shape[0] // CHUNK

    def rows_of(part):
        return slice(part * CHUNK, (part + 1) * CHUNK)

    ahead = mm(w_down_n[rows_of(0), :], dy)
    for part in range(parts):
        rows = rows_of(part)
        current = ahead
        if part + 1 < parts:
            ahead = mm(w_down_n[rows_of(part + 1), :], dy)
        dz = current.astype(bf16) * slope[rows, :]
        dz_s[rows, :] = dz
        wide = dz.astype(f32)
        sum_up_bias[rows, :] += wide[:, :BLOCK] + wide[:, BLOCK:]
        yield
    total = mm(w_up_n[...], dz_s[...])
    yield
    sum_down[...] += mm_nt(hidden[...], dy)
    yield
    units = unit[...]
    for side in range(2):
        lanes = half(side)
        grad_normed = total[:, lanes]
        back, gain_term = norm_backward(
            grad_normed, units[:, lanes].astype(f32), inverse[:, lanes], bcast[MLP_GAIN]
        )
        sum_vec[MLP_GAIN] += gain_term
        sum_vec[MLP_SHIFT] += grad_normed
        dm = g_ref[:, lanes] + back
        if dm_ref is not None:
            dm_ref[:, lanes] = dm
        sum_vec[OUT_BIAS] += dm
        do_ref[:, lanes] = dm.astype(bf16)
        yield
    sum_up[...] += mm_nt(dz_s[...], normed[...])
    yield


def back_out(do_ref, context, w_out_n, sum_out, dc_ref):
    grad = do_ref[...]
    dc_ref[...] = mm(w_out_n[...], grad).astype(bf16)
    yield
    sum_out[...] += mm_nt(grad, context[...])
    yield


def back_attention(
    dc_ref, context, qk, kt_prev, vtok, vtok_prev, probs_ref, masks, pairs, carry, dqkv
):
    q_pairs, c_pairs = pairs
    dk_carry, dv_carry = carry
    model = vtok.shape[1]
    below, _ = below_mask()
    below2 = twice(below)
    items = [(side, pair) for side in (1, 0) for pair in range(PAIRS)]
    key_win, value_win, weighted, grads, windows = {}, {}, {}, {}, {}
    for turn in range(len(items) + 2):
        if turn < len(items):
            side, pair = items[turn]
            if pair == 0:
                lanes = half(side)
                set_pairs(q_pairs.at[side], qk, lanes)
                set_pairs(c_pairs.at[side], dc_ref, lanes)
                weighted[side] = dc_ref[...][:, lanes].astype(f32) * context[...][:, lanes].astype(f32)
                if side == 1:
                    key_win[side] = qk[model:, :]
                    value_win[side] = vtok[...]
                else:
                    key_win[side] = jnp.concatenate([kt_prev[...], qk[model:, :][:, :BLOCK]], axis=1)
                    value_win[side] = jnp.concatenate([vtok_prev[...], vtok[:BLOCK, :]], axis=0)
            grads[turn] = mm(value_win[side][:, half(pair // 2)], c_pairs[side, pair])
        if turn >= 2:
            side, pair = items[turn - 2]
            lanes = half(side)
            base = 64 * (pair % 2)
            rows = slice(64 * pair, 64 * (pair + 1))
            prob_win, grad_win = windows.pop(turn - 2)
            dq = mm(key_win[side][rows, :], grad_win) * score_scale
            dk = mm_nt(q_pairs[side, pair, base : base + 64, :], grad_win) * score_scale
            dv = mm_nt(c_pairs[side, pair, base : base + 64, :], prob_win)
            dqkv[64 * pair : 64 * pair + HD, lanes] = dq[:HD, :BLOCK].astype(bf16)
            dqkv[64 * pair + HD : 64 * (pair + 1), lanes] = dq[HD:, BLOCK:].astype(bf16)
            krows = slice(model + 64 * pair, model + 64 * (pair + 1))
            vrows = slice(2 * model + 64 * pair, 2 * model + 64 * (pair + 1))
            dqkv[krows, lanes] = (dk[:, BLOCK:] + dk_carry[rows, :]).astype(bf16)
            dqkv[vrows, lanes] = (dv[:, BLOCK:] + dv_carry[rows, :]).astype(bf16)
            dk_carry[rows, :] = dk[:, :BLOCK]
            dv_carry[rows, :] = dv[:, :BLOCK]
        if 1 <= turn <= len(items):
            side, pair = items[turn - 1]
            table = grads.pop(turn - 1)
            folded = jnp.where(below2, table[BLOCK:], table[:BLOCK])
            product = weighted[side]
            delta = jnp.concatenate(
                [
                    row_sum(product[64 * pair : 64 * pair + HD]),
                    row_sum(product[64 * pair + HD : 64 * (pair + 1)]),
                ],
                axis=1,
            )
            probs = probs_ref[stack(side, pair), :]
            grad_scores = probs * (folded - delta).astype(bf16)
            prob_win = jnp.concatenate([probs * masks[0], probs * masks[1]], axis=0)
            grad_win = jnp.concatenate([grad_scores * masks[0], grad_scores * masks[1]], axis=0)
            windows[turn - 1] = (prob_win, grad_win)
        yield


def back_project(dm_ref, dqkv, unit, inverse, normed, bcast, w_qkv_n, sum_qkv, sum_vec, finish):
    grads = dqkv[...]
    model = dm_ref.shape[0]
    total = mm(w_qkv_n[...], grads)
    for side in range(2):
        sum_vec[Q_BIAS] += grads[:model, half(side)].astype(f32)
        sum_vec[V_BIAS] += grads[2 * model :, half(side)].astype(f32)
    yield
    sum_qkv[...] += mm_nt(grads, normed[...])
    yield
    units = unit[...]
    for side in range(2):
        lanes = half(side)
        grad_normed = total[:, lanes]
        back, gain_term = norm_backward(
            grad_normed, units[:, lanes].astype(f32), inverse[:, lanes], bcast[ATTN_GAIN]
        )
        sum_vec[ATTN_GAIN] += gain_term
        sum_vec[ATTN_SHIFT] += grad_normed
        finish(side, dm_ref[:, lanes].astype(f32) + back)
        yield


def unpack_first(packed, w_qkv, vec):
    owners, _, model = packed.shape
    rows = 3 * model // owners
    for owner in range(owners):
        w_qkv[rows * owner : rows * (owner + 1), :] = packed[owner, :rows, :]
        vec[32 * owner : 32 * (owner + 1), :] = packed[owner, rows:, :BLOCK].astype(f32)


def unpack_second(packed, w_out, w_up_n, w_down):
    owners = packed.shape[0]
    for owner in range(owners):
        rows = slice(32 * owner, 32 * (owner + 1))
        w_out[rows, :] = packed[owner, :32, :]
        for side in range(2):
            w_up_n[half(side), half(owner)] = packed[owner, 32:160, half(side)]
        for part in range(4):
            w_down[rows, part * CHUNK : (part + 1) * CHUNK] = packed[
                owner, 160 + 32 * part : 192 + 32 * part, :
            ]


def spread_vectors(vec, bcast, which):
    values = vec[...]
    for index in which:
        bcast[index] = spread(values[:, index : index + 1])


def token_sum(left_tokens, right_tokens, dest):
    eye = identity(left_tokens.shape[1])
    dest[...] = mm_nt(eye, left_tokens) + mm_nt(eye, right_tokens)


def kernel_one(
    rows_chunks, chunks, x, inj, seg, first_weights,
    unit_o, inv_o, normed_o, qk_o, vtok_o, probs_o, context_o,
    w_qkv, vec, bcast, u_s, v_s, ktok_s, key_win, value_win, segprev, q_pairs, masks,
):
    step = pl.program_id(0)

    @pl.when(step == 0)
    def _():
        unpack_first(first_weights, w_qkv, vec)
        spread_vectors(vec, bcast, (Q_BIAS, V_BIAS, ATTN_GAIN, ATTN_SHIFT))
        key_win[...] = jnp.zeros_like(key_win)
        value_win[...] = jnp.zeros_like(value_win)
        q_pairs[...] = jnp.zeros_like(q_pairs)
        set_masks(masks)

    @pl.when(lax.rem(step - 1, rows_chunks) == 0)
    def _():
        segprev[...] = jnp.full(segprev.shape, -2.0, f32)

    def first():
        token_sum(x[...], inj[...], u_s)
        yield
        yield from project(
            u_s, bcast, w_qkv,
            [r.at[0] for r in (unit_o, inv_o, normed_o, qk_o, vtok_o)] + [v_s, ktok_s],
        )

    def second():
        return attend(seg.at[0], segprev, masks, q_pairs, key_win, value_win, probs_o.at[0], context_o.at[0])

    def finish():
        hand_over(qk_o.at[0], v_s, ktok_s, q_pairs, key_win, value_win)

    @pl.when(step == 0)
    def _():
        weave((first(), 8))
        finish()

    @pl.when((step > 0) & (step < chunks))
    def _():
        weave((second(), 10), (first(), 8))
        finish()

    @pl.when(step == chunks)
    def _():
        weave((second(), 10))


def kernel_two(
    rows_chunks, chunks,
    x, c1, inj, cot, seg, first_weights, second_weights,
    result_o, dm_o, dc_o, du_o, grads_o, sum_qkv_o, vec_o,
    w_qkv, vec, w_out, w_up_n, w_down, bcast, up_bias, w_up, w_down_n, w_out_n, w_qkv_n,
    u1_s, u_s, m1_s, m2_s, g1_s, g2_s, v_s, ktok_s, key_win, value_win, segprev, q_pairs, c_pairs, masks,
    unit_m1, inv_m1, norm_m1, hid1, slope1,
    u2, dm2, unit2, inv2, norm2, qk2, vtok2, probs2, ctx2,
    unit_m2, inv_m2, norm_m2, hid2, slope2,
    dy1_s, dz1_s, dy2_s, dz2_s, do2_s, dc_s, dqkv_s, dk_carry, dv_carry, probs_s, slope1_s, slope2_s, unit_m1_s, unit_m2_s, unit2_s,
    norm_m1_s, norm_m2_s, norm2_s, inv_m1_s, inv_m2_s, inv2_s, dm2_s,
    sum_down, sum_up, sum_out, sum_up_bias, sum_vec,
):
    step = pl.program_id(0)
    model = w_out.shape[0]
    ff = w_up.shape[0]
    turn = chunks + 2

    @pl.when(step == 0)
    def _():
        unpack_first(first_weights, w_qkv, vec)
        unpack_second(second_weights, w_out, w_up_n, w_down)
        spread_vectors(vec, bcast, range(8))
        values = vec[...]
        for owner in range(ff // BLOCK):
            for col in range(4):
                up_bias[BLOCK * owner + 32 * col : BLOCK * owner + 32 * (col + 1), :] = spread(
                    values[32 * owner : 32 * (owner + 1), UP_BIAS + col : UP_BIAS + col + 1]
                )
        for part in range(ff // CHUNK):
            rows = slice(part * CHUNK, (part + 1) * CHUNK)
            w_up[rows, :] = flipped(w_up_n[:, rows])
            w_down_n[rows, :] = flipped(w_down[:, rows])
        w_out_n[...] = flipped(w_out[...])
        for part in range(3):
            rows = slice(part * model, (part + 1) * model)
            w_qkv_n[:, rows] = flipped(w_qkv[rows, :])
        for ref in (key_win, value_win, q_pairs, c_pairs, dk_carry, dv_carry,
                    sum_down, sum_up, sum_out, sum_up_bias, sum_vec):
            ref[...] = jnp.zeros_like(ref)
        sum_qkv_o[...] = jnp.zeros_like(sum_qkv_o)
        set_masks(masks)

    @pl.when(lax.rem(step - 1, rows_chunks) == 0)
    def _():
        segprev[...] = jnp.full(segprev.shape, -2.0, f32)

    def mlp_one():
        i = step

        def finish(side, h):
            again = mm_nt(identity(model), inj[half(side), :])
            u_s[:, half(side)] = h + again
            u2[i, :, half(side)] = h + again

        token_sum(x[...], inj[...], u1_s)
        yield
        yield from feed_forward(
            u1_s, m1_s, c1[0], bcast, up_bias, w_out, w_up, w_down,
            [r.at[i] for r in (unit_m1, inv_m1, norm_m1, hid1, slope1)], finish,
        )
        out = [r.at[i] for r in (unit2, inv2, norm2, qk2, vtok2)]
        yield from project(u_s, bcast, w_qkv, out + [v_s, ktok_s])

    def attention():
        i = step - 1
        return attend(seg.at[0], segprev, masks, q_pairs, key_win, value_win, probs2.at[i], ctx2.at[i])

    def mlp_two():
        i = step - 2

        def finish(side, h):
            low = h.astype(bf16)
            result_o[half(side), :] = mm_nt(identity(BLOCK), low).astype(bf16)

        yield from feed_forward(
            u2.at[i], m2_s, ctx2[i], bcast, up_bias, w_out, w_up, w_down,
            [r.at[i] for r in (unit_m2, inv_m2, norm_m2, hid2, slope2)], finish,
        )

    lengths = {mlp_one: 21, attention: 10, mlp_two: 13}

    def forward_turn(*which):
        weave(*[(stream(), lengths[stream]) for stream in which])
        if mlp_one in which:
            hand_over(qk2.at[step], v_s, ktok_s, q_pairs, key_win, value_win)

    @pl.when(step == 0)
    def _():
        forward_turn(mlp_one)

    @pl.when(step == 1)
    def _():
        forward_turn(attention, mlp_one)

    @pl.when((step >= 2) & (step < chunks))
    def _():
        forward_turn(mlp_two, attention, mlp_one)

    @pl.when(step == chunks)
    def _():
        forward_turn(mlp_two, attention)

    @pl.when(step == chunks + 1)
    def _():
        forward_turn(mlp_two)

    @pl.when(step == turn - 1)
    def _():
        slope2_s[...] = slope2[chunks - 1]
        unit_m2_s[...] = unit_m2[chunks - 1]
        norm_m2_s[...] = norm_m2[chunks - 1]
        inv_m2_s[...] = inv_m2[chunks - 1]

    at = step - turn
    sums = (sum_down, sum_up, sum_up_bias, sum_vec)

    def back_mlp_two():
        i = chunks - 1 - at
        g2_s[...] = mm_nt(identity(model), cot[...])
        yield
        yield from back_feed_forward(
            g2_s, dm2.at[i], [unit_m2_s, inv_m2_s, norm_m2_s, hid2.at[i], slope2_s],
            bcast, (w_down_n, w_up_n), sums, dy2_s, dz2_s, do2_s,
        )
        yield from back_out(do2_s, ctx2.at[i], w_out_n, sum_out, dc_s)

    def back_attend():
        i = chunks - at
        before = jnp.maximum(i - 1, 0)
        return back_attention(
            dc_s, ctx2.at[i], qk2.at[i], qk2.at[before, model:, BLOCK:], vtok2.at[i],
            vtok2.at[before, BLOCK:, :], probs_s, masks, (q_pairs, c_pairs),
            (dk_carry, dv_carry), dqkv_s,
        )

    def back_rest():
        i = chunks + 1 - at

        def finish(side, du):
            g1_s[:, half(side)] = du
            du_o[0, :, half(side)] = du.astype(bf16)

        yield from back_project(
            dm2_s, dqkv_s, unit2_s, inv2_s, norm2_s, bcast, w_qkv_n,
            sum_qkv_o, sum_vec, finish,
        )
        yield from back_feed_forward(
            g1_s, None, [unit_m1_s, inv_m1_s, norm_m1_s, hid1.at[i], slope1_s],
            bcast, (w_down_n, w_up_n), sums, dy1_s, dz1_s, dm_o.at[0],
        )
        yield from back_out(dm_o.at[0], c1.at[0], w_out_n, sum_out, dc_o.at[0])

    lengths_back = {back_mlp_two: 13, back_attend: 10, back_rest: 16}

    def backward_turn(*which):
        weave(*[(stream(), lengths_back[stream]) for stream in which])
        if back_mlp_two in which:
            probs_s[...] = probs2[chunks - 1 - at]
            slope2_s[...] = slope2[jnp.maximum(chunks - 2 - at, 0)]
            unit_m2_s[...] = unit_m2[jnp.maximum(chunks - 2 - at, 0)]
            norm_m2_s[...] = norm_m2[jnp.maximum(chunks - 2 - at, 0)]
            inv_m2_s[...] = inv_m2[jnp.maximum(chunks - 2 - at, 0)]
        if back_attend in which:
            slope1_s[...] = slope1[chunks - at]
            unit_m1_s[...] = unit_m1[chunks - at]
            unit2_s[...] = unit2[chunks - at]
            norm_m1_s[...] = norm_m1[chunks - at]
            norm2_s[...] = norm2[chunks - at]
            dm2_s[...] = dm2[chunks - at]
            inv_m1_s[...] = inv_m1[chunks - at]
            inv2_s[...] = inv2[chunks - at]

    @pl.when(at == 0)
    def _():
        backward_turn(back_mlp_two)

    @pl.when(at == 1)
    def _():
        backward_turn(back_attend, back_mlp_two)

    @pl.when((at >= 2) & (at < chunks))
    def _():
        backward_turn(back_rest, back_attend, back_mlp_two)

    @pl.when(at == chunks)
    def _():
        backward_turn(back_rest, back_attend)

    @pl.when(at == chunks + 1)
    def _():
        backward_turn(back_rest)
        owners = OWNERS
        for part in range(ff // CHUNK):
            rows = slice(part * CHUNK, (part + 1) * CHUNK)
            up_block = flipped(sum_up[rows, :].astype(bf16))
            for within in range(2):
                for side in range(2):
                    grads_o[within, part, 32:160, half(side)] = up_block[
                        half(side), half(within)
                    ]
            down_block = flipped(sum_down[rows, :].astype(bf16))
            for owner in range(owners):
                grads_o[owner % 2, owner // 2, 160 + 32 * part : 192 + 32 * part, :] = down_block[
                    32 * owner : 32 * (owner + 1), :
                ]
        for owner in range(owners):
            grads_o[owner % 2, owner // 2, :32, :] = sum_out[32 * owner : 32 * (owner + 1), :].astype(bf16)
        vec_o[...] = jnp.zeros_like(vec_o)
        for index in range(8):
            vec_o[:, index : index + 1] = jnp.sum(sum_vec[index], axis=1, keepdims=True)
        for owner in range(ff // BLOCK):
            for col in range(4):
                vec_o[32 * owner : 32 * (owner + 1), UP_BIAS + col : UP_BIAS + col + 1] = jnp.sum(
                    sum_up_bias[BLOCK * owner + 32 * col : BLOCK * owner + 32 * (col + 1), :],
                    axis=1, keepdims=True,
                )


def kernel_three(
    chunks,
    unit, inv, normed, qk, kt_prev, vtok, vtok_prev, probs, ctx, dm, dc, du2, first_weights, sum_qkv_i, vec_i,
    gin_o, ginj_o, grads_o,
    w_qkv, vec, bcast, w_qkv_n, q_pairs, c_pairs, masks, dqkv_s, dk_carry, dv_carry, sum_qkv, sum_vec,
):
    step = pl.program_id(0)
    model = w_qkv.shape[1]
    owners = OWNERS

    @pl.when(step == 0)
    def _():
        unpack_first(first_weights, w_qkv, vec)
        spread_vectors(vec, bcast, (ATTN_GAIN,))
        for part in range(3):
            rows = slice(part * model, (part + 1) * model)
            w_qkv_n[:, rows] = flipped(w_qkv[rows, :])
        for ref in (q_pairs, c_pairs, dk_carry, dv_carry, sum_vec):
            ref[...] = jnp.zeros_like(ref)
        sum_qkv[...] = sum_qkv_i[...]
        set_masks(masks)

    def attention():
        return back_attention(
            dc.at[0], ctx.at[0], qk.at[0], kt_prev.at[0], vtok.at[0], vtok_prev.at[0], probs.at[0],
            masks, (q_pairs, c_pairs), (dk_carry, dv_carry), dqkv_s,
        )

    def rest():
        eye = identity(BLOCK)

        def finish(side, du):
            gin_o[half(side), :] = mm_nt(eye, du.astype(bf16)).astype(bf16)
            both = du + du2[0, :, half(side)].astype(f32)
            ginj_o[half(side), :] = mm_nt(eye, both.astype(bf16)).astype(bf16)

        return back_project(
            dm.at[0], dqkv_s, unit.at[0], inv.at[0], normed.at[0], bcast, w_qkv_n,
            sum_qkv, sum_vec, finish,
        )

    @pl.when(step == 0)
    def _():
        weave((attention(), 10))

    @pl.when((step > 0) & (step < chunks))
    def _():
        weave((rest(), 4), (attention(), 10))

    @pl.when(step == chunks)
    def _():
        weave((rest(), 4))
        rows = 3 * model // owners
        vec[...] = vec_i[...]
        for index in (Q_BIAS, V_BIAS, ATTN_GAIN, ATTN_SHIFT):
            vec[:, index : index + 1] += jnp.sum(sum_vec[index], axis=1, keepdims=True)
        for owner in range(owners):
            grads_o[owner % 2, owner // 2, :rows, :] = sum_qkv[rows * owner : rows * (owner + 1), :].astype(bf16)
            grads_o[owner % 2, owner // 2, rows:, :] = twice(vec[32 * owner : 32 * (owner + 1), :].astype(bf16))


def cost(microseconds):
    return pl.CostEstimate(
        flops=int(microseconds * 1.1e9), bytes_accessed=int(microseconds * 3e6), transcendentals=0
    )


def whole(array):
    zeros = (0,) * len(array.shape)
    return pl.BlockSpec(array.shape, lambda j: zeros)


def shape(dims, kind):
    return jax.ShapeDtypeStruct(dims, kind)


def vmem(dims, kind):
    return pltpu.VMEM(dims, kind)


params = pltpu.CompilerParams(vmem_limit_bytes=62 * 1024 * 1024)


def run_one(x, inj, seg, first_weights, per_row):
    tokens, model = x.shape
    chunks = tokens // CHUNK
    last = chunks - 1

    def early(j):
        return jnp.minimum(j, last)

    def late(j):
        return jnp.maximum(j - 1, 0)

    def lead(dims, order):
        return pl.BlockSpec((1,) + dims, lambda j: (order(j),) + (0,) * len(dims))

    token_spec = pl.BlockSpec((CHUNK, model), lambda j: (early(j), 0))
    outs = [
        ((model, CHUNK), bf16, early),
        ((1, CHUNK), f32, early),
        ((model, CHUNK), bf16, early),
        ((2 * model, CHUNK), bf16, early),
        ((CHUNK, model), bf16, early),
        ((2 * PAIRS * BLOCK, CHUNK), bf16, late),
        ((model, CHUNK), bf16, late),
    ]
    return pl.pallas_call(
        partial(kernel_one, per_row, chunks),
        grid=(chunks + 1,),
        in_specs=[token_spec, token_spec, lead((1, CHUNK), late), whole(first_weights)],
        out_specs=[lead(dims, order) for dims, _, order in outs],
        out_shape=[shape((chunks,) + dims, kind) for dims, kind, _ in outs],
        scratch_shapes=[
            vmem((3 * model, model), bf16),
            vmem((model, BLOCK), f32),
            vmem((8, model, BLOCK), f32),
            vmem((model, CHUNK), f32),
            vmem((model, CHUNK), bf16),
            vmem((CHUNK, model), bf16),
            vmem((CHUNK + BLOCK, model), bf16),
            vmem((model, CHUNK + BLOCK), bf16),
            vmem((BLOCK, BLOCK), f32),
            vmem((2, PAIRS, BLOCK, CHUNK), bf16),
            vmem((2, BLOCK, CHUNK), bf16),
        ],
        compiler_params=params,
        name="attend_first",
        cost_estimate=cost(14),
    )(x, inj, seg, first_weights)


def run_two(x, c1, inj, cot, seg, first_weights, second_weights, per_row):
    tokens, model = x.shape
    chunks = tokens // CHUNK
    owners = second_weights.shape[0]
    ff = BLOCK * owners
    second_grads = shape((2, owners // 2) + second_weights.shape[1:], bf16)
    last = chunks - 1
    turn = chunks + 2

    def up(lag):
        return lambda j: jnp.clip(j - lag, 0, last)

    def down(lag):
        return lambda j: jnp.clip(last - (j - turn - lag), 0, last)

    def up_then_down(j):
        return jnp.where(j < turn, jnp.minimum(j, last), jnp.clip(last - (j - turn - 2), 0, last))

    def lead(dims, order):
        return pl.BlockSpec((1,) + dims, lambda j: (order(j),) + (0,) * len(dims))

    def tok(order):
        return pl.BlockSpec((CHUNK, model), lambda j: (order(j), 0))

    square = (model, CHUNK)
    mlp_saved = [
        vmem((chunks,) + square, bf16),
        vmem((chunks, 1, CHUNK), f32),
        vmem((chunks,) + square, bf16),
        vmem((chunks, ff, CHUNK), bf16),
        vmem((chunks, ff, CHUNK), bf16),
    ]
    back_buffers = [vmem(square, bf16), vmem((ff, CHUNK), bf16), vmem(square, bf16)]
    return pl.pallas_call(
        partial(kernel_two, per_row, chunks),
        grid=(2 * turn,),
        in_specs=[
            tok(up(0)),
            lead(square, up_then_down),
            tok(up(0)),
            tok(down(0)),
            lead((1, CHUNK), up(1)),
            whole(first_weights),
            whole(second_weights),
        ],
        out_specs=[
            tok(up(2)),
            lead(square, down(2)),
            lead(square, down(2)),
            lead(square, down(2)),
            whole(second_grads),
            pl.BlockSpec((3 * model, model), lambda j: (0, 0)),
            pl.BlockSpec((model, BLOCK), lambda j: (0, 0)),
        ],
        out_shape=[
            shape((tokens, model), bf16),
            shape((chunks,) + square, bf16),
            shape((chunks,) + square, bf16),
            shape((chunks,) + square, bf16),
            second_grads,
            shape((3 * model, model), f32),
            shape((model, BLOCK), f32),
        ],
        scratch_shapes=[
            vmem((3 * model, model), bf16),
            vmem((model, BLOCK), f32),
            vmem((model, model), bf16),
            vmem((model, ff), bf16),
            vmem((model, ff), bf16),
            vmem((8, model, BLOCK), f32),
            vmem((ff, BLOCK), f32),
            vmem((ff, model), bf16),
            vmem((ff, model), bf16),
            vmem((model, model), bf16),
            vmem((model, 3 * model), bf16),
        ]
        + [vmem(square, f32)] * 6
        + [
            vmem(square, bf16),
            vmem((CHUNK, model), bf16),
            vmem((CHUNK + BLOCK, model), bf16),
            vmem((model, CHUNK + BLOCK), bf16),
            vmem((BLOCK, BLOCK), f32),
            vmem((2, PAIRS, BLOCK, CHUNK), bf16),
            vmem((2, PAIRS, BLOCK, CHUNK), bf16),
            vmem((2, BLOCK, CHUNK), bf16),
        ]
        + mlp_saved
        + [
            vmem((chunks,) + square, f32),
            vmem((chunks,) + square, f32),
            vmem((chunks,) + square, bf16),
            vmem((chunks, 1, CHUNK), f32),
            vmem((chunks,) + square, bf16),
            vmem((chunks, 2 * model, CHUNK), bf16),
            vmem((chunks, CHUNK, model), bf16),
            vmem((chunks, 2 * PAIRS * BLOCK, CHUNK), bf16),
            vmem((chunks,) + square, bf16),
        ]
        + mlp_saved
        + back_buffers[:2]
        + back_buffers
        + [
            vmem(square, bf16),
            vmem((3 * model, CHUNK), bf16),
            vmem((model, BLOCK), f32),
            vmem((model, BLOCK), f32),
            vmem((2 * PAIRS * BLOCK, CHUNK), bf16),
            vmem((ff, CHUNK), bf16),
            vmem((ff, CHUNK), bf16),
            *[vmem(square, bf16)] * 6,
            *[vmem((1, CHUNK), f32)] * 3,
            vmem(square, f32),
            vmem((ff, model), f32),
            vmem((ff, model), f32),
            vmem((model, model), f32),
            vmem((ff, BLOCK), f32),
            vmem((8, model, BLOCK), f32),
        ],
        compiler_params=params,
        name="middle",
        cost_estimate=cost(60),
    )(x, c1, inj, cot, seg, first_weights, second_weights)


def run_three(saved, dm, dc, du2, first_weights, sum_qkv, vec_in):
    unit, inv, normed, qk, vtok, probs, ctx = saved
    chunks, model, _ = dm.shape
    tokens = chunks * CHUNK
    last = chunks - 1
    first_grads = shape((2, OWNERS // 2) + first_weights.shape[1:], bf16)

    def now(j):
        return jnp.maximum(last - j, 0)

    def past(j):
        return jnp.minimum(chunks - j, last)

    def before(j):
        return jnp.maximum(last - 1 - j, 0)

    def lead(array, order):
        dims = array.shape[1:]
        return pl.BlockSpec((1,) + dims, lambda j: (order(j),) + (0,) * len(dims))

    tok = pl.BlockSpec((CHUNK, model), lambda j: (past(j), 0))
    return pl.pallas_call(
        partial(kernel_three, chunks),
        grid=(chunks + 1,),
        in_specs=[
            lead(unit, past),
            lead(inv, past),
            lead(normed, past),
            lead(qk, now),
            pl.BlockSpec((1, model, BLOCK), lambda j: (before(j), 1, 1)),
            lead(vtok, now),
            pl.BlockSpec((1, BLOCK, model), lambda j: (before(j), 1, 0)),
            lead(probs, now),
            lead(ctx, now),
            lead(dm, past),
            lead(dc, now),
            lead(du2, past),
            whole(first_weights),
            whole(sum_qkv),
            whole(vec_in),
        ],
        out_specs=[
            tok,
            tok,
            whole(first_grads),
        ],
        out_shape=[
            shape((tokens, model), bf16),
            shape((tokens, model), bf16),
            first_grads,
        ],
        scratch_shapes=[
            vmem((3 * model, model), bf16),
            vmem((model, BLOCK), f32),
            vmem((8, model, BLOCK), f32),
            vmem((model, 3 * model), bf16),
            vmem((2, PAIRS, BLOCK, CHUNK), bf16),
            vmem((2, PAIRS, BLOCK, CHUNK), bf16),
            vmem((2, BLOCK, CHUNK), bf16),
            vmem((3 * model, CHUNK), bf16),
            vmem((model, BLOCK), f32),
            vmem((model, BLOCK), f32),
            vmem((3 * model, model), f32),
            vmem((8, model, BLOCK), f32),
        ],
        compiler_params=params,
        name="attend_back",
        cost_estimate=cost(16),
    )(unit, inv, normed, qk, qk, vtok, vtok, probs, ctx, dm, dc, du2, first_weights, sum_qkv, vec_in)


def pack_first(qkv_t, vectors):
    rows, model = qkv_t.shape
    count = rows // 96
    columns = [vector.reshape(count, 1, 32) for vector in vectors[:3] + vectors[4:]]
    columns.insert(8, vectors[3].reshape(count, 4, 32))
    block = jnp.concatenate(columns, axis=1).transpose(0, 2, 1)
    block = jnp.pad(block, ((0, 0), (0, 0), (0, model - block.shape[2])))
    return jnp.concatenate([qkv_t.reshape(count, 96, model), block], axis=1)


def unpack_vectors(block):
    columns = [block[:, :, index].reshape(-1) for index in range(8)]
    columns.insert(3, block[:, :, 8:12].transpose(0, 2, 1).reshape(-1))
    return columns


def pack_second(out_t, up, down_t):
    rows, model = out_t.shape
    count = rows // 32
    up_part = up.reshape(2, model // 2, count, 128).transpose(2, 1, 0, 3).reshape(count, 128, 256)
    down_part = down_t.reshape(count, 32, 4, 256).transpose(0, 2, 1, 3).reshape(count, 128, 256)
    return jnp.concatenate([out_t.reshape(count, 32, model), up_part, down_part], axis=1)


def unpack_second_grads(block):
    count, _, model = block.shape
    out_t = block[:, :32].reshape(count * 32, model)
    up = block[:, 32:160].reshape(count, 128, 2, 128).transpose(2, 1, 0, 3)
    down_t = block[:, 160:].reshape(count, 4, 32, 256).transpose(0, 2, 1, 3)
    return out_t, up.reshape(model, 128 * count), down_t.reshape(32 * count, 1024)


def exchange(block, axis, size, distance):
    return lax.ppermute(block, axis, [(k, k ^ distance) for k in range(size)])


def gather(block, aside):
    me = lax.axis_index("fsdp")
    block = block[None]
    for distance in (4, 2, 1):
        if distance == 2:
            block, aside = lax.optimization_barrier((block, aside))
        other = exchange(block, "fsdp", OWNERS, distance)
        upper = (me & distance) != 0
        pair = jnp.stack(
            [jnp.where(upper, other, block), jnp.where(upper, block, other)], axis=1
        )
        block = pair.reshape((-1,) + block.shape[1:])
    return block, aside


def pair_sum(parts):
    parity = lax.axis_index("fsdp") % 2
    own = lax.dynamic_index_in_dim(parts, parity, 0, False)
    away = lax.dynamic_index_in_dim(parts, 1 - parity, 0, False)
    got = exchange(away, "fsdp", OWNERS, 1)
    return (own.astype(f32) + got.astype(f32)).astype(bf16)


def column_sum(parts):
    place = lax.axis_index("fsdp") // 2
    got = [
        exchange(
            lax.dynamic_index_in_dim(parts, place ^ distance, 0, False),
            "fsdp", OWNERS, 2 * distance,
        )
        for distance in (3, 2, 1)
    ]
    total = lax.dynamic_index_in_dim(parts, place, 0, False).astype(f32)
    for block in got:
        total = total + block.astype(f32)
    return total


def group_sum(total):
    groups = lax.all_gather(total.astype(bf16), "dp", axis=0)
    return jnp.sum(groups.astype(f32), axis=0)


def in_order(parts):
    return parts.transpose(1, 0, 2, 3).reshape((-1,) + parts.shape[2:])


def scatter_sum_any(full, axis):
    own = lax.psum_scatter(full, "fsdp", scatter_dimension=axis, tiled=True)
    return lax.psum(own, "dp")


def local(
    inputs,
    inject,
    segments,
    cotangent,
    qkv_weight,
    out_weight,
    up_weight,
    down_weight,
    *vectors,
):
    row_count, length, model = inputs.shape
    tokens = row_count * length
    chunks = tokens // CHUNK
    x = inputs.reshape(tokens, model)
    inj = inject.reshape(tokens, model)
    cot = cotangent.reshape(tokens, model)
    seg = segments.reshape(chunks, 1, CHUNK)
    per_row = length // CHUNK
    packed = out_weight.shape[1] * OWNERS == model
    if packed:
        first_own = pack_first(qkv_weight.T, vectors)[0]
        first_own, out_own, up_own, down_own = lax.optimization_barrier(
            (first_own, out_weight.T, up_weight, down_weight.T)
        )
        second_own = pack_second(out_own, up_own, down_own)[0]
        first_weights, second_own = gather(first_own, second_own)
        second_weights = lax.all_gather(second_own, "fsdp", axis=0)
    else:

        def gathered(array, axis):
            return lax.all_gather(array, "fsdp", axis=axis, tiled=True)

        first_weights = pack_first(
            gathered(qkv_weight, 1).T, tuple(gathered(vector, 0) for vector in vectors)
        )
        second_weights = pack_second(
            gathered(out_weight, 1).T, gathered(up_weight, 1), gathered(down_weight, 1).T
        )
    saved = run_one(x, inj, seg, first_weights, per_row)
    result, dm, dc, du2, second_grads, sum_qkv, vec_mid = run_two(
        x, saved[-1], inj, cot, seg, first_weights, second_weights, per_row
    )
    if packed:
        second_pair, dm = lax.optimization_barrier((pair_sum(second_grads), dm))
        second_column = column_sum(second_pair).astype(bf16)
    grad_inputs, grad_inject, first_grads = run_three(
        saved, dm, dc, du2, first_weights, sum_qkv, vec_mid
    )
    if packed:
        second_column, first_grads = lax.optimization_barrier((second_column, first_grads))
        first_column = column_sum(pair_sum(first_grads)).astype(bf16)
        sums = group_sum(jnp.concatenate([first_column, second_column], axis=0))[None]
        first_sum, second_sum = sums[:, :128], sums[:, 128:]
        out_t, up, down_t = unpack_second_grads(second_sum)
        weight_grads = (first_sum[0, :96].T, out_t.T, up, down_t.T)
        vector_grads = unpack_vectors(first_sum[:, 96:])
    else:
        first_all = in_order(first_grads).astype(f32)
        out_t, up, down_t = unpack_second_grads(in_order(second_grads).astype(f32))
        weight_grads = tuple(
            scatter_sum_any(grad, 1)
            for grad in (first_all[:, :96].reshape(3 * model, model).T, out_t.T, up, down_t.T)
        )
        vector_grads = [scatter_sum_any(grad, 0) for grad in unpack_vectors(first_all[:, 96:])]
    dims = inputs.shape
    return (
        result.reshape(dims),
        grad_inputs.reshape(dims),
        grad_inject.reshape(dims),
        *weight_grads,
        *vector_grads,
    )


def solution(mesh):
    placed = (
        P(("dp", "fsdp"), None, None),
        P(("dp", "fsdp"), None, None),
        P(("dp", "fsdp"), None),
        P(("dp", "fsdp"), None, None),
        P(None, "fsdp"),
        P(None, "fsdp"),
        P(None, "fsdp"),
        P(None, "fsdp"),
        P("fsdp"),
        P("fsdp"),
        P("fsdp"),
        P("fsdp"),
        P("fsdp"),
        P("fsdp"),
        P("fsdp"),
        P("fsdp"),
        P("fsdp"),
    )
    return jax.shard_map(
        local,
        mesh=mesh,
        in_specs=placed,
        out_specs=(
            P(("dp", "fsdp"), None, None),
            P(("dp", "fsdp"), None, None),
            P(("dp", "fsdp"), None, None),
            P(None, "fsdp"),
            P(None, "fsdp"),
            P(None, "fsdp"),
            P(None, "fsdp"),
            P("fsdp"),
            P("fsdp"),
            P("fsdp"),
            P("fsdp"),
            P("fsdp"),
            P("fsdp"),
            P("fsdp"),
            P("fsdp"),
            P("fsdp"),
        ),
        check_vma=False,
    )
```

```python
import math
from functools import partial

import jax
import jax.numpy as jnp
from jax import lax
from jax.experimental import pallas as pl
from jax.experimental.pallas import tpu as pltpu
from jax.sharding import PartitionSpec as P

HEADS = 8
HD = 32
CHUNK = 256
BLOCK = 128
PAIRS = HEADS // 2
OWNERS = 8

norm_eps = 1e-05
masked_score = -1e30
score_scale = HD ** (-0.5)
exp2_scale = score_scale * math.log2(math.e)
gelu_c0 = math.sqrt(2.0 / math.pi)
gelu_c1 = 0.044715 * gelu_c0

f32 = jnp.float32
bf16 = jnp.bfloat16

(
    Q_BIAS,
    V_BIAS,
    OUT_BIAS,
    DOWN_BIAS,
    ATTN_GAIN,
    ATTN_SHIFT,
    MLP_GAIN,
    MLP_SHIFT,
    UP_BIAS,
) = range(9)


def mm(left_op, right_op):
    return lax.dot_general(
        left_op, right_op, (((1,), (0,)), ((), ())), preferred_element_type=f32
    )


def mm_nt(left_op, right_op):
    return lax.dot_general(
        left_op, right_op, (((1,), (1,)), ((), ())), preferred_element_type=f32
    )


def identity(size):
    rows = lax.broadcasted_iota(jnp.int32, (size, size), 0)
    cols = lax.broadcasted_iota(jnp.int32, (size, size), 1)
    return jnp.where(rows == cols, 1.0, 0.0).astype(bf16)


def flipped(block):
    return mm_nt(identity(block.shape[1]), block).astype(bf16)


def half(index):
    return slice(index * BLOCK, (index + 1) * BLOCK)


def spread(column):
    return jnp.broadcast_to(column, (column.shape[0], BLOCK))


def row_sum(values):
    return jnp.sum(values, axis=0, keepdims=True)


def norm_forward(values, gain, shift):
    scale = 1.0 / values.shape[0]
    centre = values - row_sum(values) * scale
    inverse = lax.rsqrt(row_sum(centre * centre) * scale + norm_eps)
    unit = centre * inverse
    return unit, inverse, unit * gain + shift


def norm_backward(grad_normed, unit, inverse, gain):
    scale = 1.0 / unit.shape[0]
    scaled = grad_normed * gain
    gain_term = grad_normed * unit
    mean_scaled = row_sum(scaled) * scale
    mean_unit = row_sum(gain_term * gain) * scale
    return inverse * (scaled - mean_scaled - unit * mean_unit), gain_term


def below_mask():
    key_at = lax.broadcasted_iota(jnp.int32, (BLOCK, BLOCK), 0)
    query_at = lax.broadcasted_iota(jnp.int32, (BLOCK, BLOCK), 1)
    return key_at <= query_at, key_at == query_at


def set_masks(masks):
    below, _ = below_mask()
    own = jnp.where(twice(below), 1.0, 0.0)
    masks[0] = (1.0 - own).astype(bf16)
    masks[1] = own.astype(bf16)


def stack(side, pair):
    base = (side * PAIRS + pair) * BLOCK
    return slice(base, base + BLOCK)


def twice(values):
    return jnp.concatenate([values, values], axis=1)


def set_pairs(dest, source, lanes):
    for pair in range(PAIRS):
        base = 64 * (pair % 2)
        for side in range(2):
            rows = source[64 * pair + HD * side : 64 * pair + HD * (side + 1), :]
            dest[pair, base + HD * side : base + HD * (side + 1), half(side)] = rows[:, lanes]


def weave(*streams):
    order = []
    for index, (_, steps) in enumerate(streams):
        order += [((turn + 0.5) / steps, index) for turn in range(steps)]
    for _, index in sorted(order):
        next(streams[index][0], None)
    for generator, _ in streams:
        for _ in generator:
            pass


def project(u_ref, bcast, w_qkv, out):
    unit_o, inv_o, normed_o, qk_o, vtok_o, v_s, ktok_s = out
    model = w_qkv.shape[1]
    for side in range(2):
        unit, inverse, normed = norm_forward(
            u_ref[:, half(side)], bcast[ATTN_GAIN], bcast[ATTN_SHIFT]
        )
        unit_o[:, half(side)] = unit.astype(bf16)
        inv_o[:, half(side)] = inverse
        normed_o[:, half(side)] = normed.astype(bf16)
        yield
    eye = identity(model)
    normed = normed_o[...]
    rows = mm(w_qkv[model : 2 * model, :], normed)
    qk_o[model:, :] = rows.astype(bf16)
    yield
    rows = mm(w_qkv[2 * model :, :], normed)
    v_s[...] = (rows + twice(bcast[V_BIAS])).astype(bf16)
    yield
    rows = mm(w_qkv[:model, :], normed)
    qk_o[:model, :] = (rows + twice(bcast[Q_BIAS])).astype(bf16)
    yield
    ktok_s[...] = mm_nt(eye, qk_o[model:, :]).astype(bf16)
    yield
    vtok_o[...] = mm_nt(eye, v_s[...]).astype(bf16)
    yield


def hand_over(qk, v_s, ktok_s, q_pairs, key_win, value_win):
    key_win[:BLOCK, :] = key_win[CHUNK:, :]
    value_win[:, :BLOCK] = value_win[:, CHUNK:]
    key_win[BLOCK:, :] = ktok_s[...]
    value_win[:, BLOCK:] = v_s[...]
    for side in range(2):
        set_pairs(q_pairs.at[side], qk, half(side))


def attend(seg_ref, segprev, masks, q_pairs, key_win, value_win, probs_o, context_o):
    below, diagonal = below_mask()
    below2 = twice(below)
    items = [(side, pair) for side in range(2) for pair in range(PAIRS)]
    biases, scores, windows = {}, {}, {}
    for turn in range(len(items) + 2):
        if turn < len(items):
            side, pair = items[turn]
            span = slice(side * BLOCK, side * BLOCK + CHUNK)
            scores[turn] = mm(key_win[span, half(pair // 2)], q_pairs[side, pair])
            if pair == 0:
                seg_row = seg_ref[:, half(side)].astype(f32)
                seg_col = jnp.transpose(jnp.broadcast_to(seg_row, (BLOCK, BLOCK)))
                seg_key = jnp.where(below, seg_col, segprev[...])
                segprev[...] = seg_col
                allowed = ((seg_key == seg_row) & (seg_row >= 0)) | diagonal
                biases[side] = jnp.where(allowed, 0.0, masked_score)
        if turn >= 2:
            side, pair = items[turn - 2]
            lanes = half(side)
            span = slice(side * BLOCK, side * BLOCK + CHUNK)
            both = mm(value_win[64 * pair : 64 * (pair + 1), span], windows.pop(turn - 2))
            context_o[64 * pair : 64 * pair + HD, lanes] = both[:HD, :BLOCK].astype(bf16)
            context_o[64 * pair + HD : 64 * (pair + 1), lanes] = both[HD:, BLOCK:].astype(bf16)
        if 1 <= turn <= len(items):
            side, pair = items[turn - 1]
            table = scores.pop(turn - 1)
            folded = jnp.where(below2, table[BLOCK:], table[:BLOCK]) * exp2_scale + twice(
                biases[side]
            )
            top = jnp.max(folded, axis=0, keepdims=True)
            weights = jnp.exp2(folded - top)
            probs = (weights * (1.0 / row_sum(weights))).astype(bf16)
            probs_o[stack(side, pair), :] = probs
            windows[turn - 1] = jnp.concatenate([probs * masks[0], probs * masks[1]], axis=0)
        yield


def feed_forward(u_ref, m_ref, context, bcast, up_bias, w_out, w_up, w_down, out, finish):
    unit_o, inv_o, normed_o, hidden_o, slope_o = out
    mixed = mm(w_out[...], context)
    yield
    for side in range(2):
        lanes = half(side)
        after = u_ref[:, lanes] + (mixed[:, lanes] + bcast[OUT_BIAS])
        m_ref[:, lanes] = after
        unit, inverse, normed = norm_forward(after, bcast[MLP_GAIN], bcast[MLP_SHIFT])
        unit_o[:, lanes] = unit.astype(bf16)
        inv_o[:, lanes] = inverse
        normed_o[:, lanes] = normed.astype(bf16)
        yield
    normed = normed_o[...]
    parts = w_up.shape[0] // CHUNK

    def rows_of(part):
        return slice(part * CHUNK, (part + 1) * CHUNK)

    pre = mm(w_up[rows_of(0), :], normed)
    for part in range(parts):
        rows = rows_of(part)
        current = pre
        if part + 1 < parts:
            pre = mm(w_up[rows_of(part + 1), :], normed)
        for piece in range(2):
            inner = slice(piece * BLOCK, (piece + 1) * BLOCK)
            outer = slice(part * CHUNK + piece * BLOCK, part * CHUNK + (piece + 1) * BLOCK)
            z = (current[inner, :] + twice(up_bias[outer, :])).astype(bf16)
            z2 = z * z
            gate = 0.5 * jnp.tanh(z * (gelu_c0 + gelu_c1 * z2)) + 0.5
            act = z * gate
            slope = gate + (act * (1.0 - gate)) * (2.0 * gelu_c0 + 6.0 * gelu_c1 * z2)
            hidden_o[outer, :] = act
            slope_o[outer, :] = slope
            yield
    total = mm(w_down[...], hidden_o[...])
    yield
    for side in range(2):
        lanes = half(side)
        finish(side, m_ref[:, lanes] + (total[:, lanes] + bcast[DOWN_BIAS]))
    yield


def back_feed_forward(g_ref, dm_ref, saved, bcast, weights, sums, dy_s, dz_s, do_ref):
    unit, inverse, normed, hidden, slope = saved
    w_down_n, w_up_n = weights
    sum_down, sum_up, sum_up_bias, sum_vec = sums
    for side in range(2):
        lanes = half(side)
        grad = g_ref[:, lanes]
        sum_vec[DOWN_BIAS] += grad
        dy_s[:, lanes] = grad.astype(bf16)
    dy = dy_s[...]
    yield
    parts = w_down_n.shape[0] // CHUNK

    def rows_of(part):
        return slice(part * CHUNK, (part + 1) * CHUNK)

    ahead = mm(w_down_n[rows_of(0), :], dy)
    for part in range(parts):
        rows = rows_of(part)
        current = ahead
        if part + 1 < parts:
            ahead = mm(w_down_n[rows_of(part + 1), :], dy)
        dz = current.astype(bf16) * slope[rows, :]
        dz_s[rows, :] = dz
        wide = dz.astype(f32)
        sum_up_bias[rows, :] += wide[:, :BLOCK] + wide[:, BLOCK:]
        yield
    total = mm(w_up_n[...], dz_s[...])
    yield
    sum_down[...] += mm_nt(hidden[...], dy)
    yield
    units = unit[...]
    for side in range(2):
        lanes = half(side)
        grad_normed = total[:, lanes]
        back, gain_term = norm_backward(
            grad_normed, units[:, lanes].astype(f32), inverse[:, lanes], bcast[MLP_GAIN]
        )
        sum_vec[MLP_GAIN] += gain_term
        sum_vec[MLP_SHIFT] += grad_normed
        dm = g_ref[:, lanes] + back
        if dm_ref is not None:
            dm_ref[:, lanes] = dm
        sum_vec[OUT_BIAS] += dm
        do_ref[:, lanes] = dm.astype(bf16)
        yield
    sum_up[...] += mm_nt(dz_s[...], normed[...])
    yield


def back_out(do_ref, context, w_out_n, sum_out, dc_ref):
    grad = do_ref[...]
    dc_ref[...] = mm(w_out_n[...], grad).astype(bf16)
    yield
    sum_out[...] += mm_nt(grad, context[...])
    yield


def back_attention(
    dc_ref, context, qk, kt_prev, vtok, vtok_prev, probs_ref, masks, pairs, carry, dqkv
):
    q_pairs, c_pairs = pairs
    dk_carry, dv_carry = carry
    model = vtok.shape[1]
    below, _ = below_mask()
    below2 = twice(below)
    items = [(side, pair) for side in (1, 0) for pair in range(PAIRS)]
    key_win, value_win, weighted, grads, windows = {}, {}, {}, {}, {}
    for turn in range(len(items) + 2):
        if turn < len(items):
            side, pair = items[turn]
            if pair == 0:
                lanes = half(side)
                set_pairs(q_pairs.at[side], qk, lanes)
                set_pairs(c_pairs.at[side], dc_ref, lanes)
                weighted[side] = dc_ref[...][:, lanes].astype(f32) * context[...][:, lanes].astype(f32)
                if side == 1:
                    key_win[side] = qk[model:, :]
                    value_win[side] = vtok[...]
                else:
                    key_win[side] = jnp.concatenate([kt_prev[...], qk[model:, :][:, :BLOCK]], axis=1)
                    value_win[side] = jnp.concatenate([vtok_prev[...], vtok[:BLOCK, :]], axis=0)
            grads[turn] = mm(value_win[side][:, half(pair // 2)], c_pairs[side, pair])
        if turn >= 2:
            side, pair = items[turn - 2]
            lanes = half(side)
            base = 64 * (pair % 2)
            rows = slice(64 * pair, 64 * (pair + 1))
            prob_win, grad_win = windows.pop(turn - 2)
            dq = mm(key_win[side][rows, :], grad_win) * score_scale
            dk = mm_nt(q_pairs[side, pair, base : base + 64, :], grad_win) * score_scale
            dv = mm_nt(c_pairs[side, pair, base : base + 64, :], prob_win)
            dqkv[64 * pair : 64 * pair + HD, lanes] = dq[:HD, :BLOCK].astype(bf16)
            dqkv[64 * pair + HD : 64 * (pair + 1), lanes] = dq[HD:, BLOCK:].astype(bf16)
            krows = slice(model + 64 * pair, model + 64 * (pair + 1))
            vrows = slice(2 * model + 64 * pair, 2 * model + 64 * (pair + 1))
            dqkv[krows, lanes] = (dk[:, BLOCK:] + dk_carry[rows, :]).astype(bf16)
            dqkv[vrows, lanes] = (dv[:, BLOCK:] + dv_carry[rows, :]).astype(bf16)
            dk_carry[rows, :] = dk[:, :BLOCK]
            dv_carry[rows, :] = dv[:, :BLOCK]
        if 1 <= turn <= len(items):
            side, pair = items[turn - 1]
            table = grads.pop(turn - 1)
            folded = jnp.where(below2, table[BLOCK:], table[:BLOCK])
            product = weighted[side]
            delta = jnp.concatenate(
                [
                    row_sum(product[64 * pair : 64 * pair + HD]),
                    row_sum(product[64 * pair + HD : 64 * (pair + 1)]),
                ],
                axis=1,
            )
            probs = probs_ref[stack(side, pair), :]
            grad_scores = probs * (folded - delta).astype(bf16)
            prob_win = jnp.concatenate([probs * masks[0], probs * masks[1]], axis=0)
            grad_win = jnp.concatenate([grad_scores * masks[0], grad_scores * masks[1]], axis=0)
            windows[turn - 1] = (prob_win, grad_win)
        yield


def back_project(dm_ref, dqkv, unit, inverse, normed, bcast, w_qkv_n, sum_qkv, sum_vec, finish):
    grads = dqkv[...]
    model = dm_ref.shape[0]
    total = mm(w_qkv_n[...], grads)
    for side in range(2):
        sum_vec[Q_BIAS] += grads[:model, half(side)].astype(f32)
        sum_vec[V_BIAS] += grads[2 * model :, half(side)].astype(f32)
    yield
    sum_qkv[...] += mm_nt(grads, normed[...])
    yield
    units = unit[...]
    for side in range(2):
        lanes = half(side)
        grad_normed = total[:, lanes]
        back, gain_term = norm_backward(
            grad_normed, units[:, lanes].astype(f32), inverse[:, lanes], bcast[ATTN_GAIN]
        )
        sum_vec[ATTN_GAIN] += gain_term
        sum_vec[ATTN_SHIFT] += grad_normed
        finish(side, dm_ref[:, lanes].astype(f32) + back)
        yield


def unpack_first(packed, w_qkv, vec):
    owners, _, model = packed.shape
    rows = 3 * model // owners
    for owner in range(owners):
        w_qkv[rows * owner : rows * (owner + 1), :] = packed[owner, :rows, :]
        vec[32 * owner : 32 * (owner + 1), :] = packed[owner, rows:, :BLOCK].astype(f32)


def unpack_second(packed, w_out, w_up_n, w_down):
    owners = packed.shape[0]
    for owner in range(owners):
        rows = slice(32 * owner, 32 * (owner + 1))
        w_out[rows, :] = packed[owner, :32, :]
        for side in range(2):
            w_up_n[half(side), half(owner)] = packed[owner, 32:160, half(side)]
        for part in range(4):
            w_down[rows, part * CHUNK : (part + 1) * CHUNK] = packed[
                owner, 160 + 32 * part : 192 + 32 * part, :
            ]


def spread_vectors(vec, bcast, which):
    values = vec[...]
    for index in which:
        bcast[index] = spread(values[:, index : index + 1])


def token_sum(left_tokens, right_tokens, dest):
    eye = identity(left_tokens.shape[1])
    dest[...] = mm_nt(eye, left_tokens) + mm_nt(eye, right_tokens)


def kernel_one(
    rows_chunks, chunks, x, inj, seg, first_weights,
    unit_o, inv_o, normed_o, qk_o, vtok_o, probs_o, context_o,
    w_qkv, vec, bcast, u_s, v_s, ktok_s, key_win, value_win, segprev, q_pairs, masks,
):
    step = pl.program_id(0)

    @pl.when(step == 0)
    def _():
        unpack_first(first_weights, w_qkv, vec)
        spread_vectors(vec, bcast, (Q_BIAS, V_BIAS, ATTN_GAIN, ATTN_SHIFT))
        key_win[...] = jnp.zeros_like(key_win)
        value_win[...] = jnp.zeros_like(value_win)
        q_pairs[...] = jnp.zeros_like(q_pairs)
        set_masks(masks)

    @pl.when(lax.rem(step - 1, rows_chunks) == 0)
    def _():
        segprev[...] = jnp.full(segprev.shape, -2.0, f32)

    def first():
        token_sum(x[...], inj[...], u_s)
        yield
        yield from project(
            u_s, bcast, w_qkv,
            [r.at[0] for r in (unit_o, inv_o, normed_o, qk_o, vtok_o)] + [v_s, ktok_s],
        )

    def second():
        return attend(seg.at[0], segprev, masks, q_pairs, key_win, value_win, probs_o.at[0], context_o.at[0])

    def finish():
        hand_over(qk_o.at[0], v_s, ktok_s, q_pairs, key_win, value_win)

    @pl.when(step == 0)
    def _():
        weave((first(), 8))
        finish()

    @pl.when((step > 0) & (step < chunks))
    def _():
        weave((second(), 10), (first(), 8))
        finish()

    @pl.when(step == chunks)
    def _():
        weave((second(), 10))


def kernel_two(
    rows_chunks, chunks,
    x, c1, inj, cot, seg, first_weights, second_weights,
    result_o, dm_o, dc_o, du_o, grads_o, sum_qkv_o, vec_o,
    w_qkv, vec, w_out, w_up_n, w_down, bcast, up_bias, w_up, w_down_n, w_out_n, w_qkv_n,
    u1_s, u_s, m1_s, m2_s, g1_s, g2_s, v_s, ktok_s, key_win, value_win, segprev, q_pairs, c_pairs, masks,
    unit_m1, inv_m1, norm_m1, hid1, slope1,
    u2, dm2, unit2, inv2, norm2, qk2, vtok2, probs2, ctx2,
    unit_m2, inv_m2, norm_m2, hid2, slope2,
    dy1_s, dz1_s, dy2_s, dz2_s, do2_s, dc_s, dqkv_s, dk_carry, dv_carry, probs_s, slope1_s, slope2_s, unit_m1_s, unit_m2_s, unit2_s,
    norm_m1_s, norm_m2_s, norm2_s, inv_m1_s, inv_m2_s, inv2_s, dm2_s,
    sum_down, sum_up, sum_out, sum_up_bias, sum_vec,
):
    step = pl.program_id(0)
    model = w_out.shape[0]
    ff = w_up.shape[0]
    turn = chunks + 2

    @pl.when(step == 0)
    def _():
        unpack_first(first_weights, w_qkv, vec)
        unpack_second(second_weights, w_out, w_up_n, w_down)
        spread_vectors(vec, bcast, range(8))
        values = vec[...]
        for owner in range(ff // BLOCK):
            for col in range(4):
                up_bias[BLOCK * owner + 32 * col : BLOCK * owner + 32 * (col + 1), :] = spread(
                    values[32 * owner : 32 * (owner + 1), UP_BIAS + col : UP_BIAS + col + 1]
                )
        for part in range(ff // CHUNK):
            rows = slice(part * CHUNK, (part + 1) * CHUNK)
            w_up[rows, :] = flipped(w_up_n[:, rows])
            w_down_n[rows, :] = flipped(w_down[:, rows])
        w_out_n[...] = flipped(w_out[...])
        for part in range(3):
            rows = slice(part * model, (part + 1) * model)
            w_qkv_n[:, rows] = flipped(w_qkv[rows, :])
        for ref in (key_win, value_win, q_pairs, c_pairs, dk_carry, dv_carry,
                    sum_down, sum_up, sum_out, sum_up_bias, sum_vec):
            ref[...] = jnp.zeros_like(ref)
        sum_qkv_o[...] = jnp.zeros_like(sum_qkv_o)
        set_masks(masks)

    @pl.when(lax.rem(step - 1, rows_chunks) == 0)
    def _():
        segprev[...] = jnp.full(segprev.shape, -2.0, f32)

    def mlp_one():
        i = step

        def finish(side, h):
            again = mm_nt(identity(model), inj[half(side), :])
            u_s[:, half(side)] = h + again
            u2[i, :, half(side)] = h + again

        token_sum(x[...], inj[...], u1_s)
        yield
        yield from feed_forward(
            u1_s, m1_s, c1[0], bcast, up_bias, w_out, w_up, w_down,
            [r.at[i] for r in (unit_m1, inv_m1, norm_m1, hid1, slope1)], finish,
        )
        out = [r.at[i] for r in (unit2, inv2, norm2, qk2, vtok2)]
        yield from project(u_s, bcast, w_qkv, out + [v_s, ktok_s])

    def attention():
        i = step - 1
        return attend(seg.at[0], segprev, masks, q_pairs, key_win, value_win, probs2.at[i], ctx2.at[i])

    def mlp_two():
        i = step - 2

        def finish(side, h):
            low = h.astype(bf16)
            result_o[half(side), :] = mm_nt(identity(BLOCK), low).astype(bf16)

        yield from feed_forward(
            u2.at[i], m2_s, ctx2[i], bcast, up_bias, w_out, w_up, w_down,
            [r.at[i] for r in (unit_m2, inv_m2, norm_m2, hid2, slope2)], finish,
        )

    lengths = {mlp_one: 21, attention: 10, mlp_two: 13}

    def forward_turn(*which):
        weave(*[(stream(), lengths[stream]) for stream in which])
        if mlp_one in which:
            hand_over(qk2.at[step], v_s, ktok_s, q_pairs, key_win, value_win)

    @pl.when(step == 0)
    def _():
        forward_turn(mlp_one)

    @pl.when(step == 1)
    def _():
        forward_turn(attention, mlp_one)

    @pl.when((step >= 2) & (step < chunks))
    def _():
        forward_turn(mlp_two, attention, mlp_one)

    @pl.when(step == chunks)
    def _():
        forward_turn(mlp_two, attention)

    @pl.when(step == chunks + 1)
    def _():
        forward_turn(mlp_two)

    @pl.when(step == turn - 1)
    def _():
        slope2_s[...] = slope2[chunks - 1]
        unit_m2_s[...] = unit_m2[chunks - 1]
        norm_m2_s[...] = norm_m2[chunks - 1]
        inv_m2_s[...] = inv_m2[chunks - 1]

    at = step - turn
    sums = (sum_down, sum_up, sum_up_bias, sum_vec)

    def back_mlp_two():
        i = chunks - 1 - at
        g2_s[...] = mm_nt(identity(model), cot[...])
        yield
        yield from back_feed_forward(
            g2_s, dm2.at[i], [unit_m2_s, inv_m2_s, norm_m2_s, hid2.at[i], slope2_s],
            bcast, (w_down_n, w_up_n), sums, dy2_s, dz2_s, do2_s,
        )
        yield from back_out(do2_s, ctx2.at[i], w_out_n, sum_out, dc_s)

    def back_attend():
        i = chunks - at
        before = jnp.maximum(i - 1, 0)
        return back_attention(
            dc_s, ctx2.at[i], qk2.at[i], qk2.at[before, model:, BLOCK:], vtok2.at[i],
            vtok2.at[before, BLOCK:, :], probs_s, masks, (q_pairs, c_pairs),
            (dk_carry, dv_carry), dqkv_s,
        )

    def back_rest():
        i = chunks + 1 - at

        def finish(side, du):
            g1_s[:, half(side)] = du
            du_o[0, :, half(side)] = du.astype(bf16)

        yield from back_project(
            dm2_s, dqkv_s, unit2_s, inv2_s, norm2_s, bcast, w_qkv_n,
            sum_qkv_o, sum_vec, finish,
        )
        yield from back_feed_forward(
            g1_s, None, [unit_m1_s, inv_m1_s, norm_m1_s, hid1.at[i], slope1_s],
            bcast, (w_down_n, w_up_n), sums, dy1_s, dz1_s, dm_o.at[0],
        )
        yield from back_out(dm_o.at[0], c1.at[0], w_out_n, sum_out, dc_o.at[0])

    lengths_back = {back_mlp_two: 13, back_attend: 10, back_rest: 16}

    def backward_turn(*which):
        weave(*[(stream(), lengths_back[stream]) for stream in which])
        if back_mlp_two in which:
            probs_s[...] = probs2[chunks - 1 - at]
            slope2_s[...] = slope2[jnp.maximum(chunks - 2 - at, 0)]
            unit_m2_s[...] = unit_m2[jnp.maximum(chunks - 2 - at, 0)]
            norm_m2_s[...] = norm_m2[jnp.maximum(chunks - 2 - at, 0)]
            inv_m2_s[...] = inv_m2[jnp.maximum(chunks - 2 - at, 0)]
        if back_attend in which:
            slope1_s[...] = slope1[chunks - at]
            unit_m1_s[...] = unit_m1[chunks - at]
            unit2_s[...] = unit2[chunks - at]
            norm_m1_s[...] = norm_m1[chunks - at]
            norm2_s[...] = norm2[chunks - at]
            dm2_s[...] = dm2[chunks - at]
            inv_m1_s[...] = inv_m1[chunks - at]
            inv2_s[...] = inv2[chunks - at]

    @pl.when(at == 0)
    def _():
        backward_turn(back_mlp_two)

    @pl.when(at == 1)
    def _():
        backward_turn(back_attend, back_mlp_two)

    @pl.when((at >= 2) & (at < chunks))
    def _():
        backward_turn(back_rest, back_attend, back_mlp_two)

    @pl.when(at == chunks)
    def _():
        backward_turn(back_rest, back_attend)

    @pl.when(at == chunks + 1)
    def _():
        backward_turn(back_rest)
        owners = OWNERS
        for part in range(ff // CHUNK):
            rows = slice(part * CHUNK, (part + 1) * CHUNK)
            up_block = flipped(sum_up[rows, :].astype(bf16))
            for within in range(2):
                for side in range(2):
                    grads_o[within, part, 32:160, half(side)] = up_block[
                        half(side), half(within)
                    ]
            down_block = flipped(sum_down[rows, :].astype(bf16))
            for owner in range(owners):
                grads_o[owner % 2, owner // 2, 160 + 32 * part : 192 + 32 * part, :] = down_block[
                    32 * owner : 32 * (owner + 1), :
                ]
        for owner in range(owners):
            grads_o[owner % 2, owner // 2, :32, :] = sum_out[32 * owner : 32 * (owner + 1), :].astype(bf16)
        vec_o[...] = jnp.zeros_like(vec_o)
        for index in range(8):
            vec_o[:, index : index + 1] = jnp.sum(sum_vec[index], axis=1, keepdims=True)
        for owner in range(ff // BLOCK):
            for col in range(4):
                vec_o[32 * owner : 32 * (owner + 1), UP_BIAS + col : UP_BIAS + col + 1] = jnp.sum(
                    sum_up_bias[BLOCK * owner + 32 * col : BLOCK * owner + 32 * (col + 1), :],
                    axis=1, keepdims=True,
                )


def kernel_three(
    chunks,
    unit, inv, normed, qk, kt_prev, vtok, vtok_prev, probs, ctx, dm, dc, du2, first_weights, sum_qkv_i, vec_i,
    gin_o, ginj_o, grads_o,
    w_qkv, vec, bcast, w_qkv_n, q_pairs, c_pairs, masks, dqkv_s, dk_carry, dv_carry, sum_qkv, sum_vec,
):
    step = pl.program_id(0)
    model = w_qkv.shape[1]
    owners = OWNERS

    @pl.when(step == 0)
    def _():
        unpack_first(first_weights, w_qkv, vec)
        spread_vectors(vec, bcast, (ATTN_GAIN,))
        for part in range(3):
            rows = slice(part * model, (part + 1) * model)
            w_qkv_n[:, rows] = flipped(w_qkv[rows, :])
        for ref in (q_pairs, c_pairs, dk_carry, dv_carry, sum_vec):
            ref[...] = jnp.zeros_like(ref)
        sum_qkv[...] = sum_qkv_i[...]
        set_masks(masks)

    def attention():
        return back_attention(
            dc.at[0], ctx.at[0], qk.at[0], kt_prev.at[0], vtok.at[0], vtok_prev.at[0], probs.at[0],
            masks, (q_pairs, c_pairs), (dk_carry, dv_carry), dqkv_s,
        )

    def rest():
        eye = identity(BLOCK)

        def finish(side, du):
            gin_o[half(side), :] = mm_nt(eye, du.astype(bf16)).astype(bf16)
            both = du + du2[0, :, half(side)].astype(f32)
            ginj_o[half(side), :] = mm_nt(eye, both.astype(bf16)).astype(bf16)

        return back_project(
            dm.at[0], dqkv_s, unit.at[0], inv.at[0], normed.at[0], bcast, w_qkv_n,
            sum_qkv, sum_vec, finish,
        )

    @pl.when(step == 0)
    def _():
        weave((attention(), 10))

    @pl.when((step > 0) & (step < chunks))
    def _():
        weave((rest(), 4), (attention(), 10))

    @pl.when(step == chunks)
    def _():
        weave((rest(), 4))
        rows = 3 * model // owners
        vec[...] = vec_i[...]
        for index in (Q_BIAS, V_BIAS, ATTN_GAIN, ATTN_SHIFT):
            vec[:, index : index + 1] += jnp.sum(sum_vec[index], axis=1, keepdims=True)
        for owner in range(owners):
            grads_o[owner % 2, owner // 2, :rows, :] = sum_qkv[rows * owner : rows * (owner + 1), :].astype(bf16)
            grads_o[owner % 2, owner // 2, rows:, :] = twice(vec[32 * owner : 32 * (owner + 1), :].astype(bf16))


def cost(microseconds):
    return pl.CostEstimate(
        flops=int(microseconds * 1.1e9), bytes_accessed=int(microseconds * 3e6), transcendentals=0
    )


def whole(array):
    zeros = (0,) * len(array.shape)
    return pl.BlockSpec(array.shape, lambda j: zeros)


def shape(dims, kind):
    return jax.ShapeDtypeStruct(dims, kind)


def vmem(dims, kind):
    return pltpu.VMEM(dims, kind)


params = pltpu.CompilerParams(vmem_limit_bytes=62 * 1024 * 1024)


def run_one(x, inj, seg, first_weights, per_row):
    tokens, model = x.shape
    chunks = tokens // CHUNK
    last = chunks - 1

    def early(j):
        return jnp.minimum(j, last)

    def late(j):
        return jnp.maximum(j - 1, 0)

    def lead(dims, order):
        return pl.BlockSpec((1,) + dims, lambda j: (order(j),) + (0,) * len(dims))

    token_spec = pl.BlockSpec((CHUNK, model), lambda j: (early(j), 0))
    outs = [
        ((model, CHUNK), bf16, early),
        ((1, CHUNK), f32, early),
        ((model, CHUNK), bf16, early),
        ((2 * model, CHUNK), bf16, early),
        ((CHUNK, model), bf16, early),
        ((2 * PAIRS * BLOCK, CHUNK), bf16, late),
        ((model, CHUNK), bf16, late),
    ]
    return pl.pallas_call(
        partial(kernel_one, per_row, chunks),
        grid=(chunks + 1,),
        in_specs=[token_spec, token_spec, lead((1, CHUNK), late), whole(first_weights)],
        out_specs=[lead(dims, order) for dims, _, order in outs],
        out_shape=[shape((chunks,) + dims, kind) for dims, kind, _ in outs],
        scratch_shapes=[
            vmem((3 * model, model), bf16),
            vmem((model, BLOCK), f32),
            vmem((8, model, BLOCK), f32),
            vmem((model, CHUNK), f32),
            vmem((model, CHUNK), bf16),
            vmem((CHUNK, model), bf16),
            vmem((CHUNK + BLOCK, model), bf16),
            vmem((model, CHUNK + BLOCK), bf16),
            vmem((BLOCK, BLOCK), f32),
            vmem((2, PAIRS, BLOCK, CHUNK), bf16),
            vmem((2, BLOCK, CHUNK), bf16),
        ],
        compiler_params=params,
        name="attend_first",
        cost_estimate=cost(14),
    )(x, inj, seg, first_weights)


def run_two(x, c1, inj, cot, seg, first_weights, second_weights, per_row):
    tokens, model = x.shape
    chunks = tokens // CHUNK
    owners = second_weights.shape[0]
    ff = BLOCK * owners
    second_grads = shape((2, owners // 2) + second_weights.shape[1:], bf16)
    last = chunks - 1
    turn = chunks + 2

    def up(lag):
        return lambda j: jnp.clip(j - lag, 0, last)

    def down(lag):
        return lambda j: jnp.clip(last - (j - turn - lag), 0, last)

    def up_then_down(j):
        return jnp.where(j < turn, jnp.minimum(j, last), jnp.clip(last - (j - turn - 2), 0, last))

    def lead(dims, order):
        return pl.BlockSpec((1,) + dims, lambda j: (order(j),) + (0,) * len(dims))

    def tok(order):
        return pl.BlockSpec((CHUNK, model), lambda j: (order(j), 0))

    square = (model, CHUNK)
    mlp_saved = [
        vmem((chunks,) + square, bf16),
        vmem((chunks, 1, CHUNK), f32),
        vmem((chunks,) + square, bf16),
        vmem((chunks, ff, CHUNK), bf16),
        vmem((chunks, ff, CHUNK), bf16),
    ]
    back_buffers = [vmem(square, bf16), vmem((ff, CHUNK), bf16), vmem(square, bf16)]
    return pl.pallas_call(
        partial(kernel_two, per_row, chunks),
        grid=(2 * turn,),
        in_specs=[
            tok(up(0)),
            lead(square, up_then_down),
            tok(up(0)),
            tok(down(0)),
            lead((1, CHUNK), up(1)),
            whole(first_weights),
            whole(second_weights),
        ],
        out_specs=[
            tok(up(2)),
            lead(square, down(2)),
            lead(square, down(2)),
            lead(square, down(2)),
            whole(second_grads),
            pl.BlockSpec((3 * model, model), lambda j: (0, 0)),
            pl.BlockSpec((model, BLOCK), lambda j: (0, 0)),
        ],
        out_shape=[
            shape((tokens, model), bf16),
            shape((chunks,) + square, bf16),
            shape((chunks,) + square, bf16),
            shape((chunks,) + square, bf16),
            second_grads,
            shape((3 * model, model), f32),
            shape((model, BLOCK), f32),
        ],
        scratch_shapes=[
            vmem((3 * model, model), bf16),
            vmem((model, BLOCK), f32),
            vmem((model, model), bf16),
            vmem((model, ff), bf16),
            vmem((model, ff), bf16),
            vmem((8, model, BLOCK), f32),
            vmem((ff, BLOCK), f32),
            vmem((ff, model), bf16),
            vmem((ff, model), bf16),
            vmem((model, model), bf16),
            vmem((model, 3 * model), bf16),
        ]
        + [vmem(square, f32)] * 6
        + [
            vmem(square, bf16),
            vmem((CHUNK, model), bf16),
            vmem((CHUNK + BLOCK, model), bf16),
            vmem((model, CHUNK + BLOCK), bf16),
            vmem((BLOCK, BLOCK), f32),
            vmem((2, PAIRS, BLOCK, CHUNK), bf16),
            vmem((2, PAIRS, BLOCK, CHUNK), bf16),
            vmem((2, BLOCK, CHUNK), bf16),
        ]
        + mlp_saved
        + [
            vmem((chunks,) + square, f32),
            vmem((chunks,) + square, f32),
            vmem((chunks,) + square, bf16),
            vmem((chunks, 1, CHUNK), f32),
            vmem((chunks,) + square, bf16),
            vmem((chunks, 2 * model, CHUNK), bf16),
            vmem((chunks, CHUNK, model), bf16),
            vmem((chunks, 2 * PAIRS * BLOCK, CHUNK), bf16),
            vmem((chunks,) + square, bf16),
        ]
        + mlp_saved
        + back_buffers[:2]
        + back_buffers
        + [
            vmem(square, bf16),
            vmem((3 * model, CHUNK), bf16),
            vmem((model, BLOCK), f32),
            vmem((model, BLOCK), f32),
            vmem((2 * PAIRS * BLOCK, CHUNK), bf16),
            vmem((ff, CHUNK), bf16),
            vmem((ff, CHUNK), bf16),
            *[vmem(square, bf16)] * 6,
            *[vmem((1, CHUNK), f32)] * 3,
            vmem(square, f32),
            vmem((ff, model), f32),
            vmem((ff, model), f32),
            vmem((model, model), f32),
            vmem((ff, BLOCK), f32),
            vmem((8, model, BLOCK), f32),
        ],
        compiler_params=params,
        name="middle",
        cost_estimate=cost(60),
    )(x, c1, inj, cot, seg, first_weights, second_weights)


def run_three(saved, dm, dc, du2, first_weights, sum_qkv, vec_in):
    unit, inv, normed, qk, vtok, probs, ctx = saved
    chunks, model, _ = dm.shape
    tokens = chunks * CHUNK
    last = chunks - 1
    first_grads = shape((2, OWNERS // 2) + first_weights.shape[1:], bf16)

    def now(j):
        return jnp.maximum(last - j, 0)

    def past(j):
        return jnp.minimum(chunks - j, last)

    def before(j):
        return jnp.maximum(last - 1 - j, 0)

    def lead(array, order):
        dims = array.shape[1:]
        return pl.BlockSpec((1,) + dims, lambda j: (order(j),) + (0,) * len(dims))

    tok = pl.BlockSpec((CHUNK, model), lambda j: (past(j), 0))
    return pl.pallas_call(
        partial(kernel_three, chunks),
        grid=(chunks + 1,),
        in_specs=[
            lead(unit, past),
            lead(inv, past),
            lead(normed, past),
            lead(qk, now),
            pl.BlockSpec((1, model, BLOCK), lambda j: (before(j), 1, 1)),
            lead(vtok, now),
            pl.BlockSpec((1, BLOCK, model), lambda j: (before(j), 1, 0)),
            lead(probs, now),
            lead(ctx, now),
            lead(dm, past),
            lead(dc, now),
            lead(du2, past),
            whole(first_weights),
            whole(sum_qkv),
            whole(vec_in),
        ],
        out_specs=[
            tok,
            tok,
            whole(first_grads),
        ],
        out_shape=[
            shape((tokens, model), bf16),
            shape((tokens, model), bf16),
            first_grads,
        ],
        scratch_shapes=[
            vmem((3 * model, model), bf16),
            vmem((model, BLOCK), f32),
            vmem((8, model, BLOCK), f32),
            vmem((model, 3 * model), bf16),
            vmem((2, PAIRS, BLOCK, CHUNK), bf16),
            vmem((2, PAIRS, BLOCK, CHUNK), bf16),
            vmem((2, BLOCK, CHUNK), bf16),
            vmem((3 * model, CHUNK), bf16),
            vmem((model, BLOCK), f32),
            vmem((model, BLOCK), f32),
            vmem((3 * model, model), f32),
            vmem((8, model, BLOCK), f32),
        ],
        compiler_params=params,
        name="attend_back",
        cost_estimate=cost(16),
    )(unit, inv, normed, qk, qk, vtok, vtok, probs, ctx, dm, dc, du2, first_weights, sum_qkv, vec_in)


def pack_first(qkv_t, vectors):
    rows, model = qkv_t.shape
    count = rows // 96
    columns = [vector.reshape(count, 1, 32) for vector in vectors[:3] + vectors[4:]]
    columns.insert(8, vectors[3].reshape(count, 4, 32))
    block = jnp.concatenate(columns, axis=1).transpose(0, 2, 1)
    block = jnp.pad(block, ((0, 0), (0, 0), (0, model - block.shape[2])))
    return jnp.concatenate([qkv_t.reshape(count, 96, model), block], axis=1)


def unpack_vectors(block):
    columns = [block[:, :, index].reshape(-1) for index in range(8)]
    columns.insert(3, block[:, :, 8:12].transpose(0, 2, 1).reshape(-1))
    return columns


def pack_second(out_t, up, down_t):
    rows, model = out_t.shape
    count = rows // 32
    up_part = up.reshape(2, model // 2, count, 128).transpose(2, 1, 0, 3).reshape(count, 128, 256)
    down_part = down_t.reshape(count, 32, 4, 256).transpose(0, 2, 1, 3).reshape(count, 128, 256)
    return jnp.concatenate([out_t.reshape(count, 32, model), up_part, down_part], axis=1)


def unpack_second_grads(block):
    count, _, model = block.shape
    out_t = block[:, :32].reshape(count * 32, model)
    up = block[:, 32:160].reshape(count, 128, 2, 128).transpose(2, 1, 0, 3)
    down_t = block[:, 160:].reshape(count, 4, 32, 256).transpose(0, 2, 1, 3)
    return out_t, up.reshape(model, 128 * count), down_t.reshape(32 * count, 1024)


def pack_kernel(qkv_t, out_t, up, down_t, *refs):
    vectors, (first_o, second_o) = refs[:9], refs[9:]
    rows = qkv_t.shape[0]
    first_o[:rows, :] = qkv_t[...]
    pieces = [vector[...].astype(f32) for vector in vectors[:3] + vectors[4:]]
    up_bias = vectors[3][...].astype(f32)
    pieces += [up_bias[:, 32 * col : 32 * (col + 1)] for col in range(4)]
    table = jnp.concatenate(pieces + [jnp.zeros((4, 32), f32)], axis=0)
    wide = jnp.concatenate([table, jnp.zeros((16, BLOCK - 32), f32)], axis=1)
    tall = jnp.concatenate([wide, jnp.zeros((BLOCK - 16, BLOCK), f32)], axis=0)
    columns = jnp.transpose(tall)[:32, :].astype(bf16)
    first_o[rows:, :] = jnp.concatenate([columns, jnp.zeros_like(columns)], axis=1)
    second_o[:32, :] = out_t[...]
    for side in range(2):
        second_o[32:160, half(side)] = up[half(side), :]
    for part in range(4):
        second_o[160 + 32 * part : 192 + 32 * part, :] = down_t[
            :, part * CHUNK : (part + 1) * CHUNK
        ]


def pack_own(qkv_t, out_t, up, down_t, vectors):
    rows, model = qkv_t.shape
    return pl.pallas_call(
        pack_kernel,
        out_shape=[shape((rows + 32, model), bf16), shape((288, model), bf16)],
        name="pack",
        cost_estimate=cost(2),
    )(qkv_t, out_t, up, down_t, *[vector.reshape(1, -1) for vector in vectors])


def unpack_kernel(first, *refs):
    seconds, (qkv_o, out_o, up_o, down_o, *vectors) = refs[:4], refs[4:]
    total = seconds[0][...].astype(f32)
    for second in seconds[1:]:
        total = total + second[...].astype(f32)
    out_o[...] = total[:32, :]
    for side in range(2):
        up_o[half(side), :] = total[32:160, half(side)]
    for part in range(4):
        start = 160 + 32 * part
        down_o[:, part * CHUNK : (part + 1) * CHUNK] = total[start : start + 32, :]
    total = first[0].astype(f32)
    for group in range(1, first.shape[0]):
        total = total + first[group].astype(f32)
    rows = qkv_o.shape[0]
    qkv_o[...] = total[:rows, :]
    columns = total[rows:, :BLOCK]
    tall = jnp.concatenate([columns, jnp.zeros((BLOCK - 32, BLOCK), f32)], axis=0)
    table = jnp.transpose(tall)
    for index, vector in enumerate(vectors[:3] + vectors[4:]):
        vector[...] = table[index : index + 1, :32]
    for col in range(4):
        vectors[3][:, 32 * col : 32 * (col + 1)] = table[8 + col : 9 + col, :32]


def unpack_sums(first, seconds, sizes):
    _, _, model = first.shape
    dims = [(96, model), (32, model), (model, BLOCK), (32, 4 * model)]
    dims += [(1, size) for size in sizes]
    return pl.pallas_call(
        unpack_kernel,
        out_shape=[shape(dim, f32) for dim in dims],
        name="unpack",
        cost_estimate=cost(2),
    )(first, *seconds)


def exchange(block, axis, size, distance):
    return lax.ppermute(block, axis, [(k, k ^ distance) for k in range(size)])


def doubled(block, distance):
    return in_pairs(block, exchange(block, "fsdp", OWNERS, distance), distance)


def in_pairs(block, other, distance):
    upper = (lax.axis_index("fsdp") & distance) != 0
    pair = jnp.stack([jnp.where(upper, other, block), jnp.where(upper, block, other)], axis=1)
    return pair.reshape((-1,) + block.shape[1:])


def pair_sum(parts):
    parity = lax.axis_index("fsdp") % 2
    own = lax.dynamic_index_in_dim(parts, parity, 0, False)
    away = lax.dynamic_index_in_dim(parts, 1 - parity, 0, False)
    got = exchange(away, "fsdp", OWNERS, 1)
    return (own.astype(f32) + got.astype(f32)).astype(bf16)


def column_sum(parts):
    place = lax.axis_index("fsdp") // 2
    got = [
        exchange(
            lax.dynamic_index_in_dim(parts, place ^ distance, 0, False),
            "fsdp", OWNERS, 2 * distance,
        )
        for distance in (3, 2, 1)
    ]
    total = lax.dynamic_index_in_dim(parts, place, 0, False).astype(f32)
    for block in got:
        total = total + block.astype(f32)
    return total


def in_order(parts):
    return parts.transpose(1, 0, 2, 3).reshape((-1,) + parts.shape[2:])


def scatter_sum_any(full, axis):
    own = lax.psum_scatter(full, "fsdp", scatter_dimension=axis, tiled=True)
    return lax.psum(own, "dp")


def local(
    inputs,
    inject,
    segments,
    cotangent,
    qkv_weight,
    out_weight,
    up_weight,
    down_weight,
    *vectors,
):
    row_count, length, model = inputs.shape
    tokens = row_count * length
    chunks = tokens // CHUNK
    x = inputs.reshape(tokens, model)
    inj = inject.reshape(tokens, model)
    cot = cotangent.reshape(tokens, model)
    seg = segments.reshape(chunks, 1, CHUNK)
    per_row = length // CHUNK
    packed = out_weight.shape[1] * OWNERS == model and lax.axis_size("dp") == 4
    if packed:
        first_own, second_own = pack_own(
            qkv_weight.T, out_weight.T, up_weight, down_weight.T, vectors
        )
        first_weights = doubled(doubled(doubled(first_own[None], 4), 2), 1)
        second_weights = doubled(second_own[None], 4)
        first_weights, second_weights = lax.optimization_barrier((first_weights, second_weights))
        second_other = exchange(second_weights, "fsdp", OWNERS, 2)
    else:

        def gathered(array, axis):
            return lax.all_gather(array, "fsdp", axis=axis, tiled=True)

        first_weights = pack_first(
            gathered(qkv_weight, 1).T, tuple(gathered(vector, 0) for vector in vectors)
        )
        second_weights = pack_second(
            gathered(out_weight, 1).T, gathered(up_weight, 1), gathered(down_weight, 1).T
        )
    saved = run_one(x, inj, seg, first_weights, per_row)
    if packed:
        second_other, context = lax.optimization_barrier((second_other, saved[-1]))
        saved = (*saved[:-1], context)
        second_weights = doubled(in_pairs(second_weights, second_other, 2), 1)
    result, dm, dc, du2, second_grads, sum_qkv, vec_mid = run_two(
        x, saved[-1], inj, cot, seg, first_weights, second_weights, per_row
    )
    if packed:
        second_pair, dm = lax.optimization_barrier((pair_sum(second_grads), dm))
        second_column = column_sum(second_pair).astype(bf16)
    grad_inputs, grad_inject, first_grads = run_three(
        saved, dm, dc, du2, first_weights, sum_qkv, vec_mid
    )
    if packed:
        second_column, first_grads = lax.optimization_barrier((second_column, first_grads))
        seconds = [second_column]
        seconds += [exchange(second_column, "dp", 4, distance) for distance in (1, 2, 3)]
        first_column = column_sum(pair_sum(first_grads)).astype(bf16)
        firsts = lax.all_gather(first_column, "dp", axis=0)
        qkv_t, out_t, up, down_t, *rows = unpack_sums(
            firsts, seconds, [vector.shape[0] for vector in vectors]
        )
        weight_grads = (qkv_t.T, out_t.T, up, down_t.T)
        vector_grads = [row.reshape(-1) for row in rows]
    else:
        first_all = in_order(first_grads).astype(f32)
        out_t, up, down_t = unpack_second_grads(in_order(second_grads).astype(f32))
        weight_grads = tuple(
            scatter_sum_any(grad, 1)
            for grad in (first_all[:, :96].reshape(3 * model, model).T, out_t.T, up, down_t.T)
        )
        vector_grads = [scatter_sum_any(grad, 0) for grad in unpack_vectors(first_all[:, 96:])]
    dims = inputs.shape
    return (
        result.reshape(dims),
        grad_inputs.reshape(dims),
        grad_inject.reshape(dims),
        *weight_grads,
        *vector_grads,
    )


def solution(mesh):
    placed = (
        P(("dp", "fsdp"), None, None),
        P(("dp", "fsdp"), None, None),
        P(("dp", "fsdp"), None),
        P(("dp", "fsdp"), None, None),
        P(None, "fsdp"),
        P(None, "fsdp"),
        P(None, "fsdp"),
        P(None, "fsdp"),
        P("fsdp"),
        P("fsdp"),
        P("fsdp"),
        P("fsdp"),
        P("fsdp"),
        P("fsdp"),
        P("fsdp"),
        P("fsdp"),
        P("fsdp"),
    )
    return jax.shard_map(
        local,
        mesh=mesh,
        in_specs=placed,
        out_specs=(
            P(("dp", "fsdp"), None, None),
            P(("dp", "fsdp"), None, None),
            P(("dp", "fsdp"), None, None),
            P(None, "fsdp"),
            P(None, "fsdp"),
            P(None, "fsdp"),
            P(None, "fsdp"),
            P("fsdp"),
            P("fsdp"),
            P("fsdp"),
            P("fsdp"),
            P("fsdp"),
            P("fsdp"),
            P("fsdp"),
            P("fsdp"),
            P("fsdp"),
        ),
        check_vma=False,
    )
```

```python
import math
from functools import partial

import jax
import jax.numpy as jnp
from jax import lax
from jax.experimental import pallas as pl
from jax.experimental.pallas import tpu as pltpu
from jax.sharding import PartitionSpec as P

HEADS = 8
HD = 32
CHUNK = 256
BLOCK = 128
PAIRS = HEADS // 2
OWNERS = 8

norm_eps = 1e-05
masked_score = -1e30
score_scale = HD ** (-0.5)
exp2_scale = score_scale * math.log2(math.e)
gelu_c0 = math.sqrt(2.0 / math.pi)
gelu_c1 = 0.044715 * gelu_c0

f32 = jnp.float32
bf16 = jnp.bfloat16

(
    Q_BIAS,
    V_BIAS,
    OUT_BIAS,
    DOWN_BIAS,
    ATTN_GAIN,
    ATTN_SHIFT,
    MLP_GAIN,
    MLP_SHIFT,
    UP_BIAS,
) = range(9)


def mm(left_op, right_op):
    return lax.dot_general(
        left_op, right_op, (((1,), (0,)), ((), ())), preferred_element_type=f32
    )


def mm_nt(left_op, right_op):
    return lax.dot_general(
        left_op, right_op, (((1,), (1,)), ((), ())), preferred_element_type=f32
    )


def identity(size):
    rows = lax.broadcasted_iota(jnp.int32, (size, size), 0)
    cols = lax.broadcasted_iota(jnp.int32, (size, size), 1)
    return jnp.where(rows == cols, 1.0, 0.0).astype(bf16)


def flipped(block):
    return mm_nt(identity(block.shape[1]), block).astype(bf16)


def half(index):
    return slice(index * BLOCK, (index + 1) * BLOCK)


def spread(column):
    return jnp.broadcast_to(column, (column.shape[0], BLOCK))


def row_sum(values):
    return jnp.sum(values, axis=0, keepdims=True)


def norm_forward(values, gain, shift):
    scale = 1.0 / values.shape[0]
    centre = values - row_sum(values) * scale
    inverse = lax.rsqrt(row_sum(centre * centre) * scale + norm_eps)
    unit = centre * inverse
    return unit, inverse, unit * gain + shift


def norm_backward(grad_normed, unit, inverse, gain):
    scale = 1.0 / unit.shape[0]
    scaled = grad_normed * gain
    gain_term = grad_normed * unit
    mean_scaled = row_sum(scaled) * scale
    mean_unit = row_sum(gain_term * gain) * scale
    return inverse * (scaled - mean_scaled - unit * mean_unit), gain_term


def below_mask():
    key_at = lax.broadcasted_iota(jnp.int32, (BLOCK, BLOCK), 0)
    query_at = lax.broadcasted_iota(jnp.int32, (BLOCK, BLOCK), 1)
    return key_at <= query_at, key_at == query_at


def set_masks(masks, turned=None):
    below, _ = below_mask()
    own = jnp.where(twice(below), 1.0, 0.0)
    masks[0] = (1.0 - own).astype(bf16)
    masks[1] = own.astype(bf16)
    if turned is not None:
        own = jnp.transpose(own)
        turned[0] = (1.0 - own).astype(bf16)
        turned[1] = own.astype(bf16)


def stack(side, pair):
    base = (side * PAIRS + pair) * BLOCK
    return slice(base, base + BLOCK)


def twice(values):
    return jnp.concatenate([values, values], axis=1)


def set_pairs(dest, source, lanes):
    for pair in range(PAIRS):
        base = 64 * (pair % 2)
        for side in range(2):
            rows = source[64 * pair + HD * side : 64 * pair + HD * (side + 1), :]
            dest[pair, base + HD * side : base + HD * (side + 1), half(side)] = rows[:, lanes]


def weave(*streams):
    order = []
    for index, (_, steps) in enumerate(streams):
        order += [((turn + 0.5) / steps, index) for turn in range(steps)]
    for _, index in sorted(order):
        next(streams[index][0], None)
    for generator, _ in streams:
        for _ in generator:
            pass


def project(u_ref, bcast, w_qkv, out):
    unit_o, inv_o, normed_o, qk_o, vtok_o, v_s, ktok_s = out
    model = w_qkv.shape[1]
    for side in range(2):
        unit, inverse, normed = norm_forward(
            u_ref[:, half(side)], bcast[ATTN_GAIN], bcast[ATTN_SHIFT]
        )
        unit_o[:, half(side)] = unit.astype(bf16)
        inv_o[:, half(side)] = inverse
        normed_o[:, half(side)] = normed.astype(bf16)
        yield
    eye = identity(model)
    normed = normed_o[...]
    rows = mm(w_qkv[model : 2 * model, :], normed)
    qk_o[model:, :] = rows.astype(bf16)
    yield
    rows = mm(w_qkv[2 * model :, :], normed)
    v_s[...] = (rows + twice(bcast[V_BIAS])).astype(bf16)
    yield
    rows = mm(w_qkv[:model, :], normed)
    qk_o[:model, :] = (rows + twice(bcast[Q_BIAS])).astype(bf16)
    yield
    ktok_s[...] = mm_nt(eye, qk_o[model:, :]).astype(bf16)
    yield
    vtok_o[...] = mm_nt(eye, v_s[...]).astype(bf16)
    yield


def hand_over(qk, v_s, ktok_s, q_pairs, key_win, value_win):
    key_win[:BLOCK, :] = key_win[CHUNK:, :]
    value_win[:, :BLOCK] = value_win[:, CHUNK:]
    key_win[BLOCK:, :] = ktok_s[...]
    value_win[:, BLOCK:] = v_s[...]
    for side in range(2):
        set_pairs(q_pairs.at[side], qk, half(side))


def attend(seg_ref, segprev, first, masks, q_pairs, key_win, value_win, probs_o, context_o):
    below, diagonal = below_mask()
    below2 = twice(below)
    items = [(side, pair) for side in range(2) for pair in range(PAIRS)]
    biases, scores, windows = {}, {}, {}
    for turn in range(len(items) + 2):
        if turn < len(items):
            side, pair = items[turn]
            span = slice(side * BLOCK, side * BLOCK + CHUNK)
            scores[turn] = mm(key_win[span, half(pair // 2)], q_pairs[side, pair])
            if pair == 0:
                seg_row = seg_ref[:, half(side)].astype(f32)
                seg_col = jnp.transpose(jnp.broadcast_to(seg_row, (BLOCK, BLOCK)))
                earlier = segprev[...]
                if side == 0:
                    earlier = jnp.where(first, -2.0, earlier)
                seg_key = jnp.where(below, seg_col, earlier)
                segprev[...] = seg_col
                allowed = ((seg_key == seg_row) & (seg_row >= 0)) | diagonal
                biases[side] = jnp.where(allowed, 0.0, masked_score)
        if turn >= 2:
            side, pair = items[turn - 2]
            lanes = half(side)
            span = slice(side * BLOCK, side * BLOCK + CHUNK)
            both = mm(value_win[64 * pair : 64 * (pair + 1), span], windows.pop(turn - 2))
            context_o[64 * pair : 64 * pair + HD, lanes] = both[:HD, :BLOCK].astype(bf16)
            context_o[64 * pair + HD : 64 * (pair + 1), lanes] = both[HD:, BLOCK:].astype(bf16)
        if 1 <= turn <= len(items):
            side, pair = items[turn - 1]
            table = scores.pop(turn - 1)
            folded = jnp.where(below2, table[BLOCK:], table[:BLOCK]) * exp2_scale + twice(
                biases[side]
            )
            top = jnp.max(folded, axis=0, keepdims=True)
            weights = jnp.exp2(folded - top)
            probs = (weights * (1.0 / row_sum(weights))).astype(bf16)
            probs_o[stack(side, pair), :] = probs
            windows[turn - 1] = jnp.concatenate([probs * masks[0], probs * masks[1]], axis=0)
        yield


def feed_forward(u_ref, m_ref, context, bcast, up_bias, w_out, w_up, w_down, out, finish):
    unit_o, inv_o, normed_o, hidden_o, slope_o = out
    mixed = mm(w_out[...], context)
    yield
    for side in range(2):
        lanes = half(side)
        after = u_ref[:, lanes] + (mixed[:, lanes] + bcast[OUT_BIAS])
        m_ref[:, lanes] = after
        unit, inverse, normed = norm_forward(after, bcast[MLP_GAIN], bcast[MLP_SHIFT])
        unit_o[:, lanes] = unit.astype(bf16)
        inv_o[:, lanes] = inverse
        normed_o[:, lanes] = normed.astype(bf16)
        yield
    normed = normed_o[...]
    parts = w_up.shape[0] // CHUNK

    def rows_of(part):
        return slice(part * CHUNK, (part + 1) * CHUNK)

    pre = mm(w_up[rows_of(0), :], normed)
    for part in range(parts):
        rows = rows_of(part)
        current = pre
        if part + 1 < parts:
            pre = mm(w_up[rows_of(part + 1), :], normed)
        for piece in range(2):
            inner = slice(piece * BLOCK, (piece + 1) * BLOCK)
            outer = slice(part * CHUNK + piece * BLOCK, part * CHUNK + (piece + 1) * BLOCK)
            z = (current[inner, :] + twice(up_bias[outer, :])).astype(bf16)
            z2 = z * z
            gate = 0.5 * jnp.tanh(z * (gelu_c0 + gelu_c1 * z2)) + 0.5
            act = z * gate
            slope = gate + (act * (1.0 - gate)) * (2.0 * gelu_c0 + 6.0 * gelu_c1 * z2)
            hidden_o[outer, :] = act
            slope_o[outer, :] = slope
            yield
    total = mm(w_down[...], hidden_o[...])
    yield
    for side in range(2):
        lanes = half(side)
        finish(side, m_ref[:, lanes] + (total[:, lanes] + bcast[DOWN_BIAS]))
    yield


def back_feed_forward(g_ref, dm_ref, saved, bcast, weights, sums, dy_s, dz_s, do_ref):
    unit, inverse, normed, hidden, slope = saved
    w_down_n, w_up_n = weights
    sum_down, sum_up, sum_up_bias, sum_vec = sums
    for side in range(2):
        lanes = half(side)
        grad = g_ref[:, lanes]
        sum_vec[DOWN_BIAS] += grad
        dy_s[:, lanes] = grad.astype(bf16)
    dy = dy_s[...]
    yield
    parts = w_down_n.shape[0] // CHUNK

    def rows_of(part):
        return slice(part * CHUNK, (part + 1) * CHUNK)

    ahead = mm(w_down_n[rows_of(0), :], dy)
    for part in range(parts):
        rows = rows_of(part)
        current = ahead
        if part + 1 < parts:
            ahead = mm(w_down_n[rows_of(part + 1), :], dy)
        dz = current.astype(bf16) * slope[rows, :]
        dz_s[rows, :] = dz
        wide = dz.astype(f32)
        sum_up_bias[rows, :] += wide[:, :BLOCK] + wide[:, BLOCK:]
        yield
    total = mm(w_up_n[...], dz_s[...])
    yield
    sum_down[...] += mm_nt(hidden[...], dy)
    yield
    units = unit[...]
    for side in range(2):
        lanes = half(side)
        grad_normed = total[:, lanes]
        back, gain_term = norm_backward(
            grad_normed, units[:, lanes].astype(f32), inverse[:, lanes], bcast[MLP_GAIN]
        )
        sum_vec[MLP_GAIN] += gain_term
        sum_vec[MLP_SHIFT] += grad_normed
        dm = g_ref[:, lanes] + back
        if dm_ref is not None:
            dm_ref[:, lanes] = dm
        sum_vec[OUT_BIAS] += dm
        do_ref[:, lanes] = dm.astype(bf16)
        yield
    sum_up[...] += mm_nt(dz_s[...], normed[...])
    yield


def back_out(do_ref, context, w_out_n, sum_out, dc_ref):
    grad = do_ref[...]
    dc_ref[...] = mm(w_out_n[...], grad).astype(bf16)
    yield
    sum_out[...] += mm_nt(grad, context[...])
    yield


def back_attention(
    dc_ref, context, qk, kt_prev, vtok, vtok_prev, probs_ref, masks, turned, pairs, carry, dqkv
):
    q_pairs, c_pairs = pairs
    dk_carry, dv_carry = carry
    model = vtok.shape[1]
    below, _ = below_mask()
    below2 = twice(below)
    items = [(side, pair) for side in (1, 0) for pair in range(PAIRS)]
    key_win, value_win, weighted, grads, windows = {}, {}, {}, {}, {}
    for turn in range(len(items) + 2):
        if turn < len(items):
            side, pair = items[turn]
            if pair == 0:
                lanes = half(side)
                set_pairs(q_pairs.at[side], qk, lanes)
                set_pairs(c_pairs.at[side], dc_ref, lanes)
                weighted[side] = dc_ref[...][:, lanes].astype(f32) * context[...][:, lanes].astype(f32)
                if side == 1:
                    key_win[side] = qk[model:, :]
                    value_win[side] = vtok[...]
                else:
                    key_win[side] = jnp.concatenate([kt_prev[...], qk[model:, :][:, :BLOCK]], axis=1)
                    value_win[side] = jnp.concatenate([vtok_prev[...], vtok[:BLOCK, :]], axis=0)
            grads[turn] = mm(value_win[side][:, half(pair // 2)], c_pairs[side, pair])
        if turn >= 2:
            side, pair = items[turn - 2]
            lanes = half(side)
            base = 64 * (pair % 2)
            rows = slice(64 * pair, 64 * (pair + 1))
            prob_win, grad_win, grad_wide = windows.pop(turn - 2)
            dq = mm(key_win[side][rows, :], grad_win) * score_scale
            dk = mm(q_pairs[side, pair, base : base + 64, :], grad_wide) * score_scale
            dv = mm(c_pairs[side, pair, base : base + 64, :], prob_win)
            dqkv[64 * pair : 64 * pair + HD, lanes] = dq[:HD, :BLOCK].astype(bf16)
            dqkv[64 * pair + HD : 64 * (pair + 1), lanes] = dq[HD:, BLOCK:].astype(bf16)
            krows = slice(model + 64 * pair, model + 64 * (pair + 1))
            vrows = slice(2 * model + 64 * pair, 2 * model + 64 * (pair + 1))
            dqkv[krows, lanes] = (dk[:, BLOCK:] + dk_carry[rows, :]).astype(bf16)
            dqkv[vrows, lanes] = (dv[:, BLOCK:] + dv_carry[rows, :]).astype(bf16)
            dk_carry[rows, :] = dk[:, :BLOCK]
            dv_carry[rows, :] = dv[:, :BLOCK]
        if 1 <= turn <= len(items):
            side, pair = items[turn - 1]
            table = grads.pop(turn - 1)
            folded = jnp.where(below2, table[BLOCK:], table[:BLOCK])
            product = weighted[side]
            delta = jnp.concatenate(
                [
                    row_sum(product[64 * pair : 64 * pair + HD]),
                    row_sum(product[64 * pair + HD : 64 * (pair + 1)]),
                ],
                axis=1,
            )
            probs = probs_ref[stack(side, pair), :]
            grad_scores = probs * (folded - delta).astype(bf16)
            grad_win = jnp.concatenate([grad_scores * masks[0], grad_scores * masks[1]], axis=0)
            prob_turned = jnp.transpose(probs)
            grad_turned = jnp.transpose(grad_scores)
            prob_win = jnp.concatenate(
                [prob_turned * turned[0], prob_turned * turned[1]], axis=1
            )
            grad_wide = jnp.concatenate(
                [grad_turned * turned[0], grad_turned * turned[1]], axis=1
            )
            windows[turn - 1] = (prob_win, grad_win, grad_wide)
        yield


def back_project(dm_ref, dqkv, unit, inverse, normed, bcast, w_qkv_n, sum_qkv, sum_vec, finish):
    grads = dqkv[...]
    model = dm_ref.shape[0]
    total = mm(w_qkv_n[...], grads)
    for side in range(2):
        sum_vec[Q_BIAS] += grads[:model, half(side)].astype(f32)
        sum_vec[V_BIAS] += grads[2 * model :, half(side)].astype(f32)
    yield
    sum_qkv[...] += mm_nt(grads, normed[...])
    yield
    units = unit[...]
    for side in range(2):
        lanes = half(side)
        grad_normed = total[:, lanes]
        back, gain_term = norm_backward(
            grad_normed, units[:, lanes].astype(f32), inverse[:, lanes], bcast[ATTN_GAIN]
        )
        sum_vec[ATTN_GAIN] += gain_term
        sum_vec[ATTN_SHIFT] += grad_normed
        finish(side, dm_ref[:, lanes].astype(f32) + back)
        yield


def unpack_first(packed, w_qkv, vec):
    owners, _, model = packed.shape
    rows = 3 * model // owners
    for owner in range(owners):
        w_qkv[rows * owner : rows * (owner + 1), :] = packed[owner, :rows, :]
        vec[32 * owner : 32 * (owner + 1), :] = packed[owner, rows:, :BLOCK].astype(f32)


def unpack_second(packed, w_out, w_up_n, w_down):
    owners = packed.shape[0]
    for owner in range(owners):
        rows = slice(32 * owner, 32 * (owner + 1))
        w_out[rows, :] = packed[owner, :32, :]
        for side in range(2):
            w_up_n[half(side), half(owner)] = packed[owner, 32:160, half(side)]
        for part in range(4):
            w_down[rows, part * CHUNK : (part + 1) * CHUNK] = packed[
                owner, 160 + 32 * part : 192 + 32 * part, :
            ]


def spread_vectors(vec, bcast, which):
    values = vec[...]
    for index in which:
        bcast[index] = spread(values[:, index : index + 1])


def token_sum(left_tokens, right_tokens, dest):
    eye = identity(left_tokens.shape[1])
    dest[...] = mm_nt(eye, left_tokens) + mm_nt(eye, right_tokens)


def kernel_one(
    rows_chunks, chunks, x, inj, seg, first_weights,
    unit_o, inv_o, normed_o, qk_o, vtok_o, probs_o, context_o,
    w_qkv, vec, bcast, u_s, v_s, ktok_s, key_win, value_win, segprev, q_pairs, masks,
):
    step = pl.program_id(0)

    @pl.when(step == 0)
    def _():
        unpack_first(first_weights, w_qkv, vec)
        spread_vectors(vec, bcast, (Q_BIAS, V_BIAS, ATTN_GAIN, ATTN_SHIFT))
        key_win[...] = jnp.zeros_like(key_win)
        value_win[...] = jnp.zeros_like(value_win)
        q_pairs[...] = jnp.zeros_like(q_pairs)
        set_masks(masks)
        segprev[...] = jnp.zeros_like(segprev)

    def first():
        token_sum(x[...], inj[...], u_s)
        yield
        yield from project(
            u_s, bcast, w_qkv,
            [r.at[0] for r in (unit_o, inv_o, normed_o, qk_o, vtok_o)] + [v_s, ktok_s],
        )

    def second():
        return attend(
            seg.at[0], segprev, lax.rem(step - 1, rows_chunks) == 0, masks, q_pairs, key_win, value_win, probs_o.at[0], context_o.at[0],
        )

    def finish():
        hand_over(qk_o.at[0], v_s, ktok_s, q_pairs, key_win, value_win)

    @pl.when(step == 0)
    def _():
        weave((first(), 8))
        finish()

    @pl.when((step > 0) & (step < chunks))
    def _():
        weave((second(), 10), (first(), 8))
        finish()

    @pl.when(step == chunks)
    def _():
        weave((second(), 10))


def kernel_two(
    rows_chunks, chunks,
    x, c1, inj, cot, seg, first_weights, second_weights,
    result_o, dm_o, dc_o, du_o, grads_o, sum_qkv_o, vec_o,
    w_qkv, vec, w_out, w_up_n, w_down, bcast, up_bias, w_up, w_down_n, w_out_n, w_qkv_n,
    u1_s, u_s, m1_s, m2_s, g1_s, g2_s, v_s, ktok_s, key_win, value_win, segprev, q_pairs, c_pairs, masks, turned,
    unit_m1, inv_m1, norm_m1, hid1, slope1,
    u2, dm2, unit2, inv2, norm2, qk2, vtok2, probs2, ctx2,
    unit_m2, inv_m2, norm_m2, hid2, slope2,
    dy1_s, dz1_s, dy2_s, dz2_s, do2_s, dc_s, dqkv_s, dk_carry, dv_carry, probs_s, slope1_s, slope2_s, unit_m1_s, unit_m2_s, unit2_s,
    norm_m1_s, norm_m2_s, norm2_s, inv_m1_s, inv_m2_s, inv2_s, dm2_s,
    sum_down, sum_up, sum_out, sum_up_bias, sum_vec,
):
    step = pl.program_id(0)
    model = w_out.shape[0]
    ff = w_up.shape[0]
    turn = chunks // 2 + 1

    @pl.when(step == 0)
    def _():
        unpack_first(first_weights, w_qkv, vec)
        unpack_second(second_weights, w_out, w_up_n, w_down)
        spread_vectors(vec, bcast, range(8))
        values = vec[...]
        for owner in range(ff // BLOCK):
            for col in range(4):
                up_bias[BLOCK * owner + 32 * col : BLOCK * owner + 32 * (col + 1), :] = spread(
                    values[32 * owner : 32 * (owner + 1), UP_BIAS + col : UP_BIAS + col + 1]
                )
        for part in range(ff // CHUNK):
            rows = slice(part * CHUNK, (part + 1) * CHUNK)
            w_up[rows, :] = flipped(w_up_n[:, rows])
            w_down_n[rows, :] = flipped(w_down[:, rows])
        w_out_n[...] = flipped(w_out[...])
        for part in range(3):
            rows = slice(part * model, (part + 1) * model)
            w_qkv_n[:, rows] = flipped(w_qkv[rows, :])
        for ref in (key_win, value_win, q_pairs, c_pairs, dk_carry, dv_carry,
                    sum_down, sum_up, sum_out, sum_up_bias, sum_vec):
            ref[...] = jnp.zeros_like(ref)
        sum_qkv_o[...] = jnp.zeros_like(sum_qkv_o)
        set_masks(masks, turned)
        segprev[...] = jnp.zeros_like(segprev)

    def mlp_one(u):
        i = 2 * step + u
        tokens = slice(u * CHUNK, (u + 1) * CHUNK)

        def finish(side, h):
            again = mm_nt(identity(model), inj[tokens, :][half(side), :])
            u_s[:, half(side)] = h + again
            u2[i, :, half(side)] = h + again

        token_sum(x[tokens, :], inj[tokens, :], u1_s)
        yield
        yield from feed_forward(
            u1_s, m1_s, c1[u], bcast, up_bias, w_out, w_up, w_down,
            [r.at[i] for r in (unit_m1, inv_m1, norm_m1, hid1, slope1)], finish,
        )
        out = [r.at[i] for r in (unit2, inv2, norm2, qk2, vtok2)]
        yield from project(u_s, bcast, w_qkv, out + [v_s, ktok_s])

    def attention(u):
        i = 2 * step + u - 1
        return attend(
            seg.at[i], segprev, lax.rem(i, rows_chunks) == 0, masks, q_pairs, key_win, value_win,
            probs2.at[i], ctx2.at[i],
        )

    def mlp_two(u):
        i = 2 * step + u - 2

        def finish(side, h):
            low = h.astype(bf16)
            place = u * CHUNK + side * BLOCK
            result_o[place : place + BLOCK, :] = mm_nt(identity(BLOCK), low).astype(bf16)

        yield from feed_forward(
            u2.at[i], m2_s, ctx2[i], bcast, up_bias, w_out, w_up, w_down,
            [r.at[i] for r in (unit_m2, inv_m2, norm_m2, hid2, slope2)], finish,
        )

    lengths = {mlp_one: 21, attention: 10, mlp_two: 13}

    def forward_turn(u, *which):
        weave(*[(stream(u), lengths[stream]) for stream in which])
        if mlp_one in which:
            hand_over(qk2.at[2 * step + u], v_s, ktok_s, q_pairs, key_win, value_win)

    @pl.when(step == 0)
    def _():
        forward_turn(0, mlp_one)
        forward_turn(1, attention, mlp_one)

    @pl.when((step > 0) & (step < turn - 1))
    def _():
        forward_turn(0, mlp_two, attention, mlp_one)
        forward_turn(1, mlp_two, attention, mlp_one)

    @pl.when(step == turn - 1)
    def _():
        forward_turn(0, mlp_two, attention)
        forward_turn(1, mlp_two)

    @pl.when(step == turn - 1)
    def _():
        slope2_s[...] = slope2[chunks - 1]
        unit_m2_s[...] = unit_m2[chunks - 1]
        norm_m2_s[...] = norm_m2[chunks - 1]
        inv_m2_s[...] = inv_m2[chunks - 1]

    at = step - turn
    sums = (sum_down, sum_up, sum_up_bias, sum_vec)

    def back_mlp_two(u):
        i = chunks - 1 - (2 * at + u)
        g2_s[...] = mm_nt(identity(model), cot[(1 - u) * CHUNK : (2 - u) * CHUNK, :])
        yield
        yield from back_feed_forward(
            g2_s, dm2.at[i], [unit_m2_s, inv_m2_s, norm_m2_s, hid2.at[i], slope2_s],
            bcast, (w_down_n, w_up_n), sums, dy2_s, dz2_s, do2_s,
        )
        yield from back_out(do2_s, ctx2.at[i], w_out_n, sum_out, dc_s)

    def back_attend(u):
        i = chunks - (2 * at + u)
        before = jnp.maximum(i - 1, 0)
        return back_attention(
            dc_s, ctx2.at[i], qk2.at[i], qk2.at[before, model:, BLOCK:], vtok2.at[i],
            vtok2.at[before, BLOCK:, :], probs_s, masks, turned, (q_pairs, c_pairs),
            (dk_carry, dv_carry), dqkv_s,
        )

    def back_rest(u):
        i = chunks + 1 - (2 * at + u)
        place = 1 - u

        def finish(side, du):
            g1_s[:, half(side)] = du
            du_o[place, :, half(side)] = du.astype(bf16)

        yield from back_project(
            dm2_s, dqkv_s, unit2_s, inv2_s, norm2_s, bcast, w_qkv_n,
            sum_qkv_o, sum_vec, finish,
        )
        yield from back_feed_forward(
            g1_s, None, [unit_m1_s, inv_m1_s, norm_m1_s, hid1.at[i], slope1_s],
            bcast, (w_down_n, w_up_n), sums, dy1_s, dz1_s, dm_o.at[place],
        )
        yield from back_out(dm_o.at[place], c1.at[place], w_out_n, sum_out, dc_o.at[place])

    lengths_back = {back_mlp_two: 13, back_attend: 10, back_rest: 16}

    def backward_turn(u, *which):
        weave(*[(stream(u), lengths_back[stream]) for stream in which])
        i = chunks - 1 - (2 * at + u)
        if back_mlp_two in which:
            before = jnp.maximum(i - 1, 0)
            probs_s[...] = probs2[i]
            slope2_s[...] = slope2[before]
            unit_m2_s[...] = unit_m2[before]
            norm_m2_s[...] = norm_m2[before]
            inv_m2_s[...] = inv_m2[before]
        if back_attend in which:
            slope1_s[...] = slope1[i + 1]
            unit_m1_s[...] = unit_m1[i + 1]
            unit2_s[...] = unit2[i + 1]
            norm_m1_s[...] = norm_m1[i + 1]
            norm2_s[...] = norm2[i + 1]
            dm2_s[...] = dm2[i + 1]
            inv_m1_s[...] = inv_m1[i + 1]
            inv2_s[...] = inv2[i + 1]

    @pl.when(at == 0)
    def _():
        backward_turn(0, back_mlp_two)
        backward_turn(1, back_attend, back_mlp_two)

    @pl.when((at > 0) & (at < turn - 1))
    def _():
        backward_turn(0, back_rest, back_attend, back_mlp_two)
        backward_turn(1, back_rest, back_attend, back_mlp_two)

    @pl.when(at == turn - 1)
    def _():
        backward_turn(0, back_rest, back_attend)
        backward_turn(1, back_rest)

    @pl.when(at == turn - 1)
    def _():
        owners = OWNERS
        for part in range(ff // CHUNK):
            rows = slice(part * CHUNK, (part + 1) * CHUNK)
            up_block = flipped(sum_up[rows, :].astype(bf16))
            for within in range(2):
                for side in range(2):
                    grads_o[within, part, 32:160, half(side)] = up_block[
                        half(side), half(within)
                    ]
            down_block = flipped(sum_down[rows, :].astype(bf16))
            for owner in range(owners):
                grads_o[owner % 2, owner // 2, 160 + 32 * part : 192 + 32 * part, :] = down_block[
                    32 * owner : 32 * (owner + 1), :
                ]
        for owner in range(owners):
            grads_o[owner % 2, owner // 2, :32, :] = sum_out[32 * owner : 32 * (owner + 1), :].astype(bf16)
        vec_o[...] = jnp.zeros_like(vec_o)
        for index in range(8):
            vec_o[:, index : index + 1] = jnp.sum(sum_vec[index], axis=1, keepdims=True)
        for owner in range(ff // BLOCK):
            for col in range(4):
                vec_o[32 * owner : 32 * (owner + 1), UP_BIAS + col : UP_BIAS + col + 1] = jnp.sum(
                    sum_up_bias[BLOCK * owner + 32 * col : BLOCK * owner + 32 * (col + 1), :],
                    axis=1, keepdims=True,
                )


def kernel_three(
    chunks,
    unit, inv, normed, qk, kt_prev, vtok, vtok_prev, probs, ctx, dm, dc, du2, first_weights, sum_qkv_i, vec_i,
    gin_o, ginj_o, grads_o,
    w_qkv, vec, bcast, w_qkv_n, q_pairs, c_pairs, masks, turned, dqkv_s, dk_carry, dv_carry, sum_qkv, sum_vec,
):
    step = pl.program_id(0)
    model = w_qkv.shape[1]
    owners = OWNERS

    @pl.when(step == 0)
    def _():
        unpack_first(first_weights, w_qkv, vec)
        spread_vectors(vec, bcast, (ATTN_GAIN,))
        for part in range(3):
            rows = slice(part * model, (part + 1) * model)
            w_qkv_n[:, rows] = flipped(w_qkv[rows, :])
        for ref in (q_pairs, c_pairs, dk_carry, dv_carry, sum_vec):
            ref[...] = jnp.zeros_like(ref)
        sum_qkv[...] = sum_qkv_i[...]
        set_masks(masks, turned)

    def attention():
        return back_attention(
            dc.at[0], ctx.at[0], qk.at[0], kt_prev.at[0], vtok.at[0], vtok_prev.at[0], probs.at[0],
            masks, turned, (q_pairs, c_pairs), (dk_carry, dv_carry), dqkv_s,
        )

    def rest():
        eye = identity(BLOCK)

        def finish(side, du):
            gin_o[half(side), :] = mm_nt(eye, du.astype(bf16)).astype(bf16)
            both = du + du2[0, :, half(side)].astype(f32)
            ginj_o[half(side), :] = mm_nt(eye, both.astype(bf16)).astype(bf16)

        return back_project(
            dm.at[0], dqkv_s, unit.at[0], inv.at[0], normed.at[0], bcast, w_qkv_n,
            sum_qkv, sum_vec, finish,
        )

    @pl.when(step == 0)
    def _():
        weave((attention(), 10))

    @pl.when((step > 0) & (step < chunks))
    def _():
        weave((rest(), 4), (attention(), 10))

    @pl.when(step == chunks)
    def _():
        weave((rest(), 4))
        rows = 3 * model // owners
        vec[...] = vec_i[...]
        for index in (Q_BIAS, V_BIAS, ATTN_GAIN, ATTN_SHIFT):
            vec[:, index : index + 1] += jnp.sum(sum_vec[index], axis=1, keepdims=True)
        for owner in range(owners):
            grads_o[owner % 2, owner // 2, :rows, :] = sum_qkv[rows * owner : rows * (owner + 1), :].astype(bf16)
            grads_o[owner % 2, owner // 2, rows:, :] = twice(vec[32 * owner : 32 * (owner + 1), :].astype(bf16))


def cost(microseconds):
    return pl.CostEstimate(
        flops=int(microseconds * 1.1e9), bytes_accessed=int(microseconds * 3e6), transcendentals=0
    )


def whole(array):
    zeros = (0,) * len(array.shape)
    return pl.BlockSpec(array.shape, lambda j: zeros)


def shape(dims, kind):
    return jax.ShapeDtypeStruct(dims, kind)


def vmem(dims, kind):
    return pltpu.VMEM(dims, kind)


params = pltpu.CompilerParams(vmem_limit_bytes=62 * 1024 * 1024)


def run_one(x, inj, seg, first_weights, per_row):
    tokens, model = x.shape
    chunks = tokens // CHUNK
    last = chunks - 1

    def early(j):
        return jnp.minimum(j, last)

    def late(j):
        return jnp.maximum(j - 1, 0)

    def lead(dims, order):
        return pl.BlockSpec((1,) + dims, lambda j: (order(j),) + (0,) * len(dims))

    token_spec = pl.BlockSpec((CHUNK, model), lambda j: (early(j), 0))
    outs = [
        ((model, CHUNK), bf16, early),
        ((1, CHUNK), f32, early),
        ((model, CHUNK), bf16, early),
        ((2 * model, CHUNK), bf16, early),
        ((CHUNK, model), bf16, early),
        ((2 * PAIRS * BLOCK, CHUNK), bf16, late),
        ((model, CHUNK), bf16, late),
    ]
    return pl.pallas_call(
        partial(kernel_one, per_row, chunks),
        grid=(chunks + 1,),
        in_specs=[token_spec, token_spec, lead((1, CHUNK), late), whole(first_weights)],
        out_specs=[lead(dims, order) for dims, _, order in outs],
        out_shape=[shape((chunks,) + dims, kind) for dims, kind, _ in outs],
        scratch_shapes=[
            vmem((3 * model, model), bf16),
            vmem((model, BLOCK), f32),
            vmem((8, model, BLOCK), f32),
            vmem((model, CHUNK), f32),
            vmem((model, CHUNK), bf16),
            vmem((CHUNK, model), bf16),
            vmem((CHUNK + BLOCK, model), bf16),
            vmem((model, CHUNK + BLOCK), bf16),
            vmem((BLOCK, BLOCK), f32),
            vmem((2, PAIRS, BLOCK, CHUNK), bf16),
            vmem((2, BLOCK, CHUNK), bf16),
        ],
        compiler_params=params,
        name="attend_first",
        cost_estimate=cost(14),
    )(x, inj, seg, first_weights)


def run_two(x, c1, inj, cot, seg, first_weights, second_weights, per_row):
    tokens, model = x.shape
    chunks = tokens // CHUNK
    owners = second_weights.shape[0]
    ff = BLOCK * owners
    second_grads = shape((2, owners // 2) + second_weights.shape[1:], bf16)
    last = chunks // 2 - 1
    turn = chunks // 2 + 1

    def up(lag):
        return lambda j: jnp.clip(j - lag, 0, last)

    def down(lag):
        return lambda j: jnp.clip(last - (j - turn - lag), 0, last)

    def up_then_down(j):
        return jnp.where(j < turn, jnp.minimum(j, last), jnp.clip(last - (j - turn - 1), 0, last))

    def lead(dims, order):
        return pl.BlockSpec((2,) + dims, lambda j: (order(j),) + (0,) * len(dims))

    def tok(order):
        return pl.BlockSpec((2 * CHUNK, model), lambda j: (order(j), 0))

    square = (model, CHUNK)
    mlp_saved = [
        vmem((chunks,) + square, bf16),
        vmem((chunks, 1, CHUNK), f32),
        vmem((chunks,) + square, bf16),
        vmem((chunks, ff, CHUNK), bf16),
        vmem((chunks, ff, CHUNK), bf16),
    ]
    back_buffers = [vmem(square, bf16), vmem((ff, CHUNK), bf16), vmem(square, bf16)]
    return pl.pallas_call(
        partial(kernel_two, per_row, chunks),
        grid=(2 * turn,),
        in_specs=[
            tok(up(0)),
            lead(square, up_then_down),
            tok(up(0)),
            tok(down(0)),
            whole(seg),
            whole(first_weights),
            whole(second_weights),
        ],
        out_specs=[
            tok(up(1)),
            lead(square, down(1)),
            lead(square, down(1)),
            lead(square, down(1)),
            whole(second_grads),
            pl.BlockSpec((3 * model, model), lambda j: (0, 0)),
            pl.BlockSpec((model, BLOCK), lambda j: (0, 0)),
        ],
        out_shape=[
            shape((tokens, model), bf16),
            shape((chunks,) + square, bf16),
            shape((chunks,) + square, bf16),
            shape((chunks,) + square, bf16),
            second_grads,
            shape((3 * model, model), f32),
            shape((model, BLOCK), f32),
        ],
        scratch_shapes=[
            vmem((3 * model, model), bf16),
            vmem((model, BLOCK), f32),
            vmem((model, model), bf16),
            vmem((model, ff), bf16),
            vmem((model, ff), bf16),
            vmem((8, model, BLOCK), f32),
            vmem((ff, BLOCK), f32),
            vmem((ff, model), bf16),
            vmem((ff, model), bf16),
            vmem((model, model), bf16),
            vmem((model, 3 * model), bf16),
        ]
        + [vmem(square, f32)] * 6
        + [
            vmem(square, bf16),
            vmem((CHUNK, model), bf16),
            vmem((CHUNK + BLOCK, model), bf16),
            vmem((model, CHUNK + BLOCK), bf16),
            vmem((BLOCK, BLOCK), f32),
            vmem((2, PAIRS, BLOCK, CHUNK), bf16),
            vmem((2, PAIRS, BLOCK, CHUNK), bf16),
            vmem((2, BLOCK, CHUNK), bf16),
            vmem((2, CHUNK, BLOCK), bf16),
        ]
        + mlp_saved
        + [
            vmem((chunks,) + square, f32),
            vmem((chunks,) + square, f32),
            vmem((chunks,) + square, bf16),
            vmem((chunks, 1, CHUNK), f32),
            vmem((chunks,) + square, bf16),
            vmem((chunks, 2 * model, CHUNK), bf16),
            vmem((chunks, CHUNK, model), bf16),
            vmem((chunks, 2 * PAIRS * BLOCK, CHUNK), bf16),
            vmem((chunks,) + square, bf16),
        ]
        + mlp_saved
        + back_buffers[:2]
        + back_buffers
        + [
            vmem(square, bf16),
            vmem((3 * model, CHUNK), bf16),
            vmem((model, BLOCK), f32),
            vmem((model, BLOCK), f32),
            vmem((2 * PAIRS * BLOCK, CHUNK), bf16),
            vmem((ff, CHUNK), bf16),
            vmem((ff, CHUNK), bf16),
            *[vmem(square, bf16)] * 6,
            *[vmem((1, CHUNK), f32)] * 3,
            vmem(square, f32),
            vmem((ff, model), f32),
            vmem((ff, model), f32),
            vmem((model, model), f32),
            vmem((ff, BLOCK), f32),
            vmem((8, model, BLOCK), f32),
        ],
        compiler_params=params,
        name="middle",
        cost_estimate=cost(60),
    )(x, c1, inj, cot, seg, first_weights, second_weights)


def run_three(saved, dm, dc, du2, first_weights, sum_qkv, vec_in):
    unit, inv, normed, qk, vtok, probs, ctx = saved
    chunks, model, _ = dm.shape
    tokens = chunks * CHUNK
    last = chunks - 1
    first_grads = shape((2, OWNERS // 2) + first_weights.shape[1:], bf16)

    def now(j):
        return jnp.maximum(last - j, 0)

    def past(j):
        return jnp.minimum(chunks - j, last)

    def before(j):
        return jnp.maximum(last - 1 - j, 0)

    def lead(array, order):
        dims = array.shape[1:]
        return pl.BlockSpec((1,) + dims, lambda j: (order(j),) + (0,) * len(dims))

    tok = pl.BlockSpec((CHUNK, model), lambda j: (past(j), 0))
    return pl.pallas_call(
        partial(kernel_three, chunks),
        grid=(chunks + 1,),
        in_specs=[
            lead(unit, past),
            lead(inv, past),
            lead(normed, past),
            lead(qk, now),
            pl.BlockSpec((1, model, BLOCK), lambda j: (before(j), 1, 1)),
            lead(vtok, now),
            pl.BlockSpec((1, BLOCK, model), lambda j: (before(j), 1, 0)),
            lead(probs, now),
            lead(ctx, now),
            lead(dm, past),
            lead(dc, now),
            lead(du2, past),
            whole(first_weights),
            whole(sum_qkv),
            whole(vec_in),
        ],
        out_specs=[
            tok,
            tok,
            whole(first_grads),
        ],
        out_shape=[
            shape((tokens, model), bf16),
            shape((tokens, model), bf16),
            first_grads,
        ],
        scratch_shapes=[
            vmem((3 * model, model), bf16),
            vmem((model, BLOCK), f32),
            vmem((8, model, BLOCK), f32),
            vmem((model, 3 * model), bf16),
            vmem((2, PAIRS, BLOCK, CHUNK), bf16),
            vmem((2, PAIRS, BLOCK, CHUNK), bf16),
            vmem((2, BLOCK, CHUNK), bf16),
            vmem((2, CHUNK, BLOCK), bf16),
            vmem((3 * model, CHUNK), bf16),
            vmem((model, BLOCK), f32),
            vmem((model, BLOCK), f32),
            vmem((3 * model, model), f32),
            vmem((8, model, BLOCK), f32),
        ],
        compiler_params=params,
        name="attend_back",
        cost_estimate=cost(16),
    )(unit, inv, normed, qk, qk, vtok, vtok, probs, ctx, dm, dc, du2, first_weights, sum_qkv, vec_in)


def pack_first(qkv_t, vectors):
    rows, model = qkv_t.shape
    count = rows // 96
    columns = [vector.reshape(count, 1, 32) for vector in vectors[:3] + vectors[4:]]
    columns.insert(8, vectors[3].reshape(count, 4, 32))
    block = jnp.concatenate(columns, axis=1).transpose(0, 2, 1)
    block = jnp.pad(block, ((0, 0), (0, 0), (0, model - block.shape[2])))
    return jnp.concatenate([qkv_t.reshape(count, 96, model), block], axis=1)


def unpack_vectors(block):
    columns = [block[:, :, index].reshape(-1) for index in range(8)]
    columns.insert(3, block[:, :, 8:12].transpose(0, 2, 1).reshape(-1))
    return columns


def pack_second(out_t, up, down_t):
    rows, model = out_t.shape
    count = rows // 32
    up_part = up.reshape(2, model // 2, count, 128).transpose(2, 1, 0, 3).reshape(count, 128, 256)
    down_part = down_t.reshape(count, 32, 4, 256).transpose(0, 2, 1, 3).reshape(count, 128, 256)
    return jnp.concatenate([out_t.reshape(count, 32, model), up_part, down_part], axis=1)


def unpack_second_grads(block):
    count, _, model = block.shape
    out_t = block[:, :32].reshape(count * 32, model)
    up = block[:, 32:160].reshape(count, 128, 2, 128).transpose(2, 1, 0, 3)
    down_t = block[:, 160:].reshape(count, 4, 32, 256).transpose(0, 2, 1, 3)
    return out_t, up.reshape(model, 128 * count), down_t.reshape(32 * count, 1024)


def pack_kernel(qkv_t, out_t, up, down_t, *refs):
    vectors, (first_o, second_o) = refs[:9], refs[9:]
    rows = qkv_t.shape[0]
    first_o[:rows, :] = qkv_t[...]
    pieces = [vector[...].astype(f32) for vector in vectors[:3] + vectors[4:]]
    up_bias = vectors[3][...].astype(f32)
    pieces += [up_bias[:, 32 * col : 32 * (col + 1)] for col in range(4)]
    table = jnp.concatenate(pieces + [jnp.zeros((4, 32), f32)], axis=0)
    wide = jnp.concatenate([table, jnp.zeros((16, BLOCK - 32), f32)], axis=1)
    tall = jnp.concatenate([wide, jnp.zeros((BLOCK - 16, BLOCK), f32)], axis=0)
    columns = jnp.transpose(tall)[:32, :].astype(bf16)
    first_o[rows:, :] = jnp.concatenate([columns, jnp.zeros_like(columns)], axis=1)
    second_o[:32, :] = out_t[...]
    for side in range(2):
        second_o[32:160, half(side)] = up[half(side), :]
    for part in range(4):
        second_o[160 + 32 * part : 192 + 32 * part, :] = down_t[
            :, part * CHUNK : (part + 1) * CHUNK
        ]


def pack_own(qkv_t, out_t, up, down_t, vectors):
    rows, model = qkv_t.shape
    return pl.pallas_call(
        pack_kernel,
        out_shape=[shape((rows + 32, model), bf16), shape((288, model), bf16)],
        name="pack",
        cost_estimate=cost(2),
    )(qkv_t, out_t, up, down_t, *[vector.reshape(1, -1) for vector in vectors])


def unpack_kernel(first, *refs):
    seconds, (qkv_o, out_o, up_o, down_o, *vectors) = refs[:4], refs[4:]
    total = seconds[0][...].astype(f32)
    for second in seconds[1:]:
        total = total + second[...].astype(f32)
    out_o[...] = total[:32, :]
    for side in range(2):
        up_o[half(side), :] = total[32:160, half(side)]
    for part in range(4):
        start = 160 + 32 * part
        down_o[:, part * CHUNK : (part + 1) * CHUNK] = total[start : start + 32, :]
    total = first[0].astype(f32)
    for group in range(1, first.shape[0]):
        total = total + first[group].astype(f32)
    rows = qkv_o.shape[0]
    qkv_o[...] = total[:rows, :]
    columns = total[rows:, :BLOCK]
    tall = jnp.concatenate([columns, jnp.zeros((BLOCK - 32, BLOCK), f32)], axis=0)
    table = jnp.transpose(tall)
    for index, vector in enumerate(vectors[:3] + vectors[4:]):
        vector[...] = table[index : index + 1, :32]
    for col in range(4):
        vectors[3][:, 32 * col : 32 * (col + 1)] = table[8 + col : 9 + col, :32]


def unpack_sums(first, seconds, sizes):
    _, _, model = first.shape
    dims = [(96, model), (32, model), (model, BLOCK), (32, 4 * model)]
    dims += [(1, size) for size in sizes]
    return pl.pallas_call(
        unpack_kernel,
        out_shape=[shape(dim, f32) for dim in dims],
        name="unpack",
        cost_estimate=cost(2),
    )(first, *seconds)


def exchange(block, axis, size, distance):
    return lax.ppermute(block, axis, [(k, k ^ distance) for k in range(size)])


def doubled(block, distance):
    return in_pairs(block, exchange(block, "fsdp", OWNERS, distance), distance)


def in_pairs(block, other, distance):
    upper = (lax.axis_index("fsdp") & distance) != 0
    pair = jnp.stack([jnp.where(upper, other, block), jnp.where(upper, block, other)], axis=1)
    return pair.reshape((-1,) + block.shape[1:])


def pair_sum(parts):
    parity = lax.axis_index("fsdp") % 2
    own = lax.dynamic_index_in_dim(parts, parity, 0, False)
    away = lax.dynamic_index_in_dim(parts, 1 - parity, 0, False)
    got = exchange(away, "fsdp", OWNERS, 1)
    return (own.astype(f32) + got.astype(f32)).astype(bf16)


def column_sum(parts):
    place = lax.axis_index("fsdp") // 2
    got = [
        exchange(
            lax.dynamic_index_in_dim(parts, place ^ distance, 0, False),
            "fsdp", OWNERS, 2 * distance,
        )
        for distance in (3, 2, 1)
    ]
    total = lax.dynamic_index_in_dim(parts, place, 0, False).astype(f32)
    for block in got:
        total = total + block.astype(f32)
    return total


def in_order(parts):
    return parts.transpose(1, 0, 2, 3).reshape((-1,) + parts.shape[2:])


def scatter_sum_any(full, axis):
    own = lax.psum_scatter(full, "fsdp", scatter_dimension=axis, tiled=True)
    return lax.psum(own, "dp")


def local(
    inputs,
    inject,
    segments,
    cotangent,
    qkv_weight,
    out_weight,
    up_weight,
    down_weight,
    *vectors,
):
    row_count, length, model = inputs.shape
    tokens = row_count * length
    chunks = tokens // CHUNK
    x = inputs.reshape(tokens, model)
    inj = inject.reshape(tokens, model)
    cot = cotangent.reshape(tokens, model)
    seg = segments.reshape(chunks, 1, CHUNK)
    per_row = length // CHUNK
    packed = out_weight.shape[1] * OWNERS == model and lax.axis_size("dp") == 4
    if packed:
        first_own, second_own = pack_own(
            qkv_weight.T, out_weight.T, up_weight, down_weight.T, vectors
        )
        first_weights = doubled(doubled(doubled(first_own[None], 4), 2), 1)
        second_weights = doubled(second_own[None], 4)
        first_weights, second_weights = lax.optimization_barrier((first_weights, second_weights))
        second_other = exchange(second_weights, "fsdp", OWNERS, 2)
    else:

        def gathered(array, axis):
            return lax.all_gather(array, "fsdp", axis=axis, tiled=True)

        first_weights = pack_first(
            gathered(qkv_weight, 1).T, tuple(gathered(vector, 0) for vector in vectors)
        )
        second_weights = pack_second(
            gathered(out_weight, 1).T, gathered(up_weight, 1), gathered(down_weight, 1).T
        )
    saved = run_one(x, inj, seg, first_weights, per_row)
    if packed:
        second_other, context = lax.optimization_barrier((second_other, saved[-1]))
        saved = (*saved[:-1], context)
        second_weights = doubled(in_pairs(second_weights, second_other, 2), 1)
    result, dm, dc, du2, second_grads, sum_qkv, vec_mid = run_two(
        x, saved[-1], inj, cot, seg, first_weights, second_weights, per_row
    )
    if packed:
        second_pair, dm = lax.optimization_barrier((pair_sum(second_grads), dm))
        second_column = column_sum(second_pair).astype(bf16)
    grad_inputs, grad_inject, first_grads = run_three(
        saved, dm, dc, du2, first_weights, sum_qkv, vec_mid
    )
    if packed:
        second_column, first_grads = lax.optimization_barrier((second_column, first_grads))
        seconds = [second_column]
        seconds += [exchange(second_column, "dp", 4, distance) for distance in (1, 2, 3)]
        first_column = column_sum(pair_sum(first_grads)).astype(bf16)
        firsts = lax.all_gather(first_column, "dp", axis=0)
        qkv_t, out_t, up, down_t, *rows = unpack_sums(
            firsts, seconds, [vector.shape[0] for vector in vectors]
        )
        weight_grads = (qkv_t.T, out_t.T, up, down_t.T)
        vector_grads = [row.reshape(-1) for row in rows]
    else:
        first_all = in_order(first_grads).astype(f32)
        out_t, up, down_t = unpack_second_grads(in_order(second_grads).astype(f32))
        weight_grads = tuple(
            scatter_sum_any(grad, 1)
            for grad in (first_all[:, :96].reshape(3 * model, model).T, out_t.T, up, down_t.T)
        )
        vector_grads = [scatter_sum_any(grad, 0) for grad in unpack_vectors(first_all[:, 96:])]
    dims = inputs.shape
    return (
        result.reshape(dims),
        grad_inputs.reshape(dims),
        grad_inject.reshape(dims),
        *weight_grads,
        *vector_grads,
    )


def solution(mesh):
    placed = (
        P(("dp", "fsdp"), None, None),
        P(("dp", "fsdp"), None, None),
        P(("dp", "fsdp"), None),
        P(("dp", "fsdp"), None, None),
        P(None, "fsdp"),
        P(None, "fsdp"),
        P(None, "fsdp"),
        P(None, "fsdp"),
        P("fsdp"),
        P("fsdp"),
        P("fsdp"),
        P("fsdp"),
        P("fsdp"),
        P("fsdp"),
        P("fsdp"),
        P("fsdp"),
        P("fsdp"),
    )
    return jax.shard_map(
        local,
        mesh=mesh,
        in_specs=placed,
        out_specs=(
            P(("dp", "fsdp"), None, None),
            P(("dp", "fsdp"), None, None),
            P(("dp", "fsdp"), None, None),
            P(None, "fsdp"),
            P(None, "fsdp"),
            P(None, "fsdp"),
            P(None, "fsdp"),
            P("fsdp"),
            P("fsdp"),
            P("fsdp"),
            P("fsdp"),
            P("fsdp"),
            P("fsdp"),
            P("fsdp"),
            P("fsdp"),
            P("fsdp"),
        ),
        check_vma=False,
    )
```

```python
import math
from functools import partial

import jax
import jax.numpy as jnp
from jax import lax
from jax.experimental import pallas as pl
from jax.experimental.pallas import tpu as pltpu
from jax.sharding import PartitionSpec as P

HEADS = 8
HD = 32
CHUNK = 256
BLOCK = 128
PAIRS = HEADS // 2
OWNERS = 8

norm_eps = 1e-05
masked_score = -1e30
score_scale = HD ** (-0.5)
exp2_scale = score_scale * math.log2(math.e)
gelu_c0 = math.sqrt(2.0 / math.pi)
gelu_c1 = 0.044715 * gelu_c0

f32 = jnp.float32
bf16 = jnp.bfloat16

(
    Q_BIAS,
    V_BIAS,
    OUT_BIAS,
    DOWN_BIAS,
    ATTN_GAIN,
    ATTN_SHIFT,
    MLP_GAIN,
    MLP_SHIFT,
    UP_BIAS,
) = range(9)


def mm(left_op, right_op):
    return lax.dot_general(
        left_op, right_op, (((1,), (0,)), ((), ())), preferred_element_type=f32
    )


def mm_nt(left_op, right_op):
    return lax.dot_general(
        left_op, right_op, (((1,), (1,)), ((), ())), preferred_element_type=f32
    )


def identity(size):
    rows = lax.broadcasted_iota(jnp.int32, (size, size), 0)
    cols = lax.broadcasted_iota(jnp.int32, (size, size), 1)
    return jnp.where(rows == cols, 1.0, 0.0).astype(bf16)


def flipped(block):
    return mm_nt(identity(block.shape[1]), block).astype(bf16)


def half(index):
    return slice(index * BLOCK, (index + 1) * BLOCK)


def spread(column):
    return jnp.broadcast_to(column, (column.shape[0], BLOCK))


def row_sum(values):
    return jnp.sum(values, axis=0, keepdims=True)


def norm_forward(values, gain, shift):
    scale = 1.0 / values.shape[0]
    centre = values - row_sum(values) * scale
    inverse = lax.rsqrt(row_sum(centre * centre) * scale + norm_eps)
    unit = centre * inverse
    return unit, inverse, unit * gain + shift


def norm_backward(grad_normed, unit, inverse, gain):
    scale = 1.0 / unit.shape[0]
    scaled = grad_normed * gain
    gain_term = grad_normed * unit
    mean_scaled = row_sum(scaled) * scale
    mean_unit = row_sum(gain_term * gain) * scale
    return inverse * (scaled - mean_scaled - unit * mean_unit), gain_term


def below_mask():
    key_at = lax.broadcasted_iota(jnp.int32, (BLOCK, BLOCK), 0)
    query_at = lax.broadcasted_iota(jnp.int32, (BLOCK, BLOCK), 1)
    return key_at <= query_at, key_at == query_at


def set_masks(masks, turned=None):
    below, _ = below_mask()
    own = jnp.where(twice(below), 1.0, 0.0)
    masks[0] = (1.0 - own).astype(bf16)
    masks[1] = own.astype(bf16)
    if turned is not None:
        own = jnp.transpose(own)
        turned[0] = (1.0 - own).astype(bf16)
        turned[1] = own.astype(bf16)


def stack(side, pair):
    base = (side * PAIRS + pair) * BLOCK
    return slice(base, base + BLOCK)


def twice(values):
    return jnp.concatenate([values, values], axis=1)


def set_pairs(dest, source, lanes):
    for pair in range(PAIRS):
        base = 64 * (pair % 2)
        for side in range(2):
            rows = source[64 * pair + HD * side : 64 * pair + HD * (side + 1), :]
            dest[pair, base + HD * side : base + HD * (side + 1), half(side)] = rows[:, lanes]


def weave(*streams):
    order = []
    for index, (_, steps, *part) in enumerate(streams):
        start, end = part or (0.0, 1.0)
        order += [(start + (end - start) * (turn + 0.5) / steps, index) for turn in range(steps)]
    for _, index in sorted(order):
        next(streams[index][0], None)
    for generator, *_ in streams:
        for _ in generator:
            pass


def project(u_ref, bcast, w_qkv, out):
    unit_o, inv_o, normed_o, qk_o, vtok_o, v_s, ktok_s = out
    model = w_qkv.shape[1]
    for side in range(2):
        unit, inverse, normed = norm_forward(
            u_ref[:, half(side)], bcast[ATTN_GAIN], bcast[ATTN_SHIFT]
        )
        unit_o[:, half(side)] = unit.astype(bf16)
        inv_o[:, half(side)] = inverse
        normed_o[:, half(side)] = normed.astype(bf16)
        yield
    eye = identity(model)
    normed = normed_o[...]
    rows = mm(w_qkv[model : 2 * model, :], normed)
    qk_o[model:, :] = rows.astype(bf16)
    yield
    rows = mm(w_qkv[2 * model :, :], normed)
    v_s[...] = (rows + twice(bcast[V_BIAS])).astype(bf16)
    yield
    rows = mm(w_qkv[:model, :], normed)
    qk_o[:model, :] = (rows + twice(bcast[Q_BIAS])).astype(bf16)
    yield
    ktok_s[...] = mm_nt(eye, qk_o[model:, :]).astype(bf16)
    yield
    vtok_o[...] = mm_nt(eye, v_s[...]).astype(bf16)
    yield


def hand_over(qk, v_s, ktok_s, q_pairs, key_win, value_win):
    key_win[:BLOCK, :] = key_win[CHUNK:, :]
    value_win[:, :BLOCK] = value_win[:, CHUNK:]
    key_win[BLOCK:, :] = ktok_s[...]
    value_win[:, BLOCK:] = v_s[...]
    for side in range(2):
        set_pairs(q_pairs.at[side], qk, half(side))


def attend(seg, item, rows_chunks, masks, q_pairs, key_win, value_win, probs_o, context_o):
    below, diagonal = below_mask()
    below2 = twice(below)
    items = [(side, pair) for side in range(2) for pair in range(PAIRS)]
    biases, scores, windows = {}, {}, {}
    for turn in range(len(items) + 2):
        if turn < len(items):
            side, pair = items[turn]
            span = slice(side * BLOCK, side * BLOCK + CHUNK)
            scores[turn] = mm(key_win[span, half(pair // 2)], q_pairs[side, pair])
            if pair == 0:
                seg_row = seg[item][:, half(side)].astype(f32)
                if side == 0:
                    earlier = seg[jnp.maximum(item - 1, 0)][:, BLOCK:].astype(f32)
                    earlier = jnp.transpose(jnp.broadcast_to(earlier, (BLOCK, BLOCK)))
                    earlier = jnp.where(lax.rem(item, rows_chunks) == 0, -2.0, earlier)
                else:
                    earlier = seg_col
                seg_col = jnp.transpose(jnp.broadcast_to(seg_row, (BLOCK, BLOCK)))
                seg_key = jnp.where(below, seg_col, earlier)
                allowed = ((seg_key == seg_row) & (seg_row >= 0)) | diagonal
                biases[side] = jnp.where(allowed, 0.0, masked_score)
        if turn >= 2:
            side, pair = items[turn - 2]
            lanes = half(side)
            span = slice(side * BLOCK, side * BLOCK + CHUNK)
            both = mm(value_win[64 * pair : 64 * (pair + 1), span], windows.pop(turn - 2))
            context_o[64 * pair : 64 * pair + HD, lanes] = both[:HD, :BLOCK].astype(bf16)
            context_o[64 * pair + HD : 64 * (pair + 1), lanes] = both[HD:, BLOCK:].astype(bf16)
        if 1 <= turn <= len(items):
            side, pair = items[turn - 1]
            table = scores.pop(turn - 1)
            folded = jnp.where(below2, table[BLOCK:], table[:BLOCK]) * exp2_scale + twice(
                biases[side]
            )
            top = jnp.max(folded, axis=0, keepdims=True)
            weights = jnp.exp2(folded - top)
            probs = (weights * (1.0 / row_sum(weights))).astype(bf16)
            probs_o[stack(side, pair), :] = probs
            windows[turn - 1] = jnp.concatenate([probs * masks[0], probs * masks[1]], axis=0)
        yield


def feed_forward(u_ref, m_ref, context, bcast, up_bias, w_out, w_up, w_down, out, finish):
    unit_o, inv_o, normed_o, hidden_o, slope_o = out
    mixed = mm(w_out[...], context)
    yield
    for side in range(2):
        lanes = half(side)
        after = u_ref[:, lanes] + (mixed[:, lanes] + bcast[OUT_BIAS])
        m_ref[:, lanes] = after
        unit, inverse, normed = norm_forward(after, bcast[MLP_GAIN], bcast[MLP_SHIFT])
        unit_o[:, lanes] = unit.astype(bf16)
        inv_o[:, lanes] = inverse
        normed_o[:, lanes] = normed.astype(bf16)
        yield
    normed = normed_o[...]
    parts = w_up.shape[0] // CHUNK

    def rows_of(part):
        return slice(part * CHUNK, (part + 1) * CHUNK)

    pre = mm(w_up[rows_of(0), :], normed)
    for part in range(parts):
        rows = rows_of(part)
        current = pre
        if part + 1 < parts:
            pre = mm(w_up[rows_of(part + 1), :], normed)
        for piece in range(2):
            inner = slice(piece * BLOCK, (piece + 1) * BLOCK)
            outer = slice(part * CHUNK + piece * BLOCK, part * CHUNK + (piece + 1) * BLOCK)
            z = (current[inner, :] + twice(up_bias[outer, :])).astype(bf16)
            z2 = z * z
            gate = 0.5 * jnp.tanh(z * (gelu_c0 + gelu_c1 * z2)) + 0.5
            act = z * gate
            slope = gate + (act * (1.0 - gate)) * (2.0 * gelu_c0 + 6.0 * gelu_c1 * z2)
            hidden_o[outer, :] = act
            slope_o[outer, :] = slope
            yield
    total = mm(w_down[...], hidden_o[...])
    yield
    for side in range(2):
        lanes = half(side)
        finish(side, m_ref[:, lanes] + (total[:, lanes] + bcast[DOWN_BIAS]))
    yield


def back_feed_forward(g_ref, dm_ref, saved, bcast, weights, sums, dy_s, dz_s, do_ref):
    unit, inverse, normed, hidden, slope = saved
    w_down_n, w_up_n = weights
    sum_down, sum_up, sum_up_bias, sum_vec = sums
    for side in range(2):
        lanes = half(side)
        grad = g_ref[:, lanes]
        sum_vec[DOWN_BIAS] += grad
        dy_s[:, lanes] = grad.astype(bf16)
    dy = dy_s[...]
    yield
    parts = w_down_n.shape[0] // CHUNK

    def rows_of(part):
        return slice(part * CHUNK, (part + 1) * CHUNK)

    ahead = mm(w_down_n[rows_of(0), :], dy)
    for part in range(parts):
        rows = rows_of(part)
        current = ahead
        if part + 1 < parts:
            ahead = mm(w_down_n[rows_of(part + 1), :], dy)
        dz = current.astype(bf16) * slope[rows, :]
        dz_s[rows, :] = dz
        wide = dz.astype(f32)
        sum_up_bias[rows, :] += wide[:, :BLOCK] + wide[:, BLOCK:]
        yield
    total = mm(w_up_n[...], dz_s[...])
    yield
    sum_down[...] += mm_nt(hidden[...], dy)
    yield
    units = unit[...]
    for side in range(2):
        lanes = half(side)
        grad_normed = total[:, lanes]
        back, gain_term = norm_backward(
            grad_normed, units[:, lanes].astype(f32), inverse[:, lanes], bcast[MLP_GAIN]
        )
        sum_vec[MLP_GAIN] += gain_term
        sum_vec[MLP_SHIFT] += grad_normed
        dm = g_ref[:, lanes] + back
        if dm_ref is not None:
            dm_ref[:, lanes] = dm
        sum_vec[OUT_BIAS] += dm
        do_ref[:, lanes] = dm.astype(bf16)
        yield
    sum_up[...] += mm_nt(dz_s[...], normed[...])
    yield


def back_out(do_ref, context, w_out_n, sum_out, dc_ref):
    grad = do_ref[...]
    dc_ref[...] = mm(w_out_n[...], grad).astype(bf16)
    yield
    sum_out[...] += mm_nt(grad, context[...])
    yield


def back_attention(
    dc_ref, context, qk, kt_prev, vtok, vtok_prev, probs_ref, masks, turned, pairs, carry, dqkv
):
    q_pairs, c_pairs = pairs
    dk_carry, dv_carry = carry
    model = vtok.shape[1]
    below, _ = below_mask()
    below2 = twice(below)
    items = [(side, pair) for side in (1, 0) for pair in range(PAIRS)]
    key_win, value_win, weighted, grads, windows = {}, {}, {}, {}, {}
    for turn in range(len(items) + 2):
        if turn < len(items):
            side, pair = items[turn]
            if pair == 0:
                lanes = half(side)
                set_pairs(q_pairs.at[side], qk, lanes)
                set_pairs(c_pairs.at[side], dc_ref, lanes)
                weighted[side] = dc_ref[...][:, lanes].astype(f32) * context[...][:, lanes].astype(f32)
                if side == 1:
                    key_win[side] = qk[model:, :]
                    value_win[side] = vtok[...]
                else:
                    key_win[side] = jnp.concatenate([kt_prev[...], qk[model:, :][:, :BLOCK]], axis=1)
                    value_win[side] = jnp.concatenate([vtok_prev[...], vtok[:BLOCK, :]], axis=0)
            grads[turn] = mm(value_win[side][:, half(pair // 2)], c_pairs[side, pair])
        if turn >= 2:
            side, pair = items[turn - 2]
            lanes = half(side)
            base = 64 * (pair % 2)
            rows = slice(64 * pair, 64 * (pair + 1))
            prob_win, grad_win, grad_wide = windows.pop(turn - 2)
            dq = mm(key_win[side][rows, :], grad_win) * score_scale
            dk = mm(q_pairs[side, pair, base : base + 64, :], grad_wide) * score_scale
            dv = mm(c_pairs[side, pair, base : base + 64, :], prob_win)
            dqkv[64 * pair : 64 * pair + HD, lanes] = dq[:HD, :BLOCK].astype(bf16)
            dqkv[64 * pair + HD : 64 * (pair + 1), lanes] = dq[HD:, BLOCK:].astype(bf16)
            krows = slice(model + 64 * pair, model + 64 * (pair + 1))
            vrows = slice(2 * model + 64 * pair, 2 * model + 64 * (pair + 1))
            dqkv[krows, lanes] = (dk[:, BLOCK:] + dk_carry[rows, :]).astype(bf16)
            dqkv[vrows, lanes] = (dv[:, BLOCK:] + dv_carry[rows, :]).astype(bf16)
            dk_carry[rows, :] = dk[:, :BLOCK]
            dv_carry[rows, :] = dv[:, :BLOCK]
        if 1 <= turn <= len(items):
            side, pair = items[turn - 1]
            table = grads.pop(turn - 1)
            folded = jnp.where(below2, table[BLOCK:], table[:BLOCK])
            product = weighted[side]
            delta = jnp.concatenate(
                [
                    row_sum(product[64 * pair : 64 * pair + HD]),
                    row_sum(product[64 * pair + HD : 64 * (pair + 1)]),
                ],
                axis=1,
            )
            probs = probs_ref[stack(side, pair), :]
            grad_scores = probs * (folded - delta).astype(bf16)
            grad_win = jnp.concatenate([grad_scores * masks[0], grad_scores * masks[1]], axis=0)
            prob_turned = jnp.transpose(probs)
            grad_turned = jnp.transpose(grad_scores)
            prob_win = jnp.concatenate(
                [prob_turned * turned[0], prob_turned * turned[1]], axis=1
            )
            grad_wide = jnp.concatenate(
                [grad_turned * turned[0], grad_turned * turned[1]], axis=1
            )
            windows[turn - 1] = (prob_win, grad_win, grad_wide)
        yield


def back_project(dm_ref, dqkv, unit, inverse, normed, bcast, w_qkv_n, sum_qkv, sum_vec, finish):
    grads = dqkv[...]
    model = dm_ref.shape[0]
    total = mm(w_qkv_n[...], grads)
    for side in range(2):
        sum_vec[Q_BIAS] += grads[:model, half(side)].astype(f32)
        sum_vec[V_BIAS] += grads[2 * model :, half(side)].astype(f32)
    yield
    sum_qkv[...] += mm_nt(grads, normed[...])
    yield
    units = unit[...]
    for side in range(2):
        lanes = half(side)
        grad_normed = total[:, lanes]
        back, gain_term = norm_backward(
            grad_normed, units[:, lanes].astype(f32), inverse[:, lanes], bcast[ATTN_GAIN]
        )
        sum_vec[ATTN_GAIN] += gain_term
        sum_vec[ATTN_SHIFT] += grad_normed
        finish(side, dm_ref[:, lanes].astype(f32) + back)
        yield


def unpack_first(packed, w_qkv, vec):
    owners, _, model = packed.shape
    rows = 3 * model // owners
    for owner in range(owners):
        w_qkv[rows * owner : rows * (owner + 1), :] = packed[owner, :rows, :]
        vec[32 * owner : 32 * (owner + 1), :] = packed[owner, rows:, :BLOCK].astype(f32)


def unpack_second(packed, w_out, w_up_n, w_down):
    owners = packed.shape[0]
    for owner in range(owners):
        rows = slice(32 * owner, 32 * (owner + 1))
        w_out[rows, :] = packed[owner, :32, :]
        for side in range(2):
            w_up_n[half(side), half(owner)] = packed[owner, 32:160, half(side)]
        for part in range(4):
            w_down[rows, part * CHUNK : (part + 1) * CHUNK] = packed[
                owner, 160 + 32 * part : 192 + 32 * part, :
            ]


def spread_vectors(vec, bcast, which):
    values = vec[...]
    for index in which:
        bcast[index] = spread(values[:, index : index + 1])


def token_sum(left_tokens, right_tokens, dest):
    eye = identity(left_tokens.shape[1])
    dest[...] = mm_nt(eye, left_tokens) + mm_nt(eye, right_tokens)


def kernel_one(
    rows_chunks, chunks, x, inj, seg, first_weights,
    unit_o, inv_o, normed_o, qk_o, vtok_o, probs_o, context_o,
    w_qkv, vec, bcast, u_s, v_s, ktok_s, key_win, value_win, q_pairs, masks,
):
    step = pl.program_id(0)
    last = chunks // 2

    @pl.when(step == 0)
    def _():
        unpack_first(first_weights, w_qkv, vec)
        spread_vectors(vec, bcast, (Q_BIAS, V_BIAS, ATTN_GAIN, ATTN_SHIFT))
        key_win[...] = jnp.zeros_like(key_win)
        value_win[...] = jnp.zeros_like(value_win)
        q_pairs[...] = jnp.zeros_like(q_pairs)
        set_masks(masks)

    def first(u):
        tokens = slice(u * CHUNK, (u + 1) * CHUNK)
        token_sum(x[tokens, :], inj[tokens, :], u_s.at[u])
        yield
        out = [r.at[u] for r in (unit_o, inv_o, normed_o, qk_o, vtok_o, v_s, ktok_s)]
        yield from project(u_s.at[u], bcast, w_qkv, out)

    def second(u):
        window = slice(u * CHUNK, u * CHUNK + CHUNK + BLOCK)
        return attend(
            seg, 2 * step - 2 + u, rows_chunks, masks, q_pairs.at[u], key_win.at[window, :],
            value_win.at[:, window], probs_o.at[u], context_o.at[u],
        )

    def finish():
        key_win[:BLOCK, :] = key_win[2 * CHUNK :, :]
        value_win[:, :BLOCK] = value_win[:, 2 * CHUNK :]
        for u in range(2):
            place = slice(BLOCK + u * CHUNK, BLOCK + (u + 1) * CHUNK)
            key_win[place, :] = ktok_s[u]
            value_win[:, place] = v_s[u]
            for side in range(2):
                set_pairs(q_pairs.at[u, side], qk_o.at[u], half(side))

    def firsts():
        return [(first(0), 8), (first(1), 8)]

    def seconds():
        return [(second(0), 10), (second(1), 10)]

    @pl.when(step == 0)
    def _():
        weave(*firsts())
        finish()

    @pl.when((step > 0) & (step < last))
    def _():
        weave(*seconds(), *firsts())
        finish()

    @pl.when(step == last)
    def _():
        weave(*seconds())


def kernel_two(
    rows_chunks, chunks,
    x, c1, inj, cot, seg, first_weights, second_weights,
    result_o, dm_o, dc_o, du_o, grads_o, sum_qkv_o, vec_o,
    w_qkv, vec, w_out, w_up_n, w_down, bcast, up_bias, w_up, w_down_n, w_out_n, w_qkv_n,
    u1_s, u_s, m1_s, m2_s, g1_s, g2_s, v_s, ktok_s, key_win, value_win, q_pairs, c_pairs, masks, turned,
    unit_m1, inv_m1, norm_m1, hid1, slope1,
    u2, dm2, unit2, inv2, norm2, qk2, vtok2, probs2, ctx2,
    unit_m2, inv_m2, norm_m2, hid2, slope2,
    dy1_s, dz1_s, dy2_s, dz2_s, do2_s, dc_s, dqkv_s, dk_carry, dv_carry, probs_s, slope1_s, slope2_s, unit_m1_s, unit_m2_s, unit2_s,
    norm_m1_s, norm_m2_s, norm2_s, inv_m1_s, inv_m2_s, inv2_s, dm2_s,
    sum_down, sum_up, sum_out, sum_up_bias, sum_vec,
):
    step = pl.program_id(0)
    model = w_out.shape[0]
    ff = w_up.shape[0]
    turn = chunks // 2 + 1

    @pl.when(step == 0)
    def _():
        unpack_first(first_weights, w_qkv, vec)
        unpack_second(second_weights, w_out, w_up_n, w_down)
        spread_vectors(vec, bcast, range(8))
        values = vec[...]
        for owner in range(ff // BLOCK):
            for col in range(4):
                up_bias[BLOCK * owner + 32 * col : BLOCK * owner + 32 * (col + 1), :] = spread(
                    values[32 * owner : 32 * (owner + 1), UP_BIAS + col : UP_BIAS + col + 1]
                )
        for part in range(ff // CHUNK):
            rows = slice(part * CHUNK, (part + 1) * CHUNK)
            w_up[rows, :] = flipped(w_up_n[:, rows])
            w_down_n[rows, :] = flipped(w_down[:, rows])
        w_out_n[...] = flipped(w_out[...])
        for part in range(3):
            rows = slice(part * model, (part + 1) * model)
            w_qkv_n[:, rows] = flipped(w_qkv[rows, :])
        for ref in (key_win, value_win, q_pairs, c_pairs, dk_carry, dv_carry,
                    sum_down, sum_up, sum_out, sum_up_bias, sum_vec):
            ref[...] = jnp.zeros_like(ref)
        sum_qkv_o[...] = jnp.zeros_like(sum_qkv_o)
        set_masks(masks, turned)

    def mlp_one(u):
        i = 2 * step + u
        tokens = slice(u * CHUNK, (u + 1) * CHUNK)

        def finish(side, h):
            again = mm_nt(identity(model), inj[tokens, :][half(side), :])
            u_s[:, half(side)] = h + again
            u2[i, :, half(side)] = h + again

        token_sum(x[tokens, :], inj[tokens, :], u1_s)
        yield
        yield from feed_forward(
            u1_s, m1_s, c1[u], bcast, up_bias, w_out, w_up, w_down,
            [r.at[i] for r in (unit_m1, inv_m1, norm_m1, hid1, slope1)], finish,
        )
        out = [r.at[i] for r in (unit2, inv2, norm2, qk2, vtok2)]
        yield from project(u_s, bcast, w_qkv, out + [v_s, ktok_s])

    def attention(u):
        i = 2 * step + u - 1
        return attend(
            seg, i, rows_chunks, masks, q_pairs, key_win, value_win,
            probs2.at[i], ctx2.at[i],
        )

    def mlp_two(u):
        i = 2 * step + u - 2

        def finish(side, h):
            low = h.astype(bf16)
            place = u * CHUNK + side * BLOCK
            result_o[place : place + BLOCK, :] = mm_nt(identity(BLOCK), low).astype(bf16)

        yield from feed_forward(
            u2.at[i], m2_s, ctx2[i], bcast, up_bias, w_out, w_up, w_down,
            [r.at[i] for r in (unit_m2, inv_m2, norm_m2, hid2, slope2)], finish,
        )

    lengths = {mlp_one: 21, attention: 10, mlp_two: 13}

    def forward_turn(u, *which):
        weave(*[(stream(u), lengths[stream]) for stream in which])
        if mlp_one in which:
            hand_over(qk2.at[2 * step + u], v_s, ktok_s, q_pairs, key_win, value_win)

    @pl.when(step == 0)
    def _():
        forward_turn(0, mlp_one)
        forward_turn(1, attention, mlp_one)

    @pl.when((step > 0) & (step < turn - 1))
    def _():
        forward_turn(0, mlp_two, attention, mlp_one)
        forward_turn(1, mlp_two, attention, mlp_one)

    @pl.when(step == turn - 1)
    def _():
        forward_turn(0, mlp_two, attention)
        forward_turn(1, mlp_two)

    @pl.when(step == turn - 1)
    def _():
        slope2_s[...] = slope2[chunks - 1]
        unit_m2_s[...] = unit_m2[chunks - 1]
        norm_m2_s[...] = norm_m2[chunks - 1]
        inv_m2_s[...] = inv_m2[chunks - 1]

    at = step - turn
    sums = (sum_down, sum_up, sum_up_bias, sum_vec)

    def back_mlp_two(u):
        i = chunks - 1 - (2 * at + u)
        g2_s[...] = mm_nt(identity(model), cot[(1 - u) * CHUNK : (2 - u) * CHUNK, :])
        yield
        yield from back_feed_forward(
            g2_s, dm2.at[i], [unit_m2_s, inv_m2_s, norm_m2_s, hid2.at[i], slope2_s],
            bcast, (w_down_n, w_up_n), sums, dy2_s, dz2_s, do2_s,
        )
        yield from back_out(do2_s, ctx2.at[i], w_out_n, sum_out, dc_s)

    def back_attend(u):
        i = chunks - (2 * at + u)
        before = jnp.maximum(i - 1, 0)
        return back_attention(
            dc_s, ctx2.at[i], qk2.at[i], qk2.at[before, model:, BLOCK:], vtok2.at[i],
            vtok2.at[before, BLOCK:, :], probs_s, masks, turned, (q_pairs, c_pairs),
            (dk_carry, dv_carry), dqkv_s,
        )

    def back_rest(u):
        i = chunks + 1 - (2 * at + u)
        place = 1 - u

        def finish(side, du):
            g1_s[:, half(side)] = du
            du_o[place, :, half(side)] = du.astype(bf16)

        yield from back_project(
            dm2_s, dqkv_s, unit2_s, inv2_s, norm2_s, bcast, w_qkv_n,
            sum_qkv_o, sum_vec, finish,
        )
        yield from back_feed_forward(
            g1_s, None, [unit_m1_s, inv_m1_s, norm_m1_s, hid1.at[i], slope1_s],
            bcast, (w_down_n, w_up_n), sums, dy1_s, dz1_s, dm_o.at[place],
        )
        yield from back_out(dm_o.at[place], c1.at[place], w_out_n, sum_out, dc_o.at[place])

    lengths_back = {back_mlp_two: 13, back_attend: 10, back_rest: 16}

    def backward_turn(u, *which):
        weave(*[(stream(u), lengths_back[stream]) for stream in which])
        i = chunks - 1 - (2 * at + u)
        if back_mlp_two in which:
            before = jnp.maximum(i - 1, 0)
            probs_s[...] = probs2[i]
            slope2_s[...] = slope2[before]
            unit_m2_s[...] = unit_m2[before]
            norm_m2_s[...] = norm_m2[before]
            inv_m2_s[...] = inv_m2[before]
        if back_attend in which:
            slope1_s[...] = slope1[i + 1]
            unit_m1_s[...] = unit_m1[i + 1]
            unit2_s[...] = unit2[i + 1]
            norm_m1_s[...] = norm_m1[i + 1]
            norm2_s[...] = norm2[i + 1]
            dm2_s[...] = dm2[i + 1]
            inv_m1_s[...] = inv_m1[i + 1]
            inv2_s[...] = inv2[i + 1]

    @pl.when(at == 0)
    def _():
        backward_turn(0, back_mlp_two)
        backward_turn(1, back_attend, back_mlp_two)

    @pl.when((at > 0) & (at < turn - 1))
    def _():
        backward_turn(0, back_rest, back_attend, back_mlp_two)
        backward_turn(1, back_rest, back_attend, back_mlp_two)

    @pl.when(at == turn - 1)
    def _():
        backward_turn(0, back_rest, back_attend)
        backward_turn(1, back_rest)

    @pl.when(at == turn - 1)
    def _():
        owners = OWNERS
        for part in range(ff // CHUNK):
            rows = slice(part * CHUNK, (part + 1) * CHUNK)
            up_block = flipped(sum_up[rows, :].astype(bf16))
            for within in range(2):
                for side in range(2):
                    grads_o[within, part, 32:160, half(side)] = up_block[
                        half(side), half(within)
                    ]
            down_block = flipped(sum_down[rows, :].astype(bf16))
            for owner in range(owners):
                grads_o[owner % 2, owner // 2, 160 + 32 * part : 192 + 32 * part, :] = down_block[
                    32 * owner : 32 * (owner + 1), :
                ]
        for owner in range(owners):
            grads_o[owner % 2, owner // 2, :32, :] = sum_out[32 * owner : 32 * (owner + 1), :].astype(bf16)
        vec_o[...] = jnp.zeros_like(vec_o)
        for index in range(8):
            vec_o[:, index : index + 1] = jnp.sum(sum_vec[index], axis=1, keepdims=True)
        for owner in range(ff // BLOCK):
            for col in range(4):
                vec_o[32 * owner : 32 * (owner + 1), UP_BIAS + col : UP_BIAS + col + 1] = jnp.sum(
                    sum_up_bias[BLOCK * owner + 32 * col : BLOCK * owner + 32 * (col + 1), :],
                    axis=1, keepdims=True,
                )


def kernel_three(
    chunks,
    unit, inv, normed, qk, kt_prev, vtok, vtok_prev, probs, ctx, dm, dc, du2, first_weights, sum_qkv_i, vec_i,
    gin_o, ginj_o, grads_o,
    w_qkv, vec, bcast, w_qkv_n, q_pairs, c_pairs, masks, turned, dqkv_s, dk_carry, dv_carry, sum_qkv, sum_vec,
):
    step = pl.program_id(0)
    model = w_qkv.shape[1]
    owners = OWNERS

    @pl.when(step == 0)
    def _():
        unpack_first(first_weights, w_qkv, vec)
        spread_vectors(vec, bcast, (ATTN_GAIN,))
        for part in range(3):
            rows = slice(part * model, (part + 1) * model)
            w_qkv_n[:, rows] = flipped(w_qkv[rows, :])
        for ref in (q_pairs, c_pairs, dk_carry, dv_carry, sum_vec):
            ref[...] = jnp.zeros_like(ref)
        sum_qkv[...] = sum_qkv_i[...]
        set_masks(masks, turned)

    def attention():
        return back_attention(
            dc.at[0], ctx.at[0], qk.at[0], kt_prev.at[0], vtok.at[0], vtok_prev.at[0], probs.at[0],
            masks, turned, (q_pairs, c_pairs), (dk_carry, dv_carry), dqkv_s,
        )

    def rest():
        eye = identity(BLOCK)

        def finish(side, du):
            gin_o[half(side), :] = mm_nt(eye, du.astype(bf16)).astype(bf16)
            both = du + du2[0, :, half(side)].astype(f32)
            ginj_o[half(side), :] = mm_nt(eye, both.astype(bf16)).astype(bf16)

        return back_project(
            dm.at[0], dqkv_s, unit.at[0], inv.at[0], normed.at[0], bcast, w_qkv_n,
            sum_qkv, sum_vec, finish,
        )

    @pl.when(step == 0)
    def _():
        weave((attention(), 10))

    @pl.when((step > 0) & (step < chunks))
    def _():
        weave((rest(), 4), (attention(), 10))

    @pl.when(step == chunks)
    def _():
        weave((rest(), 4))
        rows = 3 * model // owners
        vec[...] = vec_i[...]
        for index in (Q_BIAS, V_BIAS, ATTN_GAIN, ATTN_SHIFT):
            vec[:, index : index + 1] += jnp.sum(sum_vec[index], axis=1, keepdims=True)
        for owner in range(owners):
            grads_o[owner % 2, owner // 2, :rows, :] = sum_qkv[rows * owner : rows * (owner + 1), :].astype(bf16)
            grads_o[owner % 2, owner // 2, rows:, :] = twice(vec[32 * owner : 32 * (owner + 1), :].astype(bf16))


def cost(microseconds):
    return pl.CostEstimate(
        flops=int(microseconds * 1.1e9), bytes_accessed=int(microseconds * 3e6), transcendentals=0
    )


def whole(array):
    zeros = (0,) * len(array.shape)
    return pl.BlockSpec(array.shape, lambda j: zeros)


def shape(dims, kind):
    return jax.ShapeDtypeStruct(dims, kind)


def vmem(dims, kind):
    return pltpu.VMEM(dims, kind)


params = pltpu.CompilerParams(vmem_limit_bytes=62 * 1024 * 1024)


def run_one(x, inj, seg, first_weights, per_row):
    tokens, model = x.shape
    chunks = tokens // CHUNK
    last = chunks // 2 - 1

    def early(j):
        return jnp.minimum(j, last)

    def late(j):
        return jnp.maximum(j - 1, 0)

    def lead(dims, order):
        return pl.BlockSpec((2,) + dims, lambda j: (order(j),) + (0,) * len(dims))

    token_spec = pl.BlockSpec((2 * CHUNK, model), lambda j: (early(j), 0))
    outs = [
        ((model, CHUNK), bf16, early),
        ((1, CHUNK), f32, early),
        ((model, CHUNK), bf16, early),
        ((2 * model, CHUNK), bf16, early),
        ((CHUNK, model), bf16, early),
        ((2 * PAIRS * BLOCK, CHUNK), bf16, late),
        ((model, CHUNK), bf16, late),
    ]
    return pl.pallas_call(
        partial(kernel_one, per_row, chunks),
        grid=(chunks // 2 + 1,),
        in_specs=[token_spec, token_spec, whole(seg), whole(first_weights)],
        out_specs=[lead(dims, order) for dims, _, order in outs],
        out_shape=[shape((chunks,) + dims, kind) for dims, kind, _ in outs],
        scratch_shapes=[
            vmem((3 * model, model), bf16),
            vmem((model, BLOCK), f32),
            vmem((8, model, BLOCK), f32),
            vmem((2, model, CHUNK), f32),
            vmem((2, model, CHUNK), bf16),
            vmem((2, CHUNK, model), bf16),
            vmem((2 * CHUNK + BLOCK, model), bf16),
            vmem((model, 2 * CHUNK + BLOCK), bf16),
            vmem((2, 2, PAIRS, BLOCK, CHUNK), bf16),
            vmem((2, BLOCK, CHUNK), bf16),
        ],
        compiler_params=params,
        name="attend_first",
        cost_estimate=cost(14),
    )(x, inj, seg, first_weights)


def run_two(x, c1, inj, cot, seg, first_weights, second_weights, per_row):
    tokens, model = x.shape
    chunks = tokens // CHUNK
    owners = second_weights.shape[0]
    ff = BLOCK * owners
    second_grads = shape((2, owners // 2) + second_weights.shape[1:], bf16)
    last = chunks // 2 - 1
    turn = chunks // 2 + 1

    def up(lag):
        return lambda j: jnp.clip(j - lag, 0, last)

    def down(lag):
        return lambda j: jnp.clip(last - (j - turn - lag), 0, last)

    def up_then_down(j):
        return jnp.where(j < turn, jnp.minimum(j, last), jnp.clip(last - (j - turn - 1), 0, last))

    def lead(dims, order):
        return pl.BlockSpec((2,) + dims, lambda j: (order(j),) + (0,) * len(dims))

    def tok(order):
        return pl.BlockSpec((2 * CHUNK, model), lambda j: (order(j), 0))

    square = (model, CHUNK)
    mlp_saved = [
        vmem((chunks,) + square, bf16),
        vmem((chunks, 1, CHUNK), f32),
        vmem((chunks,) + square, bf16),
        vmem((chunks, ff, CHUNK), bf16),
        vmem((chunks, ff, CHUNK), bf16),
    ]
    back_buffers = [vmem(square, bf16), vmem((ff, CHUNK), bf16), vmem(square, bf16)]
    return pl.pallas_call(
        partial(kernel_two, per_row, chunks),
        grid=(2 * turn,),
        in_specs=[
            tok(up(0)),
            lead(square, up_then_down),
            tok(up(0)),
            tok(down(0)),
            whole(seg),
            whole(first_weights),
            whole(second_weights),
        ],
        out_specs=[
            tok(up(1)),
            lead(square, down(1)),
            lead(square, down(1)),
            lead(square, down(1)),
            whole(second_grads),
            pl.BlockSpec((3 * model, model), lambda j: (0, 0)),
            pl.BlockSpec((model, BLOCK), lambda j: (0, 0)),
        ],
        out_shape=[
            shape((tokens, model), bf16),
            shape((chunks,) + square, bf16),
            shape((chunks,) + square, bf16),
            shape((chunks,) + square, bf16),
            second_grads,
            shape((3 * model, model), f32),
            shape((model, BLOCK), f32),
        ],
        scratch_shapes=[
            vmem((3 * model, model), bf16),
            vmem((model, BLOCK), f32),
            vmem((model, model), bf16),
            vmem((model, ff), bf16),
            vmem((model, ff), bf16),
            vmem((8, model, BLOCK), f32),
            vmem((ff, BLOCK), f32),
            vmem((ff, model), bf16),
            vmem((ff, model), bf16),
            vmem((model, model), bf16),
            vmem((model, 3 * model), bf16),
        ]
        + [vmem(square, f32)] * 6
        + [
            vmem(square, bf16),
            vmem((CHUNK, model), bf16),
            vmem((CHUNK + BLOCK, model), bf16),
            vmem((model, CHUNK + BLOCK), bf16),
            vmem((2, PAIRS, BLOCK, CHUNK), bf16),
            vmem((2, PAIRS, BLOCK, CHUNK), bf16),
            vmem((2, BLOCK, CHUNK), bf16),
            vmem((2, CHUNK, BLOCK), bf16),
        ]
        + mlp_saved
        + [
            vmem((chunks,) + square, f32),
            vmem((chunks,) + square, f32),
            vmem((chunks,) + square, bf16),
            vmem((chunks, 1, CHUNK), f32),
            vmem((chunks,) + square, bf16),
            vmem((chunks, 2 * model, CHUNK), bf16),
            vmem((chunks, CHUNK, model), bf16),
            vmem((chunks, 2 * PAIRS * BLOCK, CHUNK), bf16),
            vmem((chunks,) + square, bf16),
        ]
        + mlp_saved
        + back_buffers[:2]
        + back_buffers
        + [
            vmem(square, bf16),
            vmem((3 * model, CHUNK), bf16),
            vmem((model, BLOCK), f32),
            vmem((model, BLOCK), f32),
            vmem((2 * PAIRS * BLOCK, CHUNK), bf16),
            vmem((ff, CHUNK), bf16),
            vmem((ff, CHUNK), bf16),
            *[vmem(square, bf16)] * 6,
            *[vmem((1, CHUNK), f32)] * 3,
            vmem(square, f32),
            vmem((ff, model), f32),
            vmem((ff, model), f32),
            vmem((model, model), f32),
            vmem((ff, BLOCK), f32),
            vmem((8, model, BLOCK), f32),
        ],
        compiler_params=params,
        name="middle",
        cost_estimate=cost(60),
    )(x, c1, inj, cot, seg, first_weights, second_weights)


def run_three(saved, dm, dc, du2, first_weights, sum_qkv, vec_in):
    unit, inv, normed, qk, vtok, probs, ctx = saved
    chunks, model, _ = dm.shape
    tokens = chunks * CHUNK
    last = chunks - 1
    first_grads = shape((2, OWNERS // 2) + first_weights.shape[1:], bf16)

    def now(j):
        return jnp.maximum(last - j, 0)

    def past(j):
        return jnp.minimum(chunks - j, last)

    def before(j):
        return jnp.maximum(last - 1 - j, 0)

    def lead(array, order):
        dims = array.shape[1:]
        return pl.BlockSpec((1,) + dims, lambda j: (order(j),) + (0,) * len(dims))

    tok = pl.BlockSpec((CHUNK, model), lambda j: (past(j), 0))
    return pl.pallas_call(
        partial(kernel_three, chunks),
        grid=(chunks + 1,),
        in_specs=[
            lead(unit, past),
            lead(inv, past),
            lead(normed, past),
            lead(qk, now),
            pl.BlockSpec((1, model, BLOCK), lambda j: (before(j), 1, 1)),
            lead(vtok, now),
            pl.BlockSpec((1, BLOCK, model), lambda j: (before(j), 1, 0)),
            lead(probs, now),
            lead(ctx, now),
            lead(dm, past),
            lead(dc, now),
            lead(du2, past),
            whole(first_weights),
            whole(sum_qkv),
            whole(vec_in),
        ],
        out_specs=[
            tok,
            tok,
            whole(first_grads),
        ],
        out_shape=[
            shape((tokens, model), bf16),
            shape((tokens, model), bf16),
            first_grads,
        ],
        scratch_shapes=[
            vmem((3 * model, model), bf16),
            vmem((model, BLOCK), f32),
            vmem((8, model, BLOCK), f32),
            vmem((model, 3 * model), bf16),
            vmem((2, PAIRS, BLOCK, CHUNK), bf16),
            vmem((2, PAIRS, BLOCK, CHUNK), bf16),
            vmem((2, BLOCK, CHUNK), bf16),
            vmem((2, CHUNK, BLOCK), bf16),
            vmem((3 * model, CHUNK), bf16),
            vmem((model, BLOCK), f32),
            vmem((model, BLOCK), f32),
            vmem((3 * model, model), f32),
            vmem((8, model, BLOCK), f32),
        ],
        compiler_params=params,
        name="attend_back",
        cost_estimate=cost(16),
    )(unit, inv, normed, qk, qk, vtok, vtok, probs, ctx, dm, dc, du2, first_weights, sum_qkv, vec_in)


def pack_first(qkv_t, vectors):
    rows, model = qkv_t.shape
    count = rows // 96
    columns = [vector.reshape(count, 1, 32) for vector in vectors[:3] + vectors[4:]]
    columns.insert(8, vectors[3].reshape(count, 4, 32))
    block = jnp.concatenate(columns, axis=1).transpose(0, 2, 1)
    block = jnp.pad(block, ((0, 0), (0, 0), (0, model - block.shape[2])))
    return jnp.concatenate([qkv_t.reshape(count, 96, model), block], axis=1)


def unpack_vectors(block):
    columns = [block[:, :, index].reshape(-1) for index in range(8)]
    columns.insert(3, block[:, :, 8:12].transpose(0, 2, 1).reshape(-1))
    return columns


def pack_second(out_t, up, down_t):
    rows, model = out_t.shape
    count = rows // 32
    up_part = up.reshape(2, model // 2, count, 128).transpose(2, 1, 0, 3).reshape(count, 128, 256)
    down_part = down_t.reshape(count, 32, 4, 256).transpose(0, 2, 1, 3).reshape(count, 128, 256)
    return jnp.concatenate([out_t.reshape(count, 32, model), up_part, down_part], axis=1)


def unpack_second_grads(block):
    count, _, model = block.shape
    out_t = block[:, :32].reshape(count * 32, model)
    up = block[:, 32:160].reshape(count, 128, 2, 128).transpose(2, 1, 0, 3)
    down_t = block[:, 160:].reshape(count, 4, 32, 256).transpose(0, 2, 1, 3)
    return out_t, up.reshape(model, 128 * count), down_t.reshape(32 * count, 1024)


def pack_kernel(qkv_t, out_t, up, down_t, *refs):
    vectors, (first_o, second_o) = refs[:9], refs[9:]
    rows = qkv_t.shape[0]
    first_o[:rows, :] = qkv_t[...]
    pieces = [vector[...].astype(f32) for vector in vectors[:3] + vectors[4:]]
    up_bias = vectors[3][...].astype(f32)
    pieces += [up_bias[:, 32 * col : 32 * (col + 1)] for col in range(4)]
    table = jnp.concatenate(pieces + [jnp.zeros((4, 32), f32)], axis=0)
    wide = jnp.concatenate([table, jnp.zeros((16, BLOCK - 32), f32)], axis=1)
    tall = jnp.concatenate([wide, jnp.zeros((BLOCK - 16, BLOCK), f32)], axis=0)
    columns = jnp.transpose(tall)[:32, :].astype(bf16)
    first_o[rows:, :] = jnp.concatenate([columns, jnp.zeros_like(columns)], axis=1)
    second_o[:32, :] = out_t[...]
    for side in range(2):
        second_o[32:160, half(side)] = up[half(side), :]
    for part in range(4):
        second_o[160 + 32 * part : 192 + 32 * part, :] = down_t[
            :, part * CHUNK : (part + 1) * CHUNK
        ]


def pack_own(qkv_t, out_t, up, down_t, vectors):
    rows, model = qkv_t.shape
    return pl.pallas_call(
        pack_kernel,
        out_shape=[shape((rows + 32, model), bf16), shape((288, model), bf16)],
        name="pack",
        cost_estimate=cost(2),
    )(qkv_t, out_t, up, down_t, *[vector.reshape(1, -1) for vector in vectors])


def unpack_kernel(first, *refs):
    seconds, (qkv_o, out_o, up_o, down_o, *vectors) = refs[:4], refs[4:]
    total = seconds[0][...].astype(f32)
    for second in seconds[1:]:
        total = total + second[...].astype(f32)
    out_o[...] = total[:32, :]
    for side in range(2):
        up_o[half(side), :] = total[32:160, half(side)]
    for part in range(4):
        start = 160 + 32 * part
        down_o[:, part * CHUNK : (part + 1) * CHUNK] = total[start : start + 32, :]
    total = first[0].astype(f32)
    for group in range(1, first.shape[0]):
        total = total + first[group].astype(f32)
    rows = qkv_o.shape[0]
    qkv_o[...] = total[:rows, :]
    columns = total[rows:, :BLOCK]
    tall = jnp.concatenate([columns, jnp.zeros((BLOCK - 32, BLOCK), f32)], axis=0)
    table = jnp.transpose(tall)
    for index, vector in enumerate(vectors[:3] + vectors[4:]):
        vector[...] = table[index : index + 1, :32]
    for col in range(4):
        vectors[3][:, 32 * col : 32 * (col + 1)] = table[8 + col : 9 + col, :32]


def unpack_sums(first, seconds, sizes):
    _, _, model = first.shape
    dims = [(96, model), (32, model), (model, BLOCK), (32, 4 * model)]
    dims += [(1, size) for size in sizes]
    return pl.pallas_call(
        unpack_kernel,
        out_shape=[shape(dim, f32) for dim in dims],
        name="unpack",
        cost_estimate=cost(2),
    )(first, *seconds)


def exchange(block, axis, size, distance):
    return lax.ppermute(block, axis, [(k, k ^ distance) for k in range(size)])


def doubled(block, distance):
    return in_pairs(block, exchange(block, "fsdp", OWNERS, distance), distance)


def in_pairs(block, other, distance):
    upper = (lax.axis_index("fsdp") & distance) != 0
    pair = jnp.stack([jnp.where(upper, other, block), jnp.where(upper, block, other)], axis=1)
    return pair.reshape((-1,) + block.shape[1:])


def pair_sum(parts):
    parity = lax.axis_index("fsdp") % 2
    own = lax.dynamic_index_in_dim(parts, parity, 0, False)
    away = lax.dynamic_index_in_dim(parts, 1 - parity, 0, False)
    got = exchange(away, "fsdp", OWNERS, 1)
    return (own.astype(f32) + got.astype(f32)).astype(bf16)


def column_sum(parts):
    place = lax.axis_index("fsdp") // 2
    got = [
        exchange(
            lax.dynamic_index_in_dim(parts, place ^ distance, 0, False),
            "fsdp", OWNERS, 2 * distance,
        )
        for distance in (3, 2, 1)
    ]
    total = lax.dynamic_index_in_dim(parts, place, 0, False).astype(f32)
    for block in got:
        total = total + block.astype(f32)
    return total


def in_order(parts):
    return parts.transpose(1, 0, 2, 3).reshape((-1,) + parts.shape[2:])


def scatter_sum_any(full, axis):
    own = lax.psum_scatter(full, "fsdp", scatter_dimension=axis, tiled=True)
    return lax.psum(own, "dp")


def local(
    inputs,
    inject,
    segments,
    cotangent,
    qkv_weight,
    out_weight,
    up_weight,
    down_weight,
    *vectors,
):
    row_count, length, model = inputs.shape
    tokens = row_count * length
    chunks = tokens // CHUNK
    x = inputs.reshape(tokens, model)
    inj = inject.reshape(tokens, model)
    cot = cotangent.reshape(tokens, model)
    seg = segments.reshape(chunks, 1, CHUNK)
    per_row = length // CHUNK
    packed = out_weight.shape[1] * OWNERS == model and lax.axis_size("dp") == 4
    if packed:
        first_own, second_own = pack_own(
            qkv_weight.T, out_weight.T, up_weight, down_weight.T, vectors
        )
        first_weights = doubled(doubled(doubled(first_own[None], 4), 2), 1)
        second_weights = doubled(second_own[None], 4)
        first_weights, second_weights = lax.optimization_barrier((first_weights, second_weights))
        second_other = exchange(second_weights, "fsdp", OWNERS, 2)
    else:

        def gathered(array, axis):
            return lax.all_gather(array, "fsdp", axis=axis, tiled=True)

        first_weights = pack_first(
            gathered(qkv_weight, 1).T, tuple(gathered(vector, 0) for vector in vectors)
        )
        second_weights = pack_second(
            gathered(out_weight, 1).T, gathered(up_weight, 1), gathered(down_weight, 1).T
        )
    saved = run_one(x, inj, seg, first_weights, per_row)
    if packed:
        second_other, context = lax.optimization_barrier((second_other, saved[-1]))
        saved = (*saved[:-1], context)
        second_weights = doubled(in_pairs(second_weights, second_other, 2), 1)
    result, dm, dc, du2, second_grads, sum_qkv, vec_mid = run_two(
        x, saved[-1], inj, cot, seg, first_weights, second_weights, per_row
    )
    if packed:
        second_pair, dm = lax.optimization_barrier((pair_sum(second_grads), dm))
        second_column = column_sum(second_pair).astype(bf16)
    grad_inputs, grad_inject, first_grads = run_three(
        saved, dm, dc, du2, first_weights, sum_qkv, vec_mid
    )
    if packed:
        second_column, first_grads = lax.optimization_barrier((second_column, first_grads))
        seconds = [second_column]
        seconds += [exchange(second_column, "dp", 4, distance) for distance in (1, 2, 3)]
        first_column = column_sum(pair_sum(first_grads)).astype(bf16)
        firsts = lax.all_gather(first_column, "dp", axis=0)
        qkv_t, out_t, up, down_t, *rows = unpack_sums(
            firsts, seconds, [vector.shape[0] for vector in vectors]
        )
        weight_grads = (qkv_t.T, out_t.T, up, down_t.T)
        vector_grads = [row.reshape(-1) for row in rows]
    else:
        first_all = in_order(first_grads).astype(f32)
        out_t, up, down_t = unpack_second_grads(in_order(second_grads).astype(f32))
        weight_grads = tuple(
            scatter_sum_any(grad, 1)
            for grad in (first_all[:, :96].reshape(3 * model, model).T, out_t.T, up, down_t.T)
        )
        vector_grads = [scatter_sum_any(grad, 0) for grad in unpack_vectors(first_all[:, 96:])]
    dims = inputs.shape
    return (
        result.reshape(dims),
        grad_inputs.reshape(dims),
        grad_inject.reshape(dims),
        *weight_grads,
        *vector_grads,
    )


def solution(mesh):
    placed = (
        P(("dp", "fsdp"), None, None),
        P(("dp", "fsdp"), None, None),
        P(("dp", "fsdp"), None),
        P(("dp", "fsdp"), None, None),
        P(None, "fsdp"),
        P(None, "fsdp"),
        P(None, "fsdp"),
        P(None, "fsdp"),
        P("fsdp"),
        P("fsdp"),
        P("fsdp"),
        P("fsdp"),
        P("fsdp"),
        P("fsdp"),
        P("fsdp"),
        P("fsdp"),
        P("fsdp"),
    )
    return jax.shard_map(
        local,
        mesh=mesh,
        in_specs=placed,
        out_specs=(
            P(("dp", "fsdp"), None, None),
            P(("dp", "fsdp"), None, None),
            P(("dp", "fsdp"), None, None),
            P(None, "fsdp"),
            P(None, "fsdp"),
            P(None, "fsdp"),
            P(None, "fsdp"),
            P("fsdp"),
            P("fsdp"),
            P("fsdp"),
            P("fsdp"),
            P("fsdp"),
            P("fsdp"),
            P("fsdp"),
            P("fsdp"),
            P("fsdp"),
        ),
        check_vma=False,
    )
```
